32 devices in a mesh: wide: 8 (over y, x, core), narrow: 4 (over z).
Axes of the slice: x: 2, y: 2, z: 4, core: 2. Of those that a mesh axis runs over, the one named last changes fastest.
Arguments:
- tokens: bfloat16 [16384, 768], P(('wide', 'narrow')), may hold values from -6 to 6
- block_size: int32 [8], P('wide'), may hold values from 4 to 16, as said below
- norm_gain: float32 [2, 2, 768], replicated, may hold values from 0.5 to 1.5
- norm_shift: float32 [2, 2, 768], replicated, may hold values from -2 to 2
- mixer_weight: bfloat16 [2, 768, 3, 768], P(None, None, None, 'narrow'), may hold values from -0.21875 to 0.21875
- mixer_bias: float32 [2, 3, 768], P(None, None, 'narrow'), may hold values from -2 to 2
- output_weight: bfloat16 [2, 768, 768], P(None, 'narrow'), may hold values from -1.75 to 1.75
- output_bias: float32 [2, 2, 768], replicated, may hold values from -2 to 2
- up_weight: bfloat16 [2, 768, 3072], P(None, None, 'narrow'), may hold values from -0.21875 to 0.21875
- up_bias: float32 [2, 3072], P(None, 'narrow'), may hold values from -2 to 2
- down_weight: bfloat16 [2, 3072, 768], P(None, 'narrow'), may hold values from -0.109375 to 0.109375
- cotangent: bfloat16 [16384, 768], P(('wide', 'narrow')), may hold values from -6 to 6
Outputs:
- block_out: bfloat16 [16384, 768], P(('wide', 'narrow'))
- tokens_grad: bfloat16 [16384, 768], P(('wide', 'narrow'))
- gain_grad: float32 [2, 2, 768], replicated
- shift_grad: float32 [2, 2, 768], replicated
- mixer_grad: float32 [2, 768, 3, 768], P(None, None, None, 'narrow')
- mixer_bias_grad: float32 [2, 3, 768], P(None, None, 'narrow')
- output_grad: float32 [2, 768, 768], P(None, 'narrow')
- output_bias_grad: float32 [2, 2, 768], replicated
- up_grad: float32 [2, 768, 3072], P(None, None, 'narrow')
- up_bias_grad: float32 [2, 3072], P(None, 'narrow')
- down_grad: float32 [2, 3072, 768], P(None, 'narrow')
The draws below stay inside these ranges and needn't reach their ends.
Inputs may be any that keep to these rules, and one draw needn't show every extreme that they name: `block_size`: each entry is 4, 8 or 16; some sequence has 16 and some has 4.
All inputs are finite; a program needn't handle non-finite values.
Results may differ from the reference program's by a relative error of at most 0.028.
Values may be sent and summed in bfloat16 or wider, within the bound.
No kernel may reach another device: no remote copies, remote signals or barrier semaphores. Data moves between devices by JAX's collectives and lax.ppermute only.
A program may use at most 192 MiB of HBM per device.

```python
import math
import jax
import jax.numpy as jnp
from jax import lax

D = 768
HEADS = 12
HEAD_DIM = 64
FF = 3072
LEN = 1024
LAYERS = 2
SEQS = 8
ROWS = 16384


def draw_block_size(key, part):
    key = jax.random.fold_in(key, 11)
    draw_key, pick_key = jax.random.split(key)
    powers = jax.random.randint(draw_key, (SEQS,), 0, 3)
    chosen = jax.random.permutation(pick_key, SEQS)
    powers = powers.at[chosen[0]].set(2).at[chosen[1]].set(0)
    return jnp.where(powers == 0, 4, jnp.where(powers == 1, 8, 16)).astype(jnp.int32)


def shard_levels(own_key, extent, pieces, smallest, largest):
    def one(axis_at, parts):
        steps = jax.random.uniform(jax.random.fold_in(jax.random.fold_in(own_key, 6), axis_at), (parts,), jnp.float32, smallest / len(pieces), largest / len(pieces))
        return jnp.repeat(jnp.exp(steps), extent[axis_at] // parts).reshape((-1,) + (1,) * (len(extent) - axis_at - 1))

    loudness = one(*pieces[0])
    for cut in pieces[1:]:
        loudness = loudness * one(*cut)
    return loudness


def bell_draw(stream_key, extent, scale, limit, cuts=(), kind=jnp.bfloat16):
    level = shard_levels(stream_key, extent, cuts, -0.22, 0.18) if cuts else 1.0
    array = jax.random.normal(stream_key, extent, jnp.float32) * scale * level
    return jnp.minimum(jnp.maximum(array, -limit), limit).astype(kind)


def setup_inputs(seed: int = 0) -> dict:
    keys = jax.random.split(jax.random.key(seed), 13)
    tokens = bell_draw(keys[0], (ROWS, D), 1.0, 6.0, ((0, 32),))
    block_size = draw_block_size(jax.random.fold_in(keys[12], 71), 0)
    norm_gain = jnp.clip(1.0 + 0.1 * jax.random.normal(keys[2], (LAYERS, 2, D), jnp.float32), 0.5, 1.5)
    norm_shift = bell_draw(keys[3], (LAYERS, 2, D), 0.3, 2.0, (), jnp.float32)
    mixer_weight = bell_draw(keys[4], (LAYERS, D, 3, D), D ** -0.5, 0.21875, ((3, 4),))
    mixer_bias = bell_draw(keys[5], (LAYERS, 3, D), 0.3, 2.0, ((2, 4),), jnp.float32)
    output_weight = bell_draw(keys[6], (LAYERS, D, D), (D // 64) ** -0.5, 1.75, ((1, 4),))
    output_bias = bell_draw(keys[7], (LAYERS, 2, D), 0.3, 2.0, (), jnp.float32)
    up_weight = bell_draw(keys[8], (LAYERS, D, FF), D ** -0.5, 0.21875, ((2, 4),))
    up_bias = bell_draw(keys[9], (LAYERS, FF), 0.3, 2.0, ((1, 4),), jnp.float32)
    down_weight = bell_draw(keys[10], (LAYERS, FF, D), FF ** -0.5, 0.109375, ((1, 4),))
    cotangent = bell_draw(keys[11], (ROWS, D), 1.0, 6.0, ((0, 32),))
    return {"tokens": tokens, "block_size": block_size, "norm_gain": norm_gain, "norm_shift": norm_shift, "mixer_weight": mixer_weight, "mixer_bias": mixer_bias, "output_weight": output_weight, "output_bias": output_bias, "up_weight": up_weight, "up_bias": up_bias, "down_weight": down_weight, "cotangent": cotangent}


EPSILON = 1e-05
HIGHEST = lax.Precision.HIGHEST

@jax.custom_vjp
def low(v):
    return lax.optimization_barrier(v.astype(jnp.bfloat16)).astype(jnp.float32)

@jax.custom_vjp
def low_back(v):
    return v

def low_keep(v):
    return (low(v), None)

def low_pass(kept, grad):
    return (grad,)

def back_keep(v):
    return (v, None)

def back_low(kept, grad):
    return (low(grad),)
low.defvjp(low_keep, low_pass)
low_back.defvjp(back_keep, back_low)

def layer_norm(values, gain, shift):
    center = values - lax.optimization_barrier(jnp.mean(values, axis=-1, keepdims=True))
    spread = lax.optimization_barrier(jnp.mean(center * center, axis=-1, keepdims=True))
    return center * lax.rsqrt(spread + EPSILON) * gain + shift

def rotary_tables(row_count):
    halfway = HEAD_DIM // 2
    positions = (jnp.arange(row_count, dtype=jnp.int32) % LEN).astype(jnp.float32)
    frequency = jnp.exp(jnp.arange(halfway, dtype=jnp.float32) * (-math.log(10000.0) / halfway))
    angles = positions[:, None] * frequency[None, :]
    return (jnp.cos(angles)[:, None, :], jnp.sin(angles)[:, None, :])

def rotate(heads_in, cosine, sine_table):
    halfway = heads_in.shape[-1] // 2
    first_half = heads_in[..., :halfway]
    second_half = heads_in[..., halfway:]
    return jnp.concatenate([first_half * cosine - second_half * sine_table, first_half * sine_table + second_half * cosine], axis=-1)

def allowed_pairs(query_rows, key_rows, block_width):
    noisy_query = query_rows < LEN
    noisy_key = key_rows < LEN
    query_block = query_rows % LEN // block_width
    key_block = key_rows % LEN // block_width
    same_block = query_block[:, None] == key_block[None, :]
    earlier = key_block[None, :] < query_block[:, None]
    noisy_case = jnp.where(noisy_key[None, :], same_block, earlier)
    clean_case = jnp.logical_and(jnp.logical_not(noisy_key)[None, :], jnp.logical_or(earlier, same_block))
    return jnp.where(noisy_query[:, None], noisy_case, clean_case)

def attention(queries, keys_all, values, block_width):
    row_count = queries.shape[0]
    block_rows = min(512, row_count)
    score_scale = HEAD_DIM ** (-0.5)
    key_rows = jnp.arange(row_count, dtype=jnp.int32)

    def one_block(offset):
        query_block = lax.dynamic_slice_in_dim(queries, offset, block_rows, 0)
        scores = low_back(jnp.einsum('qhd,khd->hqk', query_block, keys_all, precision=HIGHEST) * score_scale)
        query_rows = offset + jnp.arange(block_rows, dtype=jnp.int32)
        scores = jnp.where(allowed_pairs(query_rows, key_rows, block_width)[None], scores, -1e+30)
        highest = lax.optimization_barrier(jnp.max(scores, axis=-1, keepdims=True))
        weights = jnp.exp(scores - highest)
        chances = weights / lax.optimization_barrier(jnp.sum(weights, axis=-1, keepdims=True))
        return jnp.einsum('hqk,khd->qhd', low(chances), values, precision=HIGHEST)
    offsets = jnp.arange(row_count // block_rows, dtype=jnp.int32) * block_rows
    return lax.map(jax.checkpoint(one_block), offsets).reshape(queries.shape)

def layer_forward(residual, block_width, cosine, sine_table, norm_gain, norm_shift, mixer_weight, mixer_bias, output_weight, output_bias, up_weight, up_bias, down_weight):
    row_count = residual.shape[0]
    normed = low(layer_norm(residual, norm_gain[0], norm_shift[0]))
    projected = jnp.dot(normed, mixer_weight.reshape(D, 3 * D), precision=HIGHEST) + mixer_bias.reshape(3 * D)
    projected = low_back(projected).reshape(row_count, 3, HEADS, HEAD_DIM)
    queries = low(rotate(projected[:, 0], cosine, sine_table))
    keys_all = low(rotate(projected[:, 1], cosine, sine_table))
    values = low(projected[:, 2])
    attended = attention(queries, keys_all, values, block_width).reshape(row_count, D)
    attended = low_back(low(attended))
    branch = low_back(jnp.dot(attended, output_weight, precision=HIGHEST) + output_bias[0])
    middle = residual + branch
    normed = low(layer_norm(middle, norm_gain[1], norm_shift[1]))
    hidden = low_back(jnp.dot(normed, up_weight, precision=HIGHEST) + up_bias)
    active = low(jax.nn.gelu(hidden, approximate=True))
    branch = low_back(jnp.dot(active, down_weight, precision=HIGHEST) + output_bias[1])
    return middle + branch

def reference(tokens, block_size, norm_gain, norm_shift, mixer_weight, mixer_bias, output_weight, output_bias, up_weight, up_bias, down_weight, cotangent):
    cosine, sine_table = rotary_tables(2 * LEN)

    def forward(tokens_in, gain_in, shift_in, mixer_in, mixer_bias_in, output_in, output_bias_in, up_in, up_bias_in, down_in):
        sequences = tokens_in.reshape(SEQS, 2 * LEN, D)

        def one_sequence(pair_in):
            residual = pair_in[0]
            for layer_idx in range(LAYERS):
                residual = layer_forward(residual, pair_in[1], cosine, sine_table, gain_in[layer_idx], shift_in[layer_idx], mixer_in[layer_idx], mixer_bias_in[layer_idx], output_in[layer_idx], output_bias_in[layer_idx], up_in[layer_idx], up_bias_in[layer_idx], down_in[layer_idx])
            return residual
        return lax.map(jax.checkpoint(one_sequence), (sequences, block_size)).reshape(ROWS, D)
    result, pullback = jax.vjp(forward, tokens.astype(jnp.float32), norm_gain.astype(jnp.float32), norm_shift.astype(jnp.float32), mixer_weight.astype(jnp.float32), mixer_bias.astype(jnp.float32), output_weight.astype(jnp.float32), output_bias.astype(jnp.float32), up_weight.astype(jnp.float32), up_bias.astype(jnp.float32), down_weight.astype(jnp.float32))
    grads = pullback(cotangent.astype(jnp.float32))
    return (result.astype(jnp.bfloat16), grads[0].astype(jnp.bfloat16), grads[1], grads[2], grads[3], grads[4], grads[5], grads[6], grads[7], grads[8], grads[9])
```

```python
import functools
import math

import jax
import jax.numpy as jnp
from jax import lax
from jax.experimental import pallas as pl
from jax.experimental.pallas import tpu as pltpu
from jax.sharding import PartitionSpec as P

HEAD_DIM = 64
LEN = 1024
EPSILON = 1e-05
D = 768
QUARTERS = 4
HALF = 256
ROWS = 512
PIECE = 96
HEADS_COLS = 192
PARTS = 576
PACK = 224
MASKED = -1e30
BF = jnp.bfloat16
F32 = jnp.float32
NT = (((1,), (1,)), ((), ()))
TN = (((0,), (0,)), ((), ()))
VMEM_LIMIT = 56 * 1024 * 1024


def dot(a, b):
    return jnp.dot(a, b, preferred_element_type=F32)


def dot_nt(a, b):
    return lax.dot_general(a, b, NT, preferred_element_type=F32)


def dot_tn(a, b):
    return lax.dot_general(a, b, TN, preferred_element_type=F32)


def norm_parts(values):
    center = values - jnp.mean(values, axis=-1, keepdims=True)
    inverse = lax.rsqrt(jnp.mean(center * center, axis=-1, keepdims=True) + EPSILON)
    return center * inverse, inverse


def norm_backward(grad_in, unit_rows, inverse, gain):
    scaled = grad_in * gain
    return inverse * (
        scaled
        - jnp.mean(scaled, axis=-1, keepdims=True)
        - unit_rows * jnp.mean(scaled * unit_rows, axis=-1, keepdims=True)
    )


def swap_halves(u):
    lane = lax.broadcasted_iota(jnp.int32, u.shape, 1)
    return jnp.where((lane & 63) < 32, pltpu.roll(u, 96, axis=1), pltpu.roll(u, 32, axis=1))


def rot(u, cosine, sine):
    return u * cosine + swap_halves(u) * sine


def unrot(u, cosine, sine):
    return u * cosine - swap_halves(u) * sine


HOLDS = [(kb, flip ^ core) for core in (0, 1) for kb in (0, 2) for flip in (0, 2, 4, 6)]


def piece_copies(refs, idx, sems, place):
    w8, z = idx[0], idx[1]
    copies = []
    for (kb, flip), ref in zip(HOLDS, refs):
        for kk in range(2):
            k = kb + kk
            for source, target in place(ref.at[kk], k, (z - k) & 3, w8 ^ flip):
                copies.append(pltpu.make_async_copy(source, target, sems.at[len(copies)]))
    return copies


def rows_at(start, size, unit):
    return pl.ds(pl.multiple_of(start, unit), size)


def mixer_copies(refs, idx, sems, weights):
    def place(src, k, zq, wq):
        return [(src, weights.at[zq, rows_at(wq * PIECE, PIECE, 32)])]

    return piece_copies(refs, idx, sems, place)


def up_down_copies(refs, idx, sems, ups, downs):
    def place(src, k, zq, wq):
        rows = rows_at(wq * PIECE, PIECE, 32)
        return [
            (src.at[pl.ds(0, PIECE)], ups.at[k, rows]),
            (src.at[pl.ds(PIECE, PIECE)], downs.at[k, rows]),
        ]

    return piece_copies(refs, idx, sems, place)


def packed_copies(refs, idx, sems, packed):
    def place(src, k, zq, wq):
        return [(src.at[pl.ds(2 * PIECE, 32)], packed.at[zq, wq])]

    return piece_copies(refs, idx, sems, place)


def unpack_output(packed, weights):
    for zq in range(QUARTERS):
        for chip in range(4):
            for part in range(2):
                for s in range(3):
                    row = HEADS_COLS * zq + 48 * chip + 16 * s
                    weights[row : row + 16, 384 * part : 384 * part + 384] = packed[
                        zq, 2 * chip + part, 16 * (s // 2) : 16 * (s // 2) + 16, 384 * (s % 2) : 384 * (s % 2) + 384
                    ]


def any_spec():
    return pl.BlockSpec(memory_space=pl.ANY)


def vmem_spec():
    return pl.BlockSpec(memory_space=pltpu.VMEM)


def smem_spec():
    return pl.BlockSpec(memory_space=pltpu.SMEM)


def kernel_call(body, in_specs, out_shape, out_specs, scratch, args, flops, moved, aliases=None, name=None):
    return pl.pallas_call(
        body,
        in_specs=in_specs,
        out_specs=out_specs,
        out_shape=out_shape,
        scratch_shapes=scratch,
        input_output_aliases=aliases or {},
        compiler_params=pltpu.CompilerParams(vmem_limit_bytes=VMEM_LIMIT),
        cost_estimate=pl.CostEstimate(flops=int(flops), bytes_accessed=int(moved), transcendentals=0),
        name=name,
    )(*args)


def sds(shape, dtype):
    return jax.ShapeDtypeStruct(shape, dtype)


def project_body(idx, x, gain, shift, bias, cosine, sine, *rest):
    pieces, (h1, q, kv0, kv1, weights, wide, sems) = rest[:16], rest[16:]
    copies = mixer_copies(pieces, idx, sems, weights)
    for copy in copies:
        copy.start()

    def norm_rows(i, carry):
        rows = rows_at(i * 128, 128, 128)
        unit, _ = norm_parts(x[rows])
        h1[rows] = (unit * gain[...] + shift[...]).astype(BF)
        return carry

    lax.fori_loop(0, 4, norm_rows, 0)
    for copy in copies:
        copy.wait()
    for zq in range(QUARTERS):
        k = (idx[1] - zq) & 3
        p = dot(h1[...], weights[zq]) + bias[k]
        for part in range(3):
            col = D * part + HEADS_COLS * zq
            wide[:, col : col + HEADS_COLS] = p[:, HEADS_COLS * part : HEADS_COLS * (part + 1)]
    for half, kv in ((0, kv0), (1, kv1)):
        rows = slice(HALF * half, HALF * (half + 1))
        for j in range(6):
            cols = slice(128 * j, 128 * (j + 1))
            q[rows, cols] = (rot(wide[rows, cols], cosine[rows], sine[rows]) * 0.125).astype(BF)
            kcols = slice(D + 128 * j, D + 128 * (j + 1))
            kv[:, cols] = rot(wide[rows, kcols], cosine[rows], sine[rows]).astype(BF)
        kv[:, D:] = wide[rows, 2 * D :].astype(BF)


def project(idx, x, gain, shift, bias, cosine, sine, pieces):
    return kernel_call(
        project_body,
        [smem_spec()] + [vmem_spec()] * 6 + [any_spec()] * 16,
        [sds((ROWS, D), BF), sds((ROWS, D), BF), sds((HALF, 2 * D), BF), sds((HALF, 2 * D), BF)],
        [vmem_spec()] * 4,
        [
            pltpu.VMEM((QUARTERS, D, PARTS), BF),
            pltpu.VMEM((ROWS, 3 * D), F32),
            pltpu.SemaphoreType.DMA((32,)),
        ],
        (idx, x, gain, shift, bias, cosine, sine, *pieces),
        2 * ROWS * D * 3 * D,
        8e6,
        name="project",
    )


def load_keys(idx, own, near, far, far_near, kvn, kvc, kvr, sems):
    clean = idx[2] == 1
    waits = []
    for half in range(2):
        rows = pl.ds(HALF * half, HALF)
        copy = pltpu.make_async_copy(own[half], kvn.at[rows], sems.at[half])
        copy.start()
        waits.append(copy)
        for base, target, when_clean, when_noisy in ((2, kvc, own, near), (4, kvr, far, far_near)):
            sem = sems.at[base + half]
            a = pltpu.make_async_copy(when_clean[half], target.at[rows], sem)
            b = pltpu.make_async_copy(when_noisy[half], target.at[rows], sem)
            pl.when(clean)(a.start)
            pl.when(jnp.logical_not(clean))(b.start)
            waits.append(a)
    return waits


TILES = {
    0: [(0, [("c", 0, True)]), (1, [("c", 1, True), ("c", 0, False), ("r", 0, False), ("r", 1, False)])],
    1: [(1, [("c", 1, True), ("r", 0, False)]), (0, [("c", 0, True), ("c", 1, False), ("r", 0, False)])],
}


def attend_body(idx, q, kv0, kv1, c0, c1, r0, r1, n0, n1, o, lse, kvn, kvc, kvr, bias, bias_n, lcol, sems):
    waits = load_keys(idx, (kv0, kv1), (c0, c1), (r0, r1), (n0, n1), kvn, kvc, kvr, sems)
    clean, level = idx[2], idx[4]
    qi = lax.shift_right_logical(lax.broadcasted_iota(jnp.int32, (HALF, HALF), 0), level)
    ki = lax.shift_right_logical(lax.broadcasted_iota(jnp.int32, (HALF, HALF), 1), level)
    bias[...] = jnp.where(ki < qi + clean, 0.0, MASKED)
    same = jnp.where(ki == qi, 0, 1) + clean
    bias_n[...] = jnp.where(same[:128, :128] == 0, 0.0, MASKED)
    lcol[...] = jnp.zeros_like(lcol)
    for copy in waits:
        copy.wait()
    keys = {"c": kvc, "r": kvr}

    def run(tiles):
        def pair(hp, carry):
            off = pl.multiple_of(hp * 128, 128)
            cols = pl.ds(off, 128)
            vcols = pl.ds(pl.multiple_of(D + off, 128), 128)
            low_lane = lax.broadcasted_iota(jnp.int32, (HALF, 128), 1) < 64
            lane = lax.broadcasted_iota(jnp.int32, (HALF, 128), 1)
            ones = jnp.ones((HALF, 128), BF)
            for half, sources in tiles:
                rows = slice(HALF * half, HALF * (half + 1))
                q2 = q[rows, cols]
                sides = []
                for side in range(2):
                    qm = jnp.where(low_lane if side == 0 else jnp.logical_not(low_lane), q2, jnp.zeros_like(q2))
                    scores = []
                    for which, kh, diagonal in sources:
                        s = dot_nt(qm, keys[which][HALF * kh : HALF * (kh + 1), cols])
                        scores.append(s + bias[...] if diagonal else s)
                    own = [
                        dot_nt(qm[128 * t : 128 * (t + 1)], kvn[HALF * half + 128 * t : HALF * half + 128 * (t + 1), cols])
                        + bias_n[...]
                        for t in range(2)
                    ]
                    top = functools.reduce(jnp.maximum, [jnp.max(s, axis=-1, keepdims=True) for s in scores])
                    top = jnp.maximum(
                        top, jnp.concatenate([jnp.max(s, axis=-1, keepdims=True) for s in own], axis=0)
                    )
                    total = jnp.concatenate(
                        [
                            dot(
                                jnp.exp(own[t] - top[128 * t : 128 * (t + 1)]).astype(BF),
                                jnp.concatenate(
                                    [
                                        kvn[HALF * half + 128 * t : HALF * half + 128 * (t + 1), vcols],
                                        ones[:128],
                                    ],
                                    axis=1,
                                ),
                            )
                            for t in range(2)
                        ],
                        axis=0,
                    )
                    for s, (which, kh, diagonal) in zip(scores, sources):
                        v2 = jnp.concatenate([keys[which][HALF * kh : HALF * (kh + 1), vcols], ones], axis=1)
                        total = total + dot(jnp.exp(s - top).astype(BF), v2)
                    count = total[:, 128:]
                    sides.append((total[:, :128] / count, top + jnp.log(count)))
                o[rows, cols] = jnp.where(low_lane, sides[0][0], sides[1][0]).astype(BF)
                lcol[rows] = jnp.where(
                    lane == 2 * hp, sides[0][1], jnp.where(lane == 2 * hp + 1, sides[1][1], lcol[rows])
                )
            return carry

        lax.fori_loop(0, 6, pair, 0)

    for zl in range(2):
        pl.when(idx[3] == zl)(functools.partial(run, TILES[zl]))
    across = jnp.transpose(lcol[...])
    for head in range(12):
        lse[head] = across[head : head + 1]


def attend(idx, q, keys):
    return kernel_call(
        attend_body,
        [smem_spec(), vmem_spec()] + [any_spec()] * 8,
        [sds((ROWS, D), BF), sds((12, 1, ROWS), F32)],
        [vmem_spec()] * 2,
        [
            pltpu.VMEM((ROWS, 2 * D), BF),
            pltpu.VMEM((ROWS, 2 * D), BF),
            pltpu.VMEM((ROWS, 2 * D), BF),
            pltpu.VMEM((HALF, HALF), F32),
            pltpu.VMEM((128, 128), F32),
            pltpu.VMEM((ROWS, 128), F32),
            pltpu.SemaphoreType.DMA((6,)),
        ],
        (idx, q, *keys),
        12e9,
        6e6,
        name="attend",
    )


def feed_body(idx, x, o, gain, shift, out_bias, down_bias, up_bias, *rest):
    pieces, (x2, x1, h2, g, gp, ups, downs, packed, outw, sems, sems_o) = rest[:16], rest[16:]
    first = packed_copies(pieces, idx, sems_o, packed)
    later = up_down_copies(pieces, idx, sems, ups, downs)
    for copy in first + later:
        copy.start()
    for copy in first:
        copy.wait()
    unpack_output(packed, outw)
    x1[...] = x[...] + (dot(o[...], outw[...]) + out_bias[...])

    def norm_rows(i, carry):
        rows = rows_at(i * 128, 128, 128)
        unit, _ = norm_parts(x1[rows])
        h2[rows] = (unit * gain[...] + shift[...]).astype(BF)
        x2[rows] = x1[rows] + down_bias[...]
        return carry

    lax.fori_loop(0, 4, norm_rows, 0)
    for copy in later:
        copy.wait()

    def hidden(k, carry):
        for n in range(3):
            cols = slice(256 * n, 256 * (n + 1))
            u = dot(h2[...], ups[k, :, cols]) + up_bias[k, :, cols]
            uu = u * u
            t = jnp.tanh(0.7978845608028654 * u * (1.0 + 0.044715 * uu))
            half_t = 0.5 + 0.5 * t
            g[k, :, cols] = (u * half_t).astype(BF)
            slope = half_t + (0.5 * 0.7978845608028654) * u * (1.0 - t * t) * (1.0 + 0.134145 * uu)
            gp[k, :, cols] = slope.astype(BF)
        x2[...] += dot(g[k], downs[k])
        return carry

    lax.fori_loop(0, QUARTERS, hidden, 0)


WEIGHT_SCRATCH = [
    ((QUARTERS, D, D), BF),
    ((QUARTERS, D, D), BF),
    ((QUARTERS, 8, 32, D), BF),
    ((D, D), BF),
]


def feed(idx, x, o, gain, shift, out_bias, down_bias, up_bias, pieces):
    return kernel_call(
        feed_body,
        [smem_spec()] + [vmem_spec()] * 7 + [any_spec()] * 16,
        [
            sds((ROWS, D), F32),
            sds((ROWS, D), F32),
            sds((ROWS, D), BF),
            sds((QUARTERS, ROWS, D), BF),
            sds((QUARTERS, ROWS, D), BF),
        ],
        [vmem_spec()] * 5,
        [pltpu.VMEM(s, t) for s, t in WEIGHT_SCRATCH]
        + [pltpu.SemaphoreType.DMA((64,)), pltpu.SemaphoreType.DMA((32,))],
        (idx, x, o, gain, shift, out_bias, down_bias, up_bias, *pieces),
        2 * ROWS * D * D * 9,
        25e6,
        name="feed",
    )


def feed_back_body(idx, e, x1, gp, gain, *rest):
    pieces, (dm, dz, e1, da, do, small, ups, downs, packed, outw, dh2, hidden_sums, sems, sems_o) = rest[:16], rest[16:]
    first = packed_copies(pieces, idx, sems_o, packed)
    later = up_down_copies(pieces, idx, sems, ups, downs)
    for copy in later + first:
        copy.start()
    dm[...] = e[...].astype(BF)
    small[4:5] = jnp.sum(dm[...].astype(F32), axis=0, keepdims=True)
    dh2[...] = jnp.zeros_like(dh2)
    for copy in later:
        copy.wait()

    def hidden(k, carry):
        zq = (idx[1] - k) & 3
        for n in range(3):
            cols = slice(256 * n, 256 * (n + 1))
            part = (dot_nt(dm[...], downs[k, cols]) * gp[k, :, cols].astype(F32)).astype(BF)
            dz[k, :, cols] = part
            hidden_sums[zq, :, cols] = jnp.sum(part.astype(F32), axis=0, keepdims=True)
        dh2[...] += dot_nt(dz[k], ups[k])
        return carry

    lax.fori_loop(0, QUARTERS, hidden, 0)
    for copy in first:
        copy.wait()
    unpack_output(packed, outw)
    for zq in range(QUARTERS):
        small[zq : zq + 1] = hidden_sums[zq]
    small[5:8] = jnp.zeros((3, D), F32)

    def norm_rows(i, carry):
        rows = rows_at(i * 128, 128, 128)
        unit, inverse = norm_parts(x1[rows])
        grad = dh2[rows]
        up = e[rows] + norm_backward(grad, unit, inverse, gain[...])
        e1[rows] = up
        low = up.astype(BF)
        da[rows] = low
        small[5:6] += jnp.sum(low.astype(F32), axis=0, keepdims=True)
        small[6:7] += jnp.sum(grad * unit, axis=0, keepdims=True)
        small[7:8] += jnp.sum(grad, axis=0, keepdims=True)
        return carry

    lax.fori_loop(0, 4, norm_rows, 0)
    do[...] = dot_nt(da[...], outw[...]).astype(BF)


def feed_back(idx, e, x1, gp, gain, pieces):
    return kernel_call(
        feed_back_body,
        [smem_spec()] + [vmem_spec()] * 4 + [any_spec()] * 16,
        [
            sds((ROWS, D), BF),
            sds((QUARTERS, ROWS, D), BF),
            sds((ROWS, D), F32),
            sds((ROWS, D), BF),
            sds((ROWS, D), BF),
            sds((8, D), F32),
        ],
        [vmem_spec()] * 6,
        [pltpu.VMEM(s, t) for s, t in WEIGHT_SCRATCH]
        + [pltpu.VMEM((ROWS, D), F32), pltpu.VMEM((QUARTERS, 1, D), F32), pltpu.SemaphoreType.DMA((64,)), pltpu.SemaphoreType.DMA((32,))],
        (idx, e, x1, gp, gain, *pieces),
        2 * ROWS * D * D * 9,
        25e6,
        name="feed_back",
    )


def spread(idx, keep, send, source, k, wq, rows, sem):
    w8, mine = idx[0], idx[2]
    j = (wq >> 1) ^ (w8 >> 1)
    a = pltpu.make_async_copy(source, keep.at[j, k, rows], sem)
    b = pltpu.make_async_copy(source, send.at[j, k, rows], sem)
    pl.when((wq & 1) == mine)(a.start)
    pl.when((wq & 1) != mine)(b.start)
    return a


def feed_grads_body(idx, g, dm, h2, dz, o, da, keep, send, flipped, turned, d_up, d_down, d_out, sems):
    waits = []
    flipped[...] = jnp.transpose(o[...])
    turned[...] = dot(flipped[...], da[...]).astype(BF)
    for zq in range(QUARTERS):
        for chip in range(4):
            for part in range(2):
                for s in range(4):
                    rows, cols = slice(16 * (s // 2), 16 * (s // 2) + 16), slice(384 * (s % 2), 384 * (s % 2) + 384)
                    if s == 3:
                        block = jnp.zeros((16, 384), BF)
                    else:
                        row = HEADS_COLS * zq + 48 * chip + 16 * s
                        block = turned[row : row + 16, 384 * part : 384 * part + 384]
                    d_out[zq, 2 * chip + part, rows, cols] = block
    for zq in range(QUARTERS):
        k = (idx[1] - zq) & 3
        for wq in range(8):
            sem = sems.at[len(waits)]
            waits.append(spread(idx, keep, send, d_out.at[zq, wq], k, wq, pl.ds(2 * PIECE, 32), sem))
    for k in range(QUARTERS):
        flipped[...] = jnp.transpose(g[k])
        d_down[k] = dot(flipped[...], dm[...]).astype(BF)
        for wq in range(8):
            sem = sems.at[len(waits)]
            source = d_down.at[k, pl.ds(PIECE * wq, PIECE)]
            waits.append(spread(idx, keep, send, source, k, wq, pl.ds(PIECE, PIECE), sem))
    flipped[...] = jnp.transpose(h2[...])
    for k in range(QUARTERS):
        d_up[k] = dot(flipped[...], dz[k]).astype(BF)
        for wq in range(8):
            sem = sems.at[len(waits)]
            source = d_up.at[k, pl.ds(PIECE * wq, PIECE)]
            waits.append(spread(idx, keep, send, source, k, wq, pl.ds(0, PIECE), sem))
    for copy in waits:
        copy.wait()


def feed_grads(idx, g, dm, h2, dz, o, da):
    return kernel_call(
        feed_grads_body,
        [smem_spec()] + [vmem_spec()] * 6,
        [sds((4, QUARTERS, PACK, D), BF)] * 2,
        [any_spec()] * 2,
        [
            pltpu.VMEM((D, ROWS), BF),
            pltpu.VMEM((D, D), BF),
            pltpu.VMEM((QUARTERS, D, D), BF),
            pltpu.VMEM((QUARTERS, D, D), BF),
            pltpu.VMEM((QUARTERS, 8, 32, D), BF),
            pltpu.SemaphoreType.DMA((96,)),
        ],
        (idx, g, dm, h2, dz, o, da),
        2 * ROWS * D * D * 9,
        25e6,
        name="feed_grads",
    )


def attend_back_body(
    idx, q, do, o, lse, kv0, kv1, c0, c1, r0, r1, n0, n1, dq, dn, dc0, dc1, dr0, dr1, kvn, kvc, kvr, bias, bias_n, dcol, drow, sems
):
    waits = load_keys(idx, (kv0, kv1), (c0, c1), (r0, r1), (n0, n1), kvn, kvc, kvr, sems)
    clean, level = idx[2], idx[4]
    ki = lax.shift_right_logical(lax.broadcasted_iota(jnp.int32, (HALF, HALF), 0), level)
    qi = lax.shift_right_logical(lax.broadcasted_iota(jnp.int32, (HALF, HALF), 1), level)
    bias[...] = jnp.where(ki < qi + clean, 0.0, MASKED)
    same = jnp.where(ki == qi, 0, 1) + clean
    bias_n[...] = jnp.where(same[:128, :128] == 0, 0.0, MASKED)
    dcol[...] = jnp.zeros_like(dcol)

    def products(hp, carry):
        cols = pl.ds(pl.multiple_of(hp * 128, 128), 128)
        lane = lax.broadcasted_iota(jnp.int32, (ROWS, 128), 1)
        both = do[:, cols].astype(F32) * o[:, cols].astype(F32)
        first = jnp.sum(jnp.where(lane < 64, both, 0.0), axis=-1, keepdims=True)
        second = jnp.sum(jnp.where(lane < 64, 0.0, both), axis=-1, keepdims=True)
        dcol[...] = jnp.where(lane == 2 * hp, first, jnp.where(lane == 2 * hp + 1, second, dcol[...]))
        return carry

    lax.fori_loop(0, 6, products, 0)
    across = jnp.transpose(dcol[...])
    for head in range(12):
        drow[head] = across[head : head + 1]
    for copy in waits:
        copy.wait()
    keys = {"c": kvc, "r": kvr}
    outs = {("c", 0): dc0, ("c", 1): dc1, ("r", 0): dr0, ("r", 1): dr1}

    def run(tiles):
        by_key = {}
        for half, sources in tiles:
            for which, kh, diagonal in sources:
                by_key.setdefault((which, kh), []).append((half, diagonal))

        def pair(hp, carry):
            off = pl.multiple_of(hp * 128, 128)
            cols = pl.ds(off, 128)
            vcols = pl.ds(pl.multiple_of(D + off, 128), 128)

            def lows(n):
                low_lane = lax.broadcasted_iota(jnp.int32, (n, 128), 1) < 64
                return low_lane, jnp.logical_not(low_lane)

            def masked(v, side):
                return jnp.where(lows(v.shape[0])[side], v, jnp.zeros_like(v))

            def tile(k2, v2, qrow, n, bias_here):
                dk = dv = dqs = None
                q2, g2 = q[qrow : qrow + n, cols], do[qrow : qrow + n, cols]
                for side in range(2):
                    qm, gm, km = masked(q2, side), masked(g2, side), masked(k2, side)
                    head = 2 * hp + side
                    s = dot_nt(k2, qm)
                    if bias_here is not None:
                        s = s + bias_here
                    p = jnp.exp(s - lse[head, :, qrow : qrow + n])
                    dp = dot_nt(v2, gm)
                    ds = (p * (dp - drow[head, :, qrow : qrow + n])).astype(BF)
                    parts = (dot(ds, qm), dot(p.astype(BF), gm), dot_tn(ds, km))
                    if dk is None:
                        dk, dv, dqs = parts
                    else:
                        dk, dv, dqs = dk + parts[0], dv + parts[1], dqs + parts[2]
                return dk, dv, dqs

            dq_half = [None, None]
            for half in range(2):
                pieces = []
                for t in range(2):
                    row = HALF * half + 128 * t
                    dk, dv, dqs = tile(kvn[row : row + 128, cols], kvn[row : row + 128, vcols], row, 128, bias_n[...])
                    dn[row : row + 128, cols] = dk.astype(BF)
                    dn[row : row + 128, vcols] = dv.astype(BF)
                    pieces.append(dqs)
                dq_half[half] = jnp.concatenate(pieces, axis=0)
            for key in (("c", 0), ("c", 1), ("r", 0), ("r", 1)):
                if key not in by_key:
                    outs[key][:, cols] = jnp.zeros((HALF, 128), BF)
                    outs[key][:, vcols] = jnp.zeros((HALF, 128), BF)
                    continue
                krow = HALF * key[1]
                k2 = keys[key[0]][krow : krow + HALF, cols]
                v2 = keys[key[0]][krow : krow + HALF, vcols]
                total_k = total_v = None
                for half, diagonal in by_key[key]:
                    dk, dv, dqs = tile(k2, v2, HALF * half, HALF, bias[...] if diagonal else None)
                    total_k = dk if total_k is None else total_k + dk
                    total_v = dv if total_v is None else total_v + dv
                    dq_half[half] = dq_half[half] + dqs
                outs[key][:, cols] = total_k.astype(BF)
                outs[key][:, vcols] = total_v.astype(BF)
            for half in range(2):
                dq[HALF * half : HALF * (half + 1), cols] = dq_half[half] * 0.125
            return carry

        lax.fori_loop(0, 6, pair, 0)

    for zl in range(2):
        pl.when(idx[3] == zl)(functools.partial(run, TILES[zl]))


def attend_back(idx, q, do, o, lse, keys):
    return kernel_call(
        attend_back_body,
        [smem_spec()] + [vmem_spec()] * 4 + [any_spec()] * 8,
        [sds((ROWS, D), F32), sds((ROWS, 2 * D), BF)] + [sds((HALF, 2 * D), BF)] * 4,
        [vmem_spec()] * 6,
        [
            pltpu.VMEM((ROWS, 2 * D), BF),
            pltpu.VMEM((ROWS, 2 * D), BF),
            pltpu.VMEM((ROWS, 2 * D), BF),
            pltpu.VMEM((HALF, HALF), F32),
            pltpu.VMEM((128, 128), F32),
            pltpu.VMEM((ROWS, 128), F32),
            pltpu.VMEM((12, 1, ROWS), F32),
            pltpu.SemaphoreType.DMA((6,)),
        ],
        (idx, q, do, o, lse, *keys),
        30e9,
        12e6,
        name="attend_back",
    )


def project_back_body(idx, dq, dn, dc0, dc1, tc0, tc1, tr0, tr1, cosine, sine, x, e1, gain, *rest):
    pieces, (dpz, e, small, weights, wide, sems) = rest[:16], rest[16:]
    copies = mixer_copies(pieces, idx, sems, weights)
    for copy in copies:
        copy.start()
    noisy = idx[2] == 0
    for half, (dc, tc, tr) in enumerate(((dc0, tc0, tr0), (dc1, tc1, tr1))):
        rows = slice(HALF * half, HALF * (half + 1))
        for j in range(6):
            cols = slice(128 * j, 128 * (j + 1))
            wide[rows, cols] = unrot(dq[rows, cols], cosine[rows], sine[rows])

        def total(cols, half_rows=rows, dc=dc, tc=tc, tr=tr):
            summed = dc[:, cols].astype(F32) + tc[:, cols].astype(F32) + tr[:, cols].astype(F32)
            return jnp.where(noisy, dn[half_rows, cols].astype(F32), summed)

        for j in range(6):
            cols = slice(128 * j, 128 * (j + 1))
            wide[rows, D + 128 * j : D + 128 * (j + 1)] = unrot(total(cols), cosine[rows], sine[rows])
        wide[rows, 2 * D :] = total(slice(D, 2 * D))
    for copy in copies:
        copy.wait()
    small[...] = jnp.zeros_like(small)
    for zq in range(QUARTERS):
        for part in range(3):
            col = D * part + HEADS_COLS * zq
            dpz[zq, :, HEADS_COLS * part : HEADS_COLS * (part + 1)] = wide[:, col : col + HEADS_COLS].astype(BF)
        small[zq : zq + 1, :PARTS] = jnp.sum(dpz[zq].astype(F32), axis=0, keepdims=True)
        piece = dot_nt(dpz[zq], weights[zq])
        if zq == 0:
            e[...] = piece
        else:
            e[...] += piece

    def norm_rows(i, carry):
        rows = rows_at(i * 128, 128, 128)
        unit, inverse = norm_parts(x[rows])
        grad = e[rows]
        small[4:5] += jnp.sum(grad * unit, axis=0, keepdims=True)
        small[5:6] += jnp.sum(grad, axis=0, keepdims=True)
        e[rows] = e1[rows] + norm_backward(grad, unit, inverse, gain[...])
        return carry

    lax.fori_loop(0, 4, norm_rows, 0)


def project_back(idx, dq, dn, dc, tc, tr, cosine, sine, x, e1, gain, pieces):
    return kernel_call(
        project_back_body,
        [smem_spec()] + [vmem_spec()] * 13 + [any_spec()] * 16,
        [sds((QUARTERS, ROWS, PARTS), BF), sds((ROWS, D), F32), sds((8, D), F32)],
        [vmem_spec()] * 3,
        [
            pltpu.VMEM((QUARTERS, D, PARTS), BF),
            pltpu.VMEM((ROWS, 3 * D), F32),
            pltpu.SemaphoreType.DMA((32,)),
        ],
        (idx, dq, dn, *dc, *tc, *tr, cosine, sine, x, e1, gain, *pieces),
        2 * ROWS * D * 3 * D,
        12e6,
        name="project_back",
    )


def project_grads_body(idx, h1, dpz, keep, send, flipped, stage, sems):
    waits = []
    flipped[...] = jnp.transpose(h1[...])
    for zq in range(QUARTERS):
        k = (idx[1] - zq) & 3
        stage[zq] = dot(flipped[...], dpz[zq]).astype(BF)
        for wq in range(8):
            sem = sems.at[len(waits)]
            source = stage.at[zq, pl.ds(PIECE * wq, PIECE)]
            waits.append(spread(idx, keep, send, source, k, wq, pl.ds(0, PIECE), sem))
    for copy in waits:
        copy.wait()


def project_grads(idx, h1, dpz):
    return kernel_call(
        project_grads_body,
        [smem_spec()] + [vmem_spec()] * 2,
        [sds((4, QUARTERS, PIECE, PARTS), BF)] * 2,
        [any_spec()] * 2,
        [
            pltpu.VMEM((D, ROWS), BF),
            pltpu.VMEM((QUARTERS, D, PARTS), BF),
            pltpu.SemaphoreType.DMA((32,)),
        ],
        (idx, h1, dpz),
        2 * ROWS * D * 3 * D,
        9e6,
        name="project_grads",
    )


def finish_mixer_body(layer, filled, idx, *rest):
    pieces, rest = rest[:8], rest[8:]
    if filled:
        rest = rest[1:]
    out, stage, sem = rest
    for flip, piece in enumerate(pieces):
        stage[rows_at((idx[0] ^ flip) * PIECE, PIECE, 32)] = piece[...].astype(F32)
    copy = pltpu.make_async_copy(stage, out.at[layer], sem)
    copy.start()
    copy.wait()


def finish_mixer(idx, layer, layers, pieces, before):
    filled = before is not None
    return kernel_call(
        functools.partial(finish_mixer_body, layer, filled),
        [smem_spec()] + [vmem_spec()] * 8 + [any_spec()] * filled,
        sds((layers, D, PARTS), F32),
        any_spec(),
        [pltpu.VMEM((D, PARTS), F32), pltpu.SemaphoreType.DMA],
        (idx, *pieces) + ((before,) if filled else ()),
        1e6,
        4e6,
        aliases={9: 0} if filled else None,
        name="finish_mixer",
    )


def finish_feed_body(layer, filled, idx, *rest):
    pieces, rest = rest[:8], rest[8:]
    if filled:
        rest = rest[3:]
    up, down, out, up_s, down_s, out_s, sems = rest
    for flip, piece in enumerate(pieces):
        wq = idx[0] ^ flip
        rows = rows_at(wq * PIECE, PIECE, 32)
        up_s[rows] = piece[:PIECE].astype(F32)
        down_s[rows] = piece[PIECE : 2 * PIECE].astype(F32)
        cols = pl.ds(pl.multiple_of((wq & 1) * 384, 128), 384)
        for s in range(3):
            row = 2 * PIECE + 16 * (s // 2)
            block = piece[row : row + 16, 384 * (s % 2) : 384 * (s % 2) + 384]
            out_s[rows_at((wq >> 1) * 48 + 16 * s, 16, 16), cols] = block.astype(F32)
    copies = [
        pltpu.make_async_copy(stage, whole.at[layer], sems.at[i])
        for i, (stage, whole) in enumerate(((up_s, up), (down_s, down), (out_s, out)))
    ]
    for copy in copies:
        copy.start()
    for copy in copies:
        copy.wait()


def finish_feed(idx, layer, layers, pieces, before):
    filled = before is not None
    return kernel_call(
        functools.partial(finish_feed_body, layer, filled),
        [smem_spec()] + [vmem_spec()] * 8 + [any_spec()] * (3 * filled),
        [sds((layers, D, D), F32), sds((layers, D, D), F32), sds((layers, HEADS_COLS, D), F32)],
        [any_spec()] * 3,
        [
            pltpu.VMEM((D, D), F32),
            pltpu.VMEM((D, D), F32),
            pltpu.VMEM((HEADS_COLS, D), F32),
            pltpu.SemaphoreType.DMA((3,)),
        ],
        (idx, *pieces) + (tuple(before) if filled else ()),
        1e6,
        8e6,
        aliases={9: 0, 10: 1, 11: 2} if filled else None,
        name="finish_feed",
    )


def flip_wide(x, bit):
    return lax.ppermute(x, "wide", [(i, i ^ bit) for i in range(lax.axis_size("wide"))])


def shift_narrow(x, k):
    return lax.ppermute(x, "narrow", [(i, (i + k) % QUARTERS) for i in range(QUARTERS)])


def gather_pieces(piece):
    r = [piece] + [shift_narrow(piece, k) for k in range(1, QUARTERS)]
    p, q = jnp.stack(r[:2]), jnp.stack(r[2:])
    px, qy = flip_wide(p, 2), flip_wide(q, 4)
    py, qx = flip_wide(p, 4), flip_wide(q, 2)
    pxy, qxy = flip_wide(px, 4), flip_wide(qy, 2)
    here = [p, px, py, pxy, q, qx, qy, qxy]
    return here + [flip_wide(x, 1) for x in here]


def added(*terms):
    return functools.reduce(jnp.add, [t.astype(F32) for t in terms]).astype(BF)


def reduce_pieces(keep, send):
    got = flip_wide(send, 1)

    def both(js, ks):
        return added(keep[js, ks], got[js, ks])

    first, second = slice(0, 2), slice(2, 4)
    px = flip_wide(both(slice(1, 4, 2), first), 2)
    qy = flip_wide(both(slice(2, 4), second), 4)
    p = added(both(slice(0, 4, 2), first), px)
    q = added(both(slice(0, 2), second), qy)
    p = added(p[0], flip_wide(p[1], 4))
    q = added(q[0], flip_wide(q[1], 2))
    bit = 8
    while bit < lax.axis_size("wide"):
        p, q = added(p, flip_wide(p, bit)), added(q, flip_wide(q, bit))
        bit *= 2
    total = added(p[0], shift_narrow(p[1], -1), shift_narrow(q[0], -2), shift_narrow(q[1], -3))
    x, y = flip_wide(total, 2), flip_wide(total, 4)
    here = [total, x, y, flip_wide(x, 4)]
    there = [flip_wide(t, 1) for t in here]
    return [t for pair in zip(here, there) for t in pair]


def reduce_small(values):
    bit = 1
    while bit < lax.axis_size("wide"):
        values = values + flip_wide(values, bit)
        bit *= 2
    for bit in (1, 2):
        values = values + lax.ppermute(values, "narrow", [(i, i ^ bit) for i in range(QUARTERS)])
    return values


def device_pairs(move):
    pairs = []
    for w in range(lax.axis_size("wide")):
        for z in range(QUARTERS):
            target = move(w, z)
            if target is not None:
                pairs.append((w * QUARTERS + z, target[0] * QUARTERS + target[1]))
    return pairs


BOTH = ("wide", "narrow")


def relocate(rows):
    first = device_pairs(lambda w, z: ((w & ~1) | (z >> 1), ((w & 1) << 1) | (z & 1)))
    second = device_pairs(lambda w, z: ((w & ~1) | (z >> 1), ((w & 1) << 1) | (1 - (z & 1))))
    return lax.ppermute(rows[:HALF], BOTH, first), lax.ppermute(rows[HALF:], BOTH, second)


def between_chips(x, low_from):
    pairs = device_pairs(lambda w, z: (w, z ^ 1) if (w & 1) and (z & 1) in low_from else None)
    return lax.ppermute(x, BOTH, pairs)


def within_chip(x, source):
    pairs = [(i, i ^ 1) for i in range(lax.axis_size("wide")) if (i & 1) == source]
    return lax.ppermute(x, "wide", pairs)


def per_device(
    tokens,
    block_size,
    norm_gain,
    norm_shift,
    mixer_weight,
    mixer_bias,
    output_weight,
    output_bias,
    up_weight,
    up_bias,
    down_weight,
    cotangent,
):
    layers = norm_gain.shape[0]
    w, z = lax.axis_index("wide"), lax.axis_index("narrow")
    w8, core, low = w & 7, w & 1, z & 1
    sizes = jnp.where((z >> 1) == core, block_size, flip_wide(block_size, 1))[0]
    level = 2 + (sizes >= 8).astype(jnp.int32) + (sizes >= 16).astype(jnp.int32)
    idx = jnp.stack([w8, z, core, low, level, w8, w8, w8]).astype(jnp.int32)

    bases = jnp.where(low == 0, jnp.array([0, 768]), jnp.array([512, 256]))
    position = (bases[:, None] + jnp.arange(HALF)[None, :]).reshape(ROWS).astype(F32)
    halfway = HEAD_DIM // 2
    frequency = jnp.exp(jnp.arange(halfway, dtype=F32) * (-math.log(10000.0) / halfway))
    angle = position[:, None] * frequency[None, :]
    cosine = jnp.tile(jnp.cos(angle), (1, 4))
    sine = jnp.sin(angle)
    sine = jnp.concatenate([-sine, sine, -sine, sine], axis=1)

    def bias_pieces(layer):
        return mixer_bias[layer].reshape(PARTS), up_bias[layer]

    biases = jnp.concatenate([t for layer in range(layers) for t in bias_pieces(layer)])
    biases = jnp.stack([biases] + [shift_narrow(biases, k) for k in range(1, QUARTERS)])
    width = PARTS + D
    mixer_biases = [biases[:, None, width * layer : width * layer + PARTS] for layer in range(layers)]
    up_biases = [biases[:, None, width * layer + PARTS : width * (layer + 1)] for layer in range(layers)]

    def rows_of(weight, layer, start, count):
        return lax.dynamic_slice_in_dim(weight[layer], start, count, 0)

    def packed_output(layer):
        block = rows_of(output_weight, layer, (w8 >> 1) * 48, 48)
        block = lax.dynamic_slice_in_dim(block, core * 384, 384, 1).reshape(3, 16, 384)
        block = jnp.concatenate([block, jnp.zeros((1, 16, 384), BF)]).reshape(2, 2, 16, 384)
        return block.transpose(0, 2, 1, 3).reshape(32, D)

    mixer_pieces, feed_pieces = [], []
    for layer in range(layers):
        piece = rows_of(mixer_weight, layer, w8 * PIECE, PIECE).reshape(PIECE, PARTS)
        mixer_pieces.append(gather_pieces(piece))
        piece = jnp.concatenate(
            [
                rows_of(up_weight, layer, w8 * PIECE, PIECE),
                rows_of(down_weight, layer, w8 * PIECE, PIECE),
                packed_output(layer),
            ]
        )
        feed_pieces.append(gather_pieces(piece))

    x = jnp.concatenate(relocate(tokens)).astype(F32)
    e = jnp.concatenate(relocate(cotangent)).astype(F32)

    stores = []
    for layer in range(layers):
        gain, shift, bias = norm_gain[layer], norm_shift[layer], output_bias[layer]
        h1, q, kv0, kv1 = project(
            idx, x, gain[0:1], shift[0:1], mixer_biases[layer], cosine, sine, mixer_pieces[layer]
        )
        far = (between_chips(kv0, (0, 1)), between_chips(kv1, (1,)))
        near = (within_chip(kv0, 1), within_chip(kv1, 1))
        far_near = (within_chip(far[0], 1), within_chip(far[1], 1))
        keys = (kv0, kv1, *near, *far, *far_near)
        o, lse = attend(idx, q, keys)
        x2, x1, h2, g, gp = feed(
            idx, x, o, gain[1:2], shift[1:2], bias[0:1], bias[1:2], up_biases[layer], feed_pieces[layer]
        )
        stores.append((x, h1, q, keys, o, lse, x1, h2, g, gp))
        x = x2
    block_out = jnp.concatenate(relocate(x.astype(BF)))

    mixer_out, feed_out = None, None
    smalls = [None] * layers
    for layer in reversed(range(layers)):
        x, h1, q, keys, o, lse, x1, h2, g, gp = stores[layer]
        gain = norm_gain[layer]
        dm, dz, e1, da, do, small_feed = feed_back(idx, e, x1, gp, gain[1:2], feed_pieces[layer])
        dq, dn, dc0, dc1, dr0, dr1 = attend_back(idx, q, do, o, lse, keys)
        tc = (within_chip(dc0, 0), within_chip(dc1, 0))
        tr = (within_chip(dr0, 0), within_chip(dr1, 0))
        tr = (between_chips(added(dr0, tr[0]), (0, 1)), between_chips(added(dr1, tr[1]), (0,)))
        feed_grad = reduce_pieces(*feed_grads(idx, g, dm, h2, dz, o, da))
        dpz, e, small_mixer = project_back(
            idx, dq, dn, (dc0, dc1), tc, tr, cosine, sine, x, e1, gain[0:1], mixer_pieces[layer]
        )
        mixer_grad = reduce_pieces(*project_grads(idx, h1, dpz))
        feed_out = finish_feed(idx, layer, layers, feed_grad, feed_out)
        mixer_out = finish_mixer(idx, layer, layers, mixer_grad, mixer_out)
        smalls[layer] = reduce_small(jnp.concatenate([small_feed, small_mixer]))
    tokens_grad = jnp.concatenate(relocate(e.astype(BF)))

    small = jnp.stack(smalls)
    up_bias_grad = lax.dynamic_index_in_dim(small[:, 0:4], z, 1, keepdims=False)
    mixer_bias_grad = lax.dynamic_index_in_dim(small[:, 8:12, :PARTS], z, 1, keepdims=False)
    return (
        block_out,
        tokens_grad,
        jnp.stack([small[:, 12], small[:, 6]], axis=1),
        jnp.stack([small[:, 13], small[:, 7]], axis=1),
        mixer_out.reshape(layers, D, 3, HEADS_COLS),
        mixer_bias_grad.reshape(layers, 3, HEADS_COLS),
        feed_out[2],
        jnp.stack([small[:, 5], small[:, 4]], axis=1),
        feed_out[0],
        up_bias_grad,
        feed_out[1],
    )


def solution(mesh):
    rows = P(("wide", "narrow"), None)
    quarters = (
        P(None, None, None, "narrow"),
        P(None, None, "narrow"),
        P(None, "narrow", None),
        P(),
        P(None, None, "narrow"),
        P(None, "narrow"),
        P(None, "narrow", None),
    )
    return jax.shard_map(
        per_device,
        mesh=mesh,
        in_specs=(rows, P("wide"), P(), P()) + quarters + (rows,),
        out_specs=(rows, rows, P(), P()) + quarters,
        check_vma=False,
    )
```

```python
import functools
import math

import jax
import jax.numpy as jnp
from jax import lax
from jax.experimental import pallas as pl
from jax.experimental.pallas import tpu as pltpu
from jax.sharding import PartitionSpec as P

HEAD_DIM = 64
LEN = 1024
EPSILON = 1e-05
D = 768
QUARTERS = 4
HALF = 256
ROWS = 512
PIECE = 96
HEADS_COLS = 192
PARTS = 576
PACK = 224
MASKED = -1e30
BF = jnp.bfloat16
F32 = jnp.float32
NT = (((1,), (1,)), ((), ()))
TN = (((0,), (0,)), ((), ()))
VMEM_LIMIT = 56 * 1024 * 1024


def dot(a, b):
    return jnp.dot(a, b, preferred_element_type=F32)


def dot_nt(a, b):
    return lax.dot_general(a, b, NT, preferred_element_type=F32)


def dot_tn(a, b):
    return lax.dot_general(a, b, TN, preferred_element_type=F32)


def norm_parts(values):
    center = values - jnp.mean(values, axis=-1, keepdims=True)
    inverse = lax.rsqrt(jnp.mean(center * center, axis=-1, keepdims=True) + EPSILON)
    return center * inverse, inverse


def norm_backward(grad_in, unit_rows, inverse, gain):
    scaled = grad_in * gain
    return inverse * (
        scaled
        - jnp.mean(scaled, axis=-1, keepdims=True)
        - unit_rows * jnp.mean(scaled * unit_rows, axis=-1, keepdims=True)
    )


def swap_halves(u):
    lane = lax.broadcasted_iota(jnp.int32, u.shape, 1)
    return jnp.where((lane & 63) < 32, pltpu.roll(u, 96, axis=1), pltpu.roll(u, 32, axis=1))


def rot(u, cosine, sine):
    return u * cosine + swap_halves(u) * sine


def unrot(u, cosine, sine):
    return u * cosine - swap_halves(u) * sine


ORDER = (0, 2, 1, 3)


def flips(idx):
    first, second = 2 + 2 * idx[2], 4 - 2 * idx[2]
    return [0, first, second, 6, 1, 1 ^ second, 1 ^ first, 7]


def piece_copies(refs, idx, sems, place):
    copies = []
    for flip, ref in zip(flips(idx), refs):
        for at, k in enumerate(ORDER):
            for source, target in place(ref.at[at], k, idx[1] ^ k, idx[0] ^ flip):
                copies.append(pltpu.make_async_copy(source, target, sems.at[len(copies)]))
    return copies


def rows_at(start, size, unit):
    return pl.ds(pl.multiple_of(start, unit), size)


def mixer_copies(refs, idx, sems, weights):
    def place(src, k, zq, wq):
        return [(src, weights.at[zq, rows_at(wq * PIECE, PIECE, 32)])]

    return piece_copies(refs, idx, sems, place)


def up_down_copies(refs, idx, sems, ups, downs):
    def place(src, k, zq, wq):
        rows = rows_at(wq * PIECE, PIECE, 32)
        return [
            (src.at[pl.ds(0, PIECE)], ups.at[k, rows]),
            (src.at[pl.ds(PIECE, PIECE)], downs.at[k, rows]),
        ]

    return piece_copies(refs, idx, sems, place)


def packed_copies(refs, idx, sems, packed):
    def place(src, k, zq, wq):
        return [(src.at[pl.ds(2 * PIECE, 32)], packed.at[zq, wq])]

    return piece_copies(refs, idx, sems, place)


def unpack_output(packed, weights):
    for zq in range(QUARTERS):
        for chip in range(4):
            for part in range(2):
                for s in range(3):
                    row = HEADS_COLS * zq + 48 * chip + 16 * s
                    weights[row : row + 16, 384 * part : 384 * part + 384] = packed[
                        zq, 2 * chip + part, 16 * (s // 2) : 16 * (s // 2) + 16, 384 * (s % 2) : 384 * (s % 2) + 384
                    ]


def any_spec():
    return pl.BlockSpec(memory_space=pl.ANY)


def vmem_spec():
    return pl.BlockSpec(memory_space=pltpu.VMEM)


def smem_spec():
    return pl.BlockSpec(memory_space=pltpu.SMEM)


def kernel_call(body, in_specs, out_shape, out_specs, scratch, args, flops, moved, aliases=None, name=None):
    return pl.pallas_call(
        body,
        in_specs=in_specs,
        out_specs=out_specs,
        out_shape=out_shape,
        scratch_shapes=scratch,
        input_output_aliases=aliases or {},
        compiler_params=pltpu.CompilerParams(vmem_limit_bytes=VMEM_LIMIT),
        cost_estimate=pl.CostEstimate(flops=1000, bytes_accessed=1000, transcendentals=0),
        name=name,
    )(*args)


def sds(shape, dtype):
    return jax.ShapeDtypeStruct(shape, dtype)


def project_body(idx, x, gain, shift, bias, cosine, sine, *rest):
    pieces, (h1, q, kv, weights, wide, sems) = rest[:8], rest[8:]
    copies = mixer_copies(pieces, idx, sems, weights)
    for copy in copies:
        copy.start()

    def norm_rows(i, carry):
        rows = rows_at(i * 128, 128, 128)
        unit, _ = norm_parts(x[rows])
        h1[rows] = (unit * gain[...] + shift[...]).astype(BF)
        return carry

    lax.fori_loop(0, 4, norm_rows, 0)
    for copy in copies:
        copy.wait()
    for zq in range(QUARTERS):
        p = dot(h1[...], weights[zq]) + bias[idx[1] ^ zq]
        for part in range(3):
            col = D * part + HEADS_COLS * zq
            wide[:, col : col + HEADS_COLS] = p[:, HEADS_COLS * part : HEADS_COLS * (part + 1)]
    for half in range(2):
        rows = slice(HALF * half, HALF * (half + 1))
        for j in range(6):
            cols = slice(128 * j, 128 * (j + 1))
            q[rows, cols] = (rot(wide[rows, cols], cosine[rows], sine[rows]) * 0.125).astype(BF)
            kcols = slice(D + 128 * j, D + 128 * (j + 1))
            kv[rows, cols] = rot(wide[rows, kcols], cosine[rows], sine[rows]).astype(BF)
        kv[rows, D:] = wide[rows, 2 * D :].astype(BF)


def project(idx, x, gain, shift, bias, cosine, sine, pieces):
    return kernel_call(
        project_body,
        [smem_spec()] + [vmem_spec()] * 6 + [any_spec()] * 8,
        [sds((ROWS, D), BF), sds((ROWS, D), BF), sds((ROWS, 2 * D), BF)],
        [vmem_spec()] * 3,
        [
            pltpu.VMEM((QUARTERS, D, PARTS), BF),
            pltpu.VMEM((ROWS, 3 * D), F32),
            pltpu.SemaphoreType.DMA((32,)),
        ],
        (idx, x, gain, shift, bias, cosine, sine, *pieces),
        2 * ROWS * D * 3 * D,
        8e6,
        name="project",
    )


def load_near(idx, own, near, kvn, kvc, sems):
    clean = idx[2] == 1
    copy = pltpu.make_async_copy(own, kvn, sems.at[0])
    copy.start()
    a = pltpu.make_async_copy(own, kvc, sems.at[1])
    b = pltpu.make_async_copy(near, kvc, sems.at[1])
    pl.when(clean)(a.start)
    pl.when(jnp.logical_not(clean))(b.start)
    return [copy, a]


def load_far(idx, far, far_near, kvr, sem):
    clean = idx[2] == 1
    a = pltpu.make_async_copy(far, kvr, sem)
    b = pltpu.make_async_copy(far_near, kvr, sem)
    pl.when(clean)(a.start)
    pl.when(jnp.logical_not(clean))(b.start)
    return a


NEAR_TILES = {0: [(0, [(0, True)]), (1, [(1, True), (0, False)])], 1: [(1, [(1, True)]), (0, [(0, True), (1, False)])]}
FAR_TILES = {0: [(1, [0, 1])], 1: [(1, [0]), (0, [0])]}


def set_masks(idx, bias, bias_n, query_dim):
    clean, level = idx[2], idx[4]
    qi = lax.shift_right_logical(lax.broadcasted_iota(jnp.int32, (HALF, HALF), query_dim), level)
    ki = lax.shift_right_logical(lax.broadcasted_iota(jnp.int32, (HALF, HALF), 1 - query_dim), level)
    bias[...] = jnp.where(ki < qi + clean, 0.0, MASKED)
    same = jnp.where(ki == qi, 0, 1) + clean
    bias_n[...] = jnp.where(same[:128, :128] == 0, 0.0, MASKED)


def lanes(rows):
    return lax.broadcasted_iota(jnp.int32, (rows, 128), 1)


def one_head(v, side):
    low_lane = lanes(v.shape[0]) < 64
    return jnp.where(low_lane if side == 0 else jnp.logical_not(low_lane), v, jnp.zeros_like(v))


def pair_cols(hp):
    off = pl.multiple_of(hp * 128, 128)
    return pl.ds(off, 128), pl.ds(pl.multiple_of(D + off, 128), 128)


def row_max(s):
    return jnp.max(s, axis=-1, keepdims=True)


def with_ones(v):
    return jnp.concatenate([v, jnp.ones_like(v)], axis=1)


def half_rows(half):
    return slice(HALF * half, HALF * (half + 1))


def attend_near_body(idx, q, own, near, acc, tops, counts, kvn, kvc, bias, bias_n, sems):
    waits = load_near(idx, own, near, kvn, kvc, sems)
    set_masks(idx, bias, bias_n, 0)
    tops[...] = jnp.zeros_like(tops)
    counts[...] = jnp.ones_like(counts)
    for copy in waits:
        copy.wait()

    def run(tiles):
        def pair(hp, carry):
            cols, vcols = pair_cols(hp)
            lane = lanes(HALF)
            for half, sources in tiles:
                rows = half_rows(half)
                q2 = q[rows, cols]
                sides = []
                for side in range(2):
                    qm = one_head(q2, side)
                    scores = []
                    for kh, diagonal in sources:
                        s = dot_nt(qm, kvc[half_rows(kh), cols])
                        scores.append(s + bias[...] if diagonal else s)
                    blocks = [slice(HALF * half + 128 * t, HALF * half + 128 * (t + 1)) for t in range(2)]
                    parts = [slice(128 * t, 128 * (t + 1)) for t in range(2)]
                    mine = [dot_nt(qm[part], kvn[block, cols]) + bias_n[...] for part, block in zip(parts, blocks)]
                    top = jnp.concatenate([row_max(s) for s in mine], axis=0)
                    for s in scores:
                        top = jnp.maximum(top, row_max(s))
                    total = jnp.concatenate(
                        [
                            dot(jnp.exp(s - top[part]).astype(BF), with_ones(kvn[block, vcols]))
                            for s, part, block in zip(mine, parts, blocks)
                        ],
                        axis=0,
                    )
                    for s, (kh, diagonal) in zip(scores, sources):
                        total = total + dot(jnp.exp(s - top).astype(BF), with_ones(kvc[half_rows(kh), vcols]))
                    sides.append((total[:, :128], top, total[:, 128:]))
                acc[rows, cols] = jnp.where(lane < 64, sides[0][0], sides[1][0])
                for target, at in ((tops, 1), (counts, 2)):
                    target[rows] = jnp.where(
                        lane == 2 * hp, sides[0][at], jnp.where(lane == 2 * hp + 1, sides[1][at], target[rows])
                    )
            return carry

        lax.fori_loop(0, 6, pair, 0)

    for zl in range(2):
        pl.when(idx[3] == zl)(functools.partial(run, NEAR_TILES[zl]))


def attend_near(idx, q, own, near):
    return kernel_call(
        attend_near_body,
        [smem_spec(), vmem_spec()] + [any_spec()] * 2,
        [sds((ROWS, D), F32), sds((ROWS, 128), F32), sds((ROWS, 128), F32)],
        [vmem_spec()] * 3,
        [
            pltpu.VMEM((ROWS, 2 * D), BF),
            pltpu.VMEM((ROWS, 2 * D), BF),
            pltpu.VMEM((HALF, HALF), F32),
            pltpu.VMEM((128, 128), F32),
            pltpu.SemaphoreType.DMA((2,)),
        ],
        (idx, q, own, near),
        8e9,
        6e6,
        name="attend_near",
    )


def attend_far_body(idx, q, far, far_near, acc, tops, counts, o, lse, kvr, last, sem):
    copy = load_far(idx, far, far_near, kvr, sem)
    last[...] = tops[...] + jnp.log(counts[...])
    copy.wait()

    def column(values, head):
        return jnp.sum(jnp.where(lanes(HALF) == head, values, 0.0), axis=-1, keepdims=True)

    def run(tiles):
        covered = [half for half, _ in tiles]

        def pair(hp, carry):
            cols, vcols = pair_cols(hp)
            lane = lanes(HALF)
            for half in range(2):
                rows = half_rows(half)
                if half in covered:
                    sources = dict(tiles)[half]
                    q2 = q[rows, cols]
                    sides = []
                    for side in range(2):
                        qm = one_head(q2, side)
                        scores = [dot_nt(qm, kvr[half_rows(kh), cols]) for kh in sources]
                        before = column(tops[rows], 2 * hp + side)
                        top = before
                        for s in scores:
                            top = jnp.maximum(top, row_max(s))
                        shrink = jnp.exp(before - top)
                        total = None
                        for s, kh in zip(scores, sources):
                            part = dot(jnp.exp(s - top).astype(BF), with_ones(kvr[half_rows(kh), vcols]))
                            total = part if total is None else total + part
                        count = column(counts[rows], 2 * hp + side) * shrink + total[:, 128:]
                        value = (acc[rows, cols] * shrink + total[:, :128]) / count
                        sides.append((value, top + jnp.log(count)))
                    last[rows] = jnp.where(
                        lane == 2 * hp, sides[0][1], jnp.where(lane == 2 * hp + 1, sides[1][1], last[rows])
                    )
                else:
                    sides = [(acc[rows, cols] / column(counts[rows], 2 * hp + side),) for side in range(2)]
                o[rows, cols] = jnp.where(lane < 64, sides[0][0], sides[1][0]).astype(BF)
            return carry

        lax.fori_loop(0, 6, pair, 0)

    for zl in range(2):
        pl.when(idx[3] == zl)(functools.partial(run, FAR_TILES[zl]))
    across = jnp.transpose(last[...])
    for head in range(12):
        lse[head] = across[head : head + 1]


def attend_far(idx, q, far, far_near, state):
    return kernel_call(
        attend_far_body,
        [smem_spec(), vmem_spec()] + [any_spec()] * 2 + [vmem_spec()] * 3,
        [sds((ROWS, D), BF), sds((12, 1, ROWS), F32)],
        [vmem_spec()] * 2,
        [
            pltpu.VMEM((ROWS, 2 * D), BF),
            pltpu.VMEM((ROWS, 128), F32),
            pltpu.SemaphoreType.DMA,
        ],
        (idx, q, far, far_near, *state),
        5e9,
        6e6,
        name="attend_far",
    )


def feed_body(idx, x, o, gain, shift, out_bias, down_bias, up_bias, *rest):
    pieces, (x2, x1, h2, g, gp, ups, downs, packed, outw, sems, sems_o) = rest[:8], rest[8:]
    first = packed_copies(pieces, idx, sems_o, packed)
    later = up_down_copies(pieces, idx, sems, ups, downs)
    for copy in first + later:
        copy.start()
    for copy in first:
        copy.wait()
    unpack_output(packed, outw)
    x1[...] = x[...] + (dot(o[...], outw[...]) + out_bias[...])

    def norm_rows(i, carry):
        rows = rows_at(i * 128, 128, 128)
        unit, _ = norm_parts(x1[rows])
        h2[rows] = (unit * gain[...] + shift[...]).astype(BF)
        x2[rows] = x1[rows] + down_bias[...]
        return carry

    lax.fori_loop(0, 4, norm_rows, 0)
    for copy in later:
        copy.wait()

    def hidden(k, carry):
        for n in range(3):
            cols = slice(256 * n, 256 * (n + 1))
            u = dot(h2[...], ups[k, :, cols]) + up_bias[k, :, cols]
            uu = u * u
            t = jnp.tanh(0.7978845608028654 * u * (1.0 + 0.044715 * uu))
            half_t = 0.5 + 0.5 * t
            g[k, :, cols] = (u * half_t).astype(BF)
            slope = half_t + (0.5 * 0.7978845608028654) * u * (1.0 - t * t) * (1.0 + 0.134145 * uu)
            gp[k, :, cols] = slope.astype(BF)
        x2[...] += dot(g[k], downs[k])
        return carry

    lax.fori_loop(0, QUARTERS, hidden, 0)


WEIGHT_SCRATCH = [
    ((QUARTERS, D, D), BF),
    ((QUARTERS, D, D), BF),
    ((QUARTERS, 8, 32, D), BF),
    ((D, D), BF),
]


def feed(idx, x, o, gain, shift, out_bias, down_bias, up_bias, pieces):
    return kernel_call(
        feed_body,
        [smem_spec()] + [vmem_spec()] * 7 + [any_spec()] * 8,
        [
            sds((ROWS, D), F32),
            sds((ROWS, D), F32),
            sds((ROWS, D), BF),
            sds((QUARTERS, ROWS, D), BF),
            sds((QUARTERS, ROWS, D), BF),
        ],
        [vmem_spec()] * 5,
        [pltpu.VMEM(s, t) for s, t in WEIGHT_SCRATCH]
        + [pltpu.SemaphoreType.DMA((64,)), pltpu.SemaphoreType.DMA((32,))],
        (idx, x, o, gain, shift, out_bias, down_bias, up_bias, *pieces),
        2 * ROWS * D * D * 9,
        25e6,
        name="feed",
    )


def feed_back_body(idx, e, x1, gp, gain, *rest):
    pieces, (dm, dz, e1, da, do, small, ups, downs, packed, outw, dh2, hidden_sums, sems, sems_o) = rest[:8], rest[8:]
    first = packed_copies(pieces, idx, sems_o, packed)
    later = up_down_copies(pieces, idx, sems, ups, downs)
    for copy in later + first:
        copy.start()
    dm[...] = e[...].astype(BF)
    small[4:5] = jnp.sum(dm[...].astype(F32), axis=0, keepdims=True)
    dh2[...] = jnp.zeros_like(dh2)
    for copy in later:
        copy.wait()

    def hidden(k, carry):
        zq = idx[1] ^ k
        for n in range(3):
            cols = slice(256 * n, 256 * (n + 1))
            part = (dot_nt(dm[...], downs[k, cols]) * gp[k, :, cols].astype(F32)).astype(BF)
            dz[k, :, cols] = part
            hidden_sums[zq, :, cols] = jnp.sum(part.astype(F32), axis=0, keepdims=True)
        dh2[...] += dot_nt(dz[k], ups[k])
        return carry

    lax.fori_loop(0, QUARTERS, hidden, 0)
    for copy in first:
        copy.wait()
    unpack_output(packed, outw)
    for zq in range(QUARTERS):
        small[zq : zq + 1] = hidden_sums[zq]
    small[5:8] = jnp.zeros((3, D), F32)

    def norm_rows(i, carry):
        rows = rows_at(i * 128, 128, 128)
        unit, inverse = norm_parts(x1[rows])
        grad = dh2[rows]
        up = e[rows] + norm_backward(grad, unit, inverse, gain[...])
        e1[rows] = up
        low = up.astype(BF)
        da[rows] = low
        small[5:6] += jnp.sum(low.astype(F32), axis=0, keepdims=True)
        small[6:7] += jnp.sum(grad * unit, axis=0, keepdims=True)
        small[7:8] += jnp.sum(grad, axis=0, keepdims=True)
        return carry

    lax.fori_loop(0, 4, norm_rows, 0)
    do[...] = dot_nt(da[...], outw[...]).astype(BF)


def feed_back(idx, e, x1, gp, gain, pieces):
    return kernel_call(
        feed_back_body,
        [smem_spec()] + [vmem_spec()] * 4 + [any_spec()] * 8,
        [
            sds((ROWS, D), BF),
            sds((QUARTERS, ROWS, D), BF),
            sds((ROWS, D), F32),
            sds((ROWS, D), BF),
            sds((ROWS, D), BF),
            sds((8, D), F32),
        ],
        [vmem_spec()] * 6,
        [pltpu.VMEM(s, t) for s, t in WEIGHT_SCRATCH]
        + [pltpu.VMEM((ROWS, D), F32), pltpu.VMEM((QUARTERS, 1, D), F32), pltpu.SemaphoreType.DMA((64,)), pltpu.SemaphoreType.DMA((32,))],
        (idx, e, x1, gp, gain, *pieces),
        2 * ROWS * D * D * 9,
        25e6,
        name="feed_back",
    )


def spread(idx, keep, send, source, k, wq, rows, sem):
    w8, mine = idx[0], idx[2]
    j = (wq >> 1) ^ (w8 >> 1)
    turned = ((j & 1) << 1) | (j >> 1)
    at = ((k & 1) << 1) | (k >> 1)
    here, there = jnp.where(mine == 1, j, turned), jnp.where(mine == 1, turned, j)
    a = pltpu.make_async_copy(source, keep.at[here, at, rows], sem)
    b = pltpu.make_async_copy(source, send.at[there, at, rows], sem)
    pl.when((wq & 1) == mine)(a.start)
    pl.when((wq & 1) != mine)(b.start)
    return a


def feed_grads_body(idx, g, dm, h2, dz, o, da, keep, send, flipped, turned, d_up, d_down, d_out, sems):
    waits = []
    flipped[...] = jnp.transpose(o[...])
    turned[...] = dot(flipped[...], da[...]).astype(BF)
    for zq in range(QUARTERS):
        for chip in range(4):
            for part in range(2):
                for s in range(4):
                    rows, cols = slice(16 * (s // 2), 16 * (s // 2) + 16), slice(384 * (s % 2), 384 * (s % 2) + 384)
                    if s == 3:
                        block = jnp.zeros((16, 384), BF)
                    else:
                        row = HEADS_COLS * zq + 48 * chip + 16 * s
                        block = turned[row : row + 16, 384 * part : 384 * part + 384]
                    d_out[zq, 2 * chip + part, rows, cols] = block
    for zq in range(QUARTERS):
        k = idx[1] ^ zq
        for wq in range(8):
            sem = sems.at[len(waits)]
            waits.append(spread(idx, keep, send, d_out.at[zq, wq], k, wq, pl.ds(2 * PIECE, 32), sem))
    for k in range(QUARTERS):
        flipped[...] = jnp.transpose(g[k])
        d_down[k] = dot(flipped[...], dm[...]).astype(BF)
        for wq in range(8):
            sem = sems.at[len(waits)]
            source = d_down.at[k, pl.ds(PIECE * wq, PIECE)]
            waits.append(spread(idx, keep, send, source, k, wq, pl.ds(PIECE, PIECE), sem))
    flipped[...] = jnp.transpose(h2[...])
    for k in range(QUARTERS):
        d_up[k] = dot(flipped[...], dz[k]).astype(BF)
        for wq in range(8):
            sem = sems.at[len(waits)]
            source = d_up.at[k, pl.ds(PIECE * wq, PIECE)]
            waits.append(spread(idx, keep, send, source, k, wq, pl.ds(0, PIECE), sem))
    for copy in waits:
        copy.wait()


def feed_grads(idx, g, dm, h2, dz, o, da):
    return kernel_call(
        feed_grads_body,
        [smem_spec()] + [vmem_spec()] * 6,
        [sds((4, QUARTERS, PACK, D), BF)] * 2,
        [any_spec()] * 2,
        [
            pltpu.VMEM((D, ROWS), BF),
            pltpu.VMEM((D, D), BF),
            pltpu.VMEM((QUARTERS, D, D), BF),
            pltpu.VMEM((QUARTERS, D, D), BF),
            pltpu.VMEM((QUARTERS, 8, 32, D), BF),
            pltpu.SemaphoreType.DMA((96,)),
        ],
        (idx, g, dm, h2, dz, o, da),
        2 * ROWS * D * D * 9,
        25e6,
        name="feed_grads",
    )


def back_tile(q, do, lse, drow, cols, hp, k2, v2, qrow, n, bias_here):
    q2, g2 = q[qrow : qrow + n, cols], do[qrow : qrow + n, cols]
    sums = None
    for side in range(2):
        qm, gm, km = one_head(q2, side), one_head(g2, side), one_head(k2, side)
        head = 2 * hp + side
        s = dot_nt(k2, qm)
        if bias_here is not None:
            s = s + bias_here
        p = jnp.exp(s - lse[head, :, qrow : qrow + n])
        dp = dot_nt(v2, gm)
        ds = (p * (dp - drow[head, :, qrow : qrow + n])).astype(BF)
        parts = (dot(ds, qm), dot(p.astype(BF), gm), dot_tn(ds, km))
        sums = parts if sums is None else tuple(a + b for a, b in zip(sums, parts))
    return sums


def attend_back_far_body(idx, q, do, o, lse, far, far_near, dq, dr, drow, kvr, dcol, sem):
    copy = load_far(idx, far, far_near, kvr, sem)
    dcol[...] = jnp.zeros_like(dcol)

    def products(hp, carry):
        cols, _ = pair_cols(hp)
        lane = lanes(ROWS)
        both = do[:, cols].astype(F32) * o[:, cols].astype(F32)
        first = jnp.sum(jnp.where(lane < 64, both, 0.0), axis=-1, keepdims=True)
        second = jnp.sum(jnp.where(lane < 64, 0.0, both), axis=-1, keepdims=True)
        dcol[...] = jnp.where(lane == 2 * hp, first, jnp.where(lane == 2 * hp + 1, second, dcol[...]))
        return carry

    lax.fori_loop(0, 6, products, 0)
    across = jnp.transpose(dcol[...])
    for head in range(12):
        drow[head] = across[head : head + 1]
    copy.wait()

    def run(tiles):
        def pair(hp, carry):
            cols, vcols = pair_cols(hp)
            dq_half = [None, None]
            for kh in range(2):
                keys = half_rows(kh)
                total = None
                for half, sources in tiles:
                    if kh in sources:
                        parts = back_tile(
                            q, do, lse, drow, cols, hp, kvr[keys, cols], kvr[keys, vcols], HALF * half, HALF, None
                        )
                        total = parts[:2] if total is None else (total[0] + parts[0], total[1] + parts[1])
                        dq_half[half] = parts[2] if dq_half[half] is None else dq_half[half] + parts[2]
                if total is None:
                    total = (jnp.zeros((HALF, 128), F32),) * 2
                dr[keys, cols] = total[0].astype(BF)
                dr[keys, vcols] = total[1].astype(BF)
            for half in range(2):
                part = dq_half[half]
                dq[half_rows(half), cols] = jnp.zeros((HALF, 128), F32) if part is None else part
            return carry

        lax.fori_loop(0, 6, pair, 0)

    for zl in range(2):
        pl.when(idx[3] == zl)(functools.partial(run, FAR_TILES[zl]))


def attend_back_far(idx, q, do, o, lse, far, far_near):
    return kernel_call(
        attend_back_far_body,
        [smem_spec()] + [vmem_spec()] * 4 + [any_spec()] * 2,
        [sds((ROWS, D), F32), sds((ROWS, 2 * D), BF), sds((12, 1, ROWS), F32)],
        [vmem_spec()] * 3,
        [
            pltpu.VMEM((ROWS, 2 * D), BF),
            pltpu.VMEM((ROWS, 128), F32),
            pltpu.SemaphoreType.DMA,
        ],
        (idx, q, do, o, lse, far, far_near),
        12e9,
        8e6,
        name="attend_back_far",
    )


def attend_back_near_body(idx, q, do, lse, drow, dq_far, own, near, dq, dn, dc, kvn, kvc, bias, bias_n, sems):
    waits = load_near(idx, own, near, kvn, kvc, sems)
    set_masks(idx, bias, bias_n, 1)
    for copy in waits:
        copy.wait()

    def run(tiles):
        def pair(hp, carry):
            cols, vcols = pair_cols(hp)
            dq_half = [None, None]
            for half in range(2):
                pieces = []
                for t in range(2):
                    rows = slice(HALF * half + 128 * t, HALF * half + 128 * (t + 1))
                    dk, dv, dqs = back_tile(
                        q, do, lse, drow, cols, hp, kvn[rows, cols], kvn[rows, vcols], rows.start, 128, bias_n[...]
                    )
                    dn[rows, cols] = dk.astype(BF)
                    dn[rows, vcols] = dv.astype(BF)
                    pieces.append(dqs)
                dq_half[half] = dq_far[half_rows(half), cols] + jnp.concatenate(pieces, axis=0)
            for kh in range(2):
                keys = half_rows(kh)
                total = None
                for half, sources in tiles:
                    if kh in dict(sources):
                        parts = back_tile(
                            q,
                            do,
                            lse,
                            drow,
                            cols,
                            hp,
                            kvc[keys, cols],
                            kvc[keys, vcols],
                            HALF * half,
                            HALF,
                            bias[...] if dict(sources)[kh] else None,
                        )
                        total = parts[:2] if total is None else (total[0] + parts[0], total[1] + parts[1])
                        dq_half[half] = dq_half[half] + parts[2]
                dc[keys, cols] = total[0].astype(BF)
                dc[keys, vcols] = total[1].astype(BF)
            for half in range(2):
                dq[half_rows(half), cols] = dq_half[half] * 0.125
            return carry

        lax.fori_loop(0, 6, pair, 0)

    for zl in range(2):
        pl.when(idx[3] == zl)(functools.partial(run, NEAR_TILES[zl]))


def attend_back_near(idx, q, do, lse, drow, dq_far, own, near):
    return kernel_call(
        attend_back_near_body,
        [smem_spec()] + [vmem_spec()] * 5 + [any_spec()] * 2,
        [sds((ROWS, D), F32), sds((ROWS, 2 * D), BF), sds((ROWS, 2 * D), BF)],
        [vmem_spec()] * 3,
        [
            pltpu.VMEM((ROWS, 2 * D), BF),
            pltpu.VMEM((ROWS, 2 * D), BF),
            pltpu.VMEM((HALF, HALF), F32),
            pltpu.VMEM((128, 128), F32),
            pltpu.SemaphoreType.DMA((2,)),
        ],
        (idx, q, do, lse, drow, dq_far, own, near),
        18e9,
        12e6,
        name="attend_back_near",
    )


def project_back_body(idx, dq, dn, dcr, got, far, cosine, sine, x, e1, gain, *rest):
    pieces, (dpz, e, small, weights, wide, sems) = rest[:8], rest[8:]
    copies = mixer_copies(pieces, idx, sems, weights)
    for copy in copies:
        copy.start()
    noisy = idx[2] == 0
    for half in range(2):
        rows = slice(HALF * half, HALF * (half + 1))
        for j in range(6):
            cols = slice(128 * j, 128 * (j + 1))
            wide[rows, cols] = unrot(dq[rows, cols], cosine[rows], sine[rows])

        def total(cols, at=rows):
            summed = dcr[at, cols].astype(F32) + got[at, cols].astype(F32) + far[at, cols].astype(F32)
            return jnp.where(noisy, dn[at, cols].astype(F32), summed)

        for j in range(6):
            cols = slice(128 * j, 128 * (j + 1))
            wide[rows, D + 128 * j : D + 128 * (j + 1)] = unrot(total(cols), cosine[rows], sine[rows])
        wide[rows, 2 * D :] = total(slice(D, 2 * D))
    for copy in copies:
        copy.wait()
    small[...] = jnp.zeros_like(small)
    for zq in range(QUARTERS):
        for part in range(3):
            col = D * part + HEADS_COLS * zq
            dpz[zq, :, HEADS_COLS * part : HEADS_COLS * (part + 1)] = wide[:, col : col + HEADS_COLS].astype(BF)
        small[zq : zq + 1, :PARTS] = jnp.sum(dpz[zq].astype(F32), axis=0, keepdims=True)
        piece = dot_nt(dpz[zq], weights[zq])
        if zq == 0:
            e[...] = piece
        else:
            e[...] += piece

    def norm_rows(i, carry):
        rows = rows_at(i * 128, 128, 128)
        unit, inverse = norm_parts(x[rows])
        grad = e[rows]
        small[4:5] += jnp.sum(grad * unit, axis=0, keepdims=True)
        small[5:6] += jnp.sum(grad, axis=0, keepdims=True)
        e[rows] = e1[rows] + norm_backward(grad, unit, inverse, gain[...])
        return carry

    lax.fori_loop(0, 4, norm_rows, 0)


def project_back(idx, dq, dn, dcr, got, far, cosine, sine, x, e1, gain, pieces):
    return kernel_call(
        project_back_body,
        [smem_spec()] + [vmem_spec()] * 10 + [any_spec()] * 8,
        [sds((QUARTERS, ROWS, PARTS), BF), sds((ROWS, D), F32), sds((8, D), F32)],
        [vmem_spec()] * 3,
        [
            pltpu.VMEM((QUARTERS, D, PARTS), BF),
            pltpu.VMEM((ROWS, 3 * D), F32),
            pltpu.SemaphoreType.DMA((32,)),
        ],
        (idx, dq, dn, dcr, got, far, cosine, sine, x, e1, gain, *pieces),
        2 * ROWS * D * 3 * D,
        12e6,
        name="project_back",
    )


def project_grads_body(idx, h1, dpz, keep, send, flipped, stage, sems):
    waits = []
    flipped[...] = jnp.transpose(h1[...])
    for zq in range(QUARTERS):
        k = idx[1] ^ zq
        stage[zq] = dot(flipped[...], dpz[zq]).astype(BF)
        for wq in range(8):
            sem = sems.at[len(waits)]
            source = stage.at[zq, pl.ds(PIECE * wq, PIECE)]
            waits.append(spread(idx, keep, send, source, k, wq, pl.ds(0, PIECE), sem))
    for copy in waits:
        copy.wait()


def project_grads(idx, h1, dpz):
    return kernel_call(
        project_grads_body,
        [smem_spec()] + [vmem_spec()] * 2,
        [sds((4, QUARTERS, PIECE, PARTS), BF)] * 2,
        [any_spec()] * 2,
        [
            pltpu.VMEM((D, ROWS), BF),
            pltpu.VMEM((QUARTERS, D, PARTS), BF),
            pltpu.SemaphoreType.DMA((32,)),
        ],
        (idx, h1, dpz),
        2 * ROWS * D * 3 * D,
        9e6,
        name="project_grads",
    )


def finish_mixer_body(layer, filled, idx, *rest):
    pieces, rest = rest[:8], rest[8:]
    if filled:
        rest = rest[1:]
    out, stage, sem = rest
    for flip, piece in zip(flips(idx), pieces):
        stage[rows_at((idx[0] ^ flip) * PIECE, PIECE, 32)] = piece[...].astype(F32)
    copy = pltpu.make_async_copy(stage, out.at[layer], sem)
    copy.start()
    copy.wait()


def finish_mixer(idx, layer, layers, pieces, before):
    filled = before is not None
    return kernel_call(
        functools.partial(finish_mixer_body, layer, filled),
        [smem_spec()] + [vmem_spec()] * 8 + [any_spec()] * filled,
        sds((layers, D, PARTS), F32),
        any_spec(),
        [pltpu.VMEM((D, PARTS), F32), pltpu.SemaphoreType.DMA],
        (idx, *pieces) + ((before,) if filled else ()),
        1e6,
        4e6,
        aliases={9: 0} if filled else None,
        name="finish_mixer",
    )


def finish_feed_body(layer, filled, idx, *rest):
    pieces, rest = rest[:8], rest[8:]
    if filled:
        rest = rest[3:]
    up, down, out, up_s, down_s, out_s, sems = rest
    for flip, piece in zip(flips(idx), pieces):
        wq = idx[0] ^ flip
        rows = rows_at(wq * PIECE, PIECE, 32)
        up_s[rows] = piece[:PIECE].astype(F32)
        down_s[rows] = piece[PIECE : 2 * PIECE].astype(F32)
        cols = pl.ds(pl.multiple_of((wq & 1) * 384, 128), 384)
        for s in range(3):
            row = 2 * PIECE + 16 * (s // 2)
            block = piece[row : row + 16, 384 * (s % 2) : 384 * (s % 2) + 384]
            out_s[rows_at((wq >> 1) * 48 + 16 * s, 16, 16), cols] = block.astype(F32)
    copies = [
        pltpu.make_async_copy(stage, whole.at[layer], sems.at[i])
        for i, (stage, whole) in enumerate(((up_s, up), (down_s, down), (out_s, out)))
    ]
    for copy in copies:
        copy.start()
    for copy in copies:
        copy.wait()


def finish_feed(idx, layer, layers, pieces, before):
    filled = before is not None
    return kernel_call(
        functools.partial(finish_feed_body, layer, filled),
        [smem_spec()] + [vmem_spec()] * 8 + [any_spec()] * (3 * filled),
        [sds((layers, D, D), F32), sds((layers, D, D), F32), sds((layers, HEADS_COLS, D), F32)],
        [any_spec()] * 3,
        [
            pltpu.VMEM((D, D), F32),
            pltpu.VMEM((D, D), F32),
            pltpu.VMEM((HEADS_COLS, D), F32),
            pltpu.SemaphoreType.DMA((3,)),
        ],
        (idx, *pieces) + (tuple(before) if filled else ()),
        1e6,
        8e6,
        aliases={9: 0, 10: 1, 11: 2} if filled else None,
        name="finish_feed",
    )


def pack_body(idx, ups, downs, outs, *rest):
    targets, (zeros, sems) = rest[:-2], rest[-2:]
    zeros[...] = jnp.zeros_like(zeros)
    rows = rows_at(idx[0] * PIECE, PIECE, 32)
    cols = pl.ds(pl.multiple_of(idx[2] * 384, 128), 384)
    copies = []
    for layer, target in enumerate(targets):
        moves = [
            (ups.at[layer, rows], target.at[pl.ds(0, PIECE)]),
            (downs.at[layer, rows], target.at[pl.ds(PIECE, PIECE)]),
        ]
        for s in range(4):
            place = target.at[pl.ds(2 * PIECE + 16 * (s // 2), 16), pl.ds(384 * (s % 2), 384)]
            if s == 3:
                moves.append((zeros, place))
            else:
                moves.append((outs.at[layer, rows_at((idx[0] >> 1) * 48 + 16 * s, 16, 16), cols], place))
        for source, place in moves:
            copies.append(pltpu.make_async_copy(source, place, sems.at[len(copies)]))
    for copy in copies:
        copy.start()
    for copy in copies:
        copy.wait()


def pack(idx, ups, downs, outs):
    layers = ups.shape[0]
    return kernel_call(
        pack_body,
        [smem_spec()] + [any_spec()] * 3,
        [sds((PACK, D), BF)] * layers,
        [vmem_spec()] * layers,
        [pltpu.VMEM((16, 384), BF), pltpu.SemaphoreType.DMA((6 * layers,))],
        (idx, ups, downs, outs),
        1e6,
        1e6,
        name="pack",
    )


def flip_wide(x, bit):
    return lax.ppermute(x, "wide", [(i, i ^ bit) for i in range(lax.axis_size("wide"))])


def flip_narrow(x, bit):
    return lax.ppermute(x, "narrow", [(i, i ^ bit) for i in range(QUARTERS)])


def first_axis(x):
    return lax.ppermute(x, "wide", [(i, i ^ (4 if i & 1 else 2)) for i in range(lax.axis_size("wide"))])


def second_axis(x):
    return lax.ppermute(x, "wide", [(i, i ^ (2 if i & 1 else 4)) for i in range(lax.axis_size("wide"))])


def gate_body(*refs):
    return None


def gate(tree):
    leaves, shape = jax.tree.flatten(tree)
    out = pl.pallas_call(
        gate_body,
        in_specs=[any_spec() for _ in leaves],
        out_specs=[any_spec() for _ in leaves],
        out_shape=[sds(x.shape, x.dtype) for x in leaves],
        input_output_aliases={i: i for i in range(len(leaves))},
        name="gate",
    )(*leaves)
    return jax.tree.unflatten(shape, out)


def gather_direct(piece):
    return [piece] + [flip_narrow(piece, k) for k in ORDER[1:]]


def gather_far(piece):
    return piece, flip_narrow(piece, 2)


def gather_near(pair):
    pair = jnp.stack(pair)
    return pair, flip_narrow(pair, 1)


def whole(parts):
    return jnp.stack(parts) if parts[0].ndim == 2 else jnp.concatenate(parts)


def gather_first(own):
    return own, first_axis(own)


def gather_second(parts):
    own, first = parts
    return [own, first, second_axis(own), second_axis(first)]


def gather_last(here):
    return here + [flip_wide(x, 1) for x in here]


def added(*terms):
    return functools.reduce(jnp.add, [t.astype(F32) for t in terms]).astype(BF)


def reduce_core(pair):
    keep, send = pair
    return keep, flip_wide(send, 1)


def reduce_first(pair):
    keep, got = pair
    return keep, got, first_axis(added(keep[2:], got[2:]))


def reduce_second(parts):
    keep, got, first = parts
    return keep, got, first, second_axis(added(keep[1], got[1], first[1]))


def reduce_near(parts):
    keep, got, first, second = parts
    total = added(keep[0], got[0], first[0], second)
    bit = 8
    while bit < lax.axis_size("wide"):
        total = added(total, flip_wide(total, bit))
        bit *= 2
    return total, flip_narrow(total[2:], 1)


def reduce_far(parts):
    total, near = parts
    return total, near, flip_narrow(added(total[1], near[1]), 2)


def spread_first(parts):
    total, near, far = parts
    return gather_first(added(total[0], near[0], far))


def device_pairs(move):
    pairs = []
    for w in range(lax.axis_size("wide")):
        for z in range(QUARTERS):
            target = move(w, z)
            if target is not None:
                pairs.append((w * QUARTERS + z, target[0] * QUARTERS + target[1]))
    return pairs


BOTH = ("wide", "narrow")


def relocate(rows):
    first = device_pairs(lambda w, z: ((w & ~1) | (z >> 1), ((w & 1) << 1) | (z & 1)))
    second = device_pairs(lambda w, z: ((w & ~1) | (z >> 1), ((w & 1) << 1) | (1 - (z & 1))))
    return lax.ppermute(rows[:HALF], BOTH, first), lax.ppermute(rows[HALF:], BOTH, second)


def between_chips(x):
    pairs = device_pairs(lambda w, z: (w, z ^ 1) if w & 1 else None)
    return lax.ppermute(x, BOTH, pairs)


def within_chip(x, source):
    pairs = [(i, i ^ 1) for i in range(lax.axis_size("wide")) if (i & 1) == source]
    return lax.ppermute(x, "wide", pairs)


def per_device(
    tokens,
    block_size,
    norm_gain,
    norm_shift,
    mixer_weight,
    mixer_bias,
    output_weight,
    output_bias,
    up_weight,
    up_bias,
    down_weight,
    cotangent,
):
    layers = norm_gain.shape[0]
    w, z = lax.axis_index("wide"), lax.axis_index("narrow")
    w8, core, low = w & 7, w & 1, z & 1
    sizes = jnp.where((z >> 1) == core, block_size, flip_wide(block_size, 1))[0]
    level = 2 + (sizes >= 8).astype(jnp.int32) + (sizes >= 16).astype(jnp.int32)
    idx = jnp.stack([w8, z, core, low, level, w8, w8, w8]).astype(jnp.int32)

    bases = jnp.where(low == 0, jnp.array([0, 768]), jnp.array([512, 256]))
    position = (bases[:, None] + jnp.arange(HALF)[None, :]).reshape(ROWS).astype(F32)
    halfway = HEAD_DIM // 2
    frequency = jnp.exp(jnp.arange(halfway, dtype=F32) * (-math.log(10000.0) / halfway))
    angle = position[:, None] * frequency[None, :]
    cosine = jnp.tile(jnp.cos(angle), (1, 4))
    sine = jnp.sin(angle)
    sine = jnp.concatenate([-sine, sine, -sine, sine], axis=1)

    def bias_pieces(layer):
        return mixer_bias[layer].reshape(PARTS), up_bias[layer]

    biases = jnp.concatenate([t for layer in range(layers) for t in bias_pieces(layer)])
    width = PARTS + D

    def bias_of(layer, start, size):
        at = width * layer + start
        by_flip = dict(zip(ORDER, biases))
        return jnp.stack([by_flip[k][at : at + size] for k in range(QUARTERS)])[:, None]

    def mixer_piece(layer):
        return lax.dynamic_slice_in_dim(mixer_weight[layer], w8 * PIECE, PIECE, 0).reshape(PIECE, PARTS)

    def run_project(layer, x, pieces):
        gain, shift = norm_gain[layer], norm_shift[layer]
        return project(idx, x, gain[0:1], shift[0:1], bias_of(layer, 0, PARTS), cosine, sine, pieces)

    def run_feed(layer, x, o, pieces):
        gain, shift, bias = norm_gain[layer], norm_shift[layer], output_bias[layer]
        return feed(
            idx, x, o, gain[1:2], shift[1:2], bias[0:1], bias[1:2], bias_of(layer, PARTS, D), pieces
        )

    mixer0 = gather_direct(mixer_piece(0))
    feed0, feed1 = pack(idx, up_weight, down_weight, output_weight)
    mixer0, tokens, feed0, biases = gate((mixer0, tokens, feed0, biases))
    mixer0 = gather_first(whole(mixer0))
    rows = relocate(tokens)
    mixer0, feed0, biases, mixer1 = gate((mixer0, feed0, biases, mixer_piece(1)))
    own, first = mixer0
    mixer0 = [own, first, second_axis(own), second_axis(first)]
    feed0, biases = gather_direct(feed0), gather_direct(biases)
    mixer0, rows, biases = gate((mixer0, rows, biases))
    mixer0 = gather_last(mixer0)
    x0 = jnp.concatenate(rows).astype(F32)
    h1_0, q_0, kv = run_project(0, x0, mixer0)
    own_0 = gate(kv)
    near_0, far = within_chip(own_0, 1), between_chips(own_0)
    near_0, q_0, feed0, mixer1 = gate((near_0, q_0, feed0, mixer1))
    own, first = gather_first(whole(feed0))
    state = attend_near(idx, q_0, own_0, near_0)
    state, far_0, own, first, mixer1, feed1 = gate((state, far, own, first, mixer1, feed1))
    far_near_0 = within_chip(far_0, 1)
    second = second_axis(own)
    mixer1 = gather_direct(mixer1)
    o_0, lse_0 = attend_far(idx, q_0, far_0, far_near_0, state)
    o_0, own, first, second, mixer1, feed1 = gate((o_0, own, first, second, mixer1, feed1))
    third = second_axis(first)
    others = [flip_wide(own, 1), flip_wide(first, 1), flip_wide(second, 1)]
    mixer1, feed1 = gather_first(whole(mixer1)), gather_far(feed1)
    third, others, o_0, mixer1, feed1 = gate((third, others, o_0, mixer1, feed1))
    feed0 = [own, first, second, third] + others + [flip_wide(third, 1)]
    mixer1, feed1 = gather_second(mixer1), gather_near(feed1)
    x1, x1_0, h2_0, g_0, gp_0 = run_feed(0, x0, o_0, feed0)
    x1, mixer1, feed1 = gate((x1, mixer1, feed1))
    mixer1 = gather_last(mixer1)
    own, first = gather_first(whole(feed1))
    h1_1, q_1, kv = run_project(1, x1, mixer1)
    own_1 = gate(kv)
    near_1, far = within_chip(own_1, 1), between_chips(own_1)
    near_1, q_1, own, first = gate((near_1, q_1, own, first))
    second = second_axis(own)
    state = attend_near(idx, q_1, own_1, near_1)
    state, far_1, own, first, second, cotangent = gate((state, far, own, first, second, cotangent))
    far_near_1 = within_chip(far_1, 1)
    third = second_axis(first)
    others = [flip_wide(own, 1), flip_wide(first, 1), flip_wide(second, 1)]
    e = relocate(cotangent)
    o_1, lse_1 = attend_far(idx, q_1, far_1, far_near_1, state)
    o_1, third, others, e = gate((o_1, third, others, e))
    feed1 = [own, first, second, third] + others + [flip_wide(third, 1)]
    x2, x1_1, h2_1, g_1, gp_1 = run_feed(1, x1, o_1, feed1)
    x_out = relocate(x2.astype(BF))

    e = jnp.concatenate(e).astype(F32)
    dm, dz, e1, da, do, small_feed1 = feed_back(idx, e, x1_1, gp_1, norm_gain[1, 1:2], feed1)
    g_feed1 = feed_grads(idx, g_1, dm, h2_1, dz, o_1, da)
    do, x_out, g_feed1 = gate((do, x_out, g_feed1))
    g_feed1 = reduce_core(g_feed1)
    dq, dr, drow = attend_back_far(idx, q_1, do, o_1, lse_1, far_1, far_near_1)
    dr, dq, g_feed1 = gate((dr, dq, g_feed1))
    far = between_chips(added(dr, within_chip(dr, 0)))
    g_feed1 = reduce_first(g_feed1)
    dq, dn, dc = attend_back_near(idx, q_1, do, lse_1, drow, dq, own_1, near_1)
    dc, far, g_feed1 = gate((dc, far, g_feed1))
    got = within_chip(dc, 0)
    g_feed1 = reduce_second(g_feed1)
    dpz, e, small_mixer1 = project_back(
        idx, dq, dn, dc, got, far, cosine, sine, x1, e1, norm_gain[1, 0:1], mixer1
    )
    dpz, e, g_feed1 = gate((dpz, e, g_feed1))
    g_feed1 = reduce_near(g_feed1)
    g_mixer1 = project_grads(idx, h1_1, dpz)
    e, g_mixer1 = gate((e, g_mixer1))
    g_mixer1 = reduce_core(g_mixer1)
    dm, dz, e1, da, do, small_feed0 = feed_back(idx, e, x1_0, gp_0, norm_gain[0, 1:2], feed0)
    dm, do, g_feed1, g_mixer1 = gate((dm, do, g_feed1, g_mixer1))
    g_feed1, g_mixer1 = reduce_far(g_feed1), reduce_first(g_mixer1)
    g_feed0 = feed_grads(idx, g_0, dm, h2_0, dz, o_0, da)
    do, g_feed1, g_mixer1, g_feed0 = gate((do, g_feed1, g_mixer1, g_feed0))
    g_feed1, g_mixer1, g_feed0 = spread_first(g_feed1), reduce_second(g_mixer1), reduce_core(g_feed0)
    dq, dr, drow = attend_back_far(idx, q_0, do, o_0, lse_0, far_0, far_near_0)
    dr, dq, g_feed1, g_mixer1, g_feed0 = gate((dr, dq, g_feed1, g_mixer1, g_feed0))
    far = between_chips(added(dr, within_chip(dr, 0)))
    g_feed0, g_mixer1 = reduce_first(g_feed0), reduce_near(g_mixer1)
    dq, dn, dc = attend_back_near(idx, q_0, do, lse_0, drow, dq, own_0, near_0)
    dc, far, g_feed0, g_mixer1 = gate((dc, far, g_feed0, g_mixer1))
    got = within_chip(dc, 0)
    g_feed0, g_mixer1 = reduce_second(g_feed0), reduce_far(g_mixer1)
    dpz, e, small_mixer0 = project_back(
        idx, dq, dn, dc, got, far, cosine, sine, x0, e1, norm_gain[0, 0:1], mixer0
    )
    dpz, g_feed0, g_feed1, g_mixer1 = gate((dpz, g_feed0, g_feed1, g_mixer1))
    g_feed0, g_feed1, g_mixer1 = reduce_near(g_feed0), gather_second(g_feed1), spread_first(g_mixer1)
    g_mixer0 = project_grads(idx, h1_0, dpz)
    smalls = jnp.concatenate([small_feed0, small_mixer0, small_feed1, small_mixer1])
    e, g_mixer0, g_feed1, g_mixer1, smalls = gate((e, g_mixer0, g_feed1, g_mixer1, smalls))
    g_mixer0 = reduce_core(g_mixer0)
    g_feed1, g_mixer1 = gather_last(g_feed1), gather_second(g_mixer1)
    smalls = smalls, flip_wide(smalls, 1)
    g_mixer0, g_feed1, g_mixer1, smalls, e = gate((g_mixer0, g_feed1, g_mixer1, smalls, e))
    g_mixer0, g_mixer1 = reduce_first(g_mixer0), gather_last(g_mixer1)
    rows = relocate(e.astype(BF))
    smalls = smalls[0] + smalls[1]
    smalls = smalls, first_axis(smalls)
    feed_out = finish_feed(idx, 1, layers, g_feed1, None)
    g_mixer0, g_feed0, g_mixer1, smalls = gate((g_mixer0, g_feed0, g_mixer1, smalls))
    g_mixer0, g_feed0 = reduce_second(g_mixer0), reduce_far(g_feed0)
    smalls = smalls[0] + smalls[1]
    smalls = smalls, second_axis(smalls)
    mixer_out = finish_mixer(idx, 1, layers, g_mixer1, None)
    g_mixer0, smalls, rows = gate((g_mixer0, smalls, rows))
    g_mixer0 = reduce_near(g_mixer0)
    smalls = smalls[0] + smalls[1]
    bit = 8
    while bit < lax.axis_size("wide"):
        smalls = smalls + flip_wide(smalls, bit)
        bit *= 2
    smalls = smalls, flip_narrow(smalls, 1)
    g_mixer0, g_feed0, smalls = gate((g_mixer0, g_feed0, smalls))
    g_mixer0, g_feed0 = reduce_far(g_mixer0), spread_first(g_feed0)
    smalls = smalls[0] + smalls[1]
    smalls = smalls, flip_narrow(smalls, 2)
    g_mixer0, g_feed0, smalls = gate((g_mixer0, g_feed0, smalls))
    g_mixer0, g_feed0 = spread_first(g_mixer0), gather_second(g_feed0)
    smalls = smalls[0] + smalls[1]
    g_mixer0, g_feed0 = gate((g_mixer0, g_feed0))
    g_mixer0, g_feed0 = gather_second(g_mixer0), gather_last(g_feed0)
    g_mixer0, feed_out, g_feed0 = gate((g_mixer0, feed_out, g_feed0))
    g_mixer0 = gather_last(g_mixer0)
    feed_out = finish_feed(idx, 0, layers, g_feed0, feed_out)
    mixer_out = finish_mixer(idx, 0, layers, g_mixer0, mixer_out)
    tokens_grad = jnp.concatenate(rows)
    x_out = jnp.concatenate(x_out)

    small = smalls.reshape(layers, 16, D)
    up_bias_grad = lax.dynamic_index_in_dim(small[:, 0:4], z, 1, keepdims=False)
    mixer_bias_grad = lax.dynamic_index_in_dim(small[:, 8:12, :PARTS], z, 1, keepdims=False)
    return (
        x_out,
        tokens_grad,
        jnp.stack([small[:, 12], small[:, 6]], axis=1),
        jnp.stack([small[:, 13], small[:, 7]], axis=1),
        mixer_out.reshape(layers, D, 3, HEADS_COLS),
        mixer_bias_grad.reshape(layers, 3, HEADS_COLS),
        feed_out[2],
        jnp.stack([small[:, 5], small[:, 4]], axis=1),
        feed_out[0],
        up_bias_grad,
        feed_out[1],
    )


def solution(mesh):
    rows = P(("wide", "narrow"), None)
    quarters = (
        P(None, None, None, "narrow"),
        P(None, None, "narrow"),
        P(None, "narrow", None),
        P(),
        P(None, None, "narrow"),
        P(None, "narrow"),
        P(None, "narrow", None),
    )
    return jax.shard_map(
        per_device,
        mesh=mesh,
        in_specs=(rows, P("wide"), P(), P()) + quarters + (rows,),
        out_specs=(rows, rows, P(), P()) + quarters,
        check_vma=False,
    )
```

```python
import functools
import math

import jax
import jax.numpy as jnp
from jax import lax
from jax.experimental import pallas as pl
from jax.experimental.pallas import tpu as pltpu
from jax.sharding import PartitionSpec as P

HEAD_DIM = 64
LEN = 1024
EPSILON = 1e-05
D = 768
QUARTERS = 4
HALF = 256
ROWS = 512
PIECE = 96
HEADS_COLS = 192
PARTS = 576
PACK = 224
MASKED = -1e30
BF = jnp.bfloat16
F32 = jnp.float32
NT = (((1,), (1,)), ((), ()))
TN = (((0,), (0,)), ((), ()))
VMEM_LIMIT = 56 * 1024 * 1024


def dot(a, b):
    return jnp.dot(a, b, preferred_element_type=F32)


def dot_nt(a, b):
    return lax.dot_general(a, b, NT, preferred_element_type=F32)


def dot_tn(a, b):
    return lax.dot_general(a, b, TN, preferred_element_type=F32)


def norm_parts(values):
    center = values - jnp.mean(values, axis=-1, keepdims=True)
    inverse = lax.rsqrt(jnp.mean(center * center, axis=-1, keepdims=True) + EPSILON)
    return center * inverse, inverse


def norm_backward(grad_in, unit_rows, inverse, gain):
    scaled = grad_in * gain
    return inverse * (
        scaled
        - jnp.mean(scaled, axis=-1, keepdims=True)
        - unit_rows * jnp.mean(scaled * unit_rows, axis=-1, keepdims=True)
    )


def swap_halves(u):
    lane = lax.broadcasted_iota(jnp.int32, u.shape, 1)
    return jnp.where((lane & 63) < 32, pltpu.roll(u, 96, axis=1), pltpu.roll(u, 32, axis=1))


def rot(u, cosine, sine):
    return u * cosine + swap_halves(u) * sine


def unrot(u, cosine, sine):
    return u * cosine - swap_halves(u) * sine


ORDER = (0, 2, 1, 3)


def flips(idx):
    first, second = 2 + 2 * idx[2], 4 - 2 * idx[2]
    return [0, first, second, 6, 1, 1 ^ second, 1 ^ first, 7]


def piece_copies(refs, idx, sems, place):
    copies = []
    for flip, ref in zip(flips(idx), refs):
        for at, k in enumerate(ORDER):
            for source, target in place(ref.at[at], k, idx[1] ^ k, idx[0] ^ flip):
                copies.append(pltpu.make_async_copy(source, target, sems.at[len(copies)]))
    return copies


def rows_at(start, size, unit):
    return pl.ds(pl.multiple_of(start, unit), size)


def mixer_copies(refs, idx, sems, weights):
    def place(src, k, zq, wq):
        return [(src, weights.at[zq, rows_at(wq * PIECE, PIECE, 32)])]

    return piece_copies(refs, idx, sems, place)


def up_down_copies(refs, idx, sems, ups, downs):
    def place(src, k, zq, wq):
        rows = rows_at(wq * PIECE, PIECE, 32)
        return [
            (src.at[pl.ds(0, PIECE)], ups.at[k, rows]),
            (src.at[pl.ds(PIECE, PIECE)], downs.at[k, rows]),
        ]

    return piece_copies(refs, idx, sems, place)


def packed_copies(refs, idx, sems, packed):
    def place(src, k, zq, wq):
        return [(src.at[pl.ds(2 * PIECE, 32)], packed.at[zq, wq])]

    return piece_copies(refs, idx, sems, place)


def unpack_output(packed, weights):
    for zq in range(QUARTERS):
        for chip in range(4):
            for part in range(2):
                for s in range(3):
                    row = HEADS_COLS * zq + 48 * chip + 16 * s
                    weights[row : row + 16, 384 * part : 384 * part + 384] = packed[
                        zq, 2 * chip + part, 16 * (s // 2) : 16 * (s // 2) + 16, 384 * (s % 2) : 384 * (s % 2) + 384
                    ]


def any_spec():
    return pl.BlockSpec(memory_space=pl.ANY)


def vmem_spec():
    return pl.BlockSpec(memory_space=pltpu.VMEM)


def smem_spec():
    return pl.BlockSpec(memory_space=pltpu.SMEM)


def kernel_call(body, in_specs, out_shape, out_specs, scratch, args, flops, moved, aliases=None, name=None):
    return pl.pallas_call(
        body,
        in_specs=in_specs,
        out_specs=out_specs,
        out_shape=out_shape,
        scratch_shapes=scratch,
        input_output_aliases=aliases or {},
        compiler_params=pltpu.CompilerParams(vmem_limit_bytes=VMEM_LIMIT),
        cost_estimate=pl.CostEstimate(flops=1000, bytes_accessed=1000, transcendentals=0),
        name=name,
    )(*args)


def sds(shape, dtype):
    return jax.ShapeDtypeStruct(shape, dtype)


def project_body(idx, x, gain, shift, bias, cosine, sine, *rest):
    pieces, (h1, q, kv, weights, wide, sems) = rest[:8], rest[8:]
    copies = mixer_copies(pieces, idx, sems, weights)
    for copy in copies:
        copy.start()

    def norm_rows(i, carry):
        rows = rows_at(i * 128, 128, 128)
        unit, _ = norm_parts(x[rows])
        h1[rows] = (unit * gain[...] + shift[...]).astype(BF)
        return carry

    lax.fori_loop(0, 4, norm_rows, 0)
    for copy in copies:
        copy.wait()
    for zq in range(QUARTERS):
        p = dot(h1[...], weights[zq]) + bias[idx[1] ^ zq]
        for part in range(3):
            col = D * part + HEADS_COLS * zq
            wide[:, col : col + HEADS_COLS] = p[:, HEADS_COLS * part : HEADS_COLS * (part + 1)]
    for half in range(2):
        rows = slice(HALF * half, HALF * (half + 1))
        for j in range(6):
            cols = slice(128 * j, 128 * (j + 1))
            q[rows, cols] = (rot(wide[rows, cols], cosine[rows], sine[rows]) * 0.125).astype(BF)
            kcols = slice(D + 128 * j, D + 128 * (j + 1))
            kv[rows, cols] = rot(wide[rows, kcols], cosine[rows], sine[rows]).astype(BF)
        kv[rows, D:] = wide[rows, 2 * D :].astype(BF)


def project(idx, x, gain, shift, bias, cosine, sine, pieces):
    return kernel_call(
        project_body,
        [smem_spec()] + [vmem_spec()] * 6 + [any_spec()] * 8,
        [sds((ROWS, D), BF), sds((ROWS, D), BF), sds((ROWS, 2 * D), BF)],
        [vmem_spec()] * 3,
        [
            pltpu.VMEM((QUARTERS, D, PARTS), BF),
            pltpu.VMEM((ROWS, 3 * D), F32),
            pltpu.SemaphoreType.DMA((32,)),
        ],
        (idx, x, gain, shift, bias, cosine, sine, *pieces),
        2 * ROWS * D * 3 * D,
        8e6,
        name="project",
    )


def load_near(idx, own, near, kvn, kvc, sems):
    clean = idx[2] == 1
    copy = pltpu.make_async_copy(own, kvn, sems.at[0])
    copy.start()
    a = pltpu.make_async_copy(own, kvc, sems.at[1])
    b = pltpu.make_async_copy(near, kvc, sems.at[1])
    pl.when(clean)(a.start)
    pl.when(jnp.logical_not(clean))(b.start)
    return [copy, a]


def load_far(idx, far, far_near, kvr, sem):
    clean = idx[2] == 1
    a = pltpu.make_async_copy(far, kvr, sem)
    b = pltpu.make_async_copy(far_near, kvr, sem)
    pl.when(clean)(a.start)
    pl.when(jnp.logical_not(clean))(b.start)
    return a


NEAR_TILES = {0: [(0, [(0, True)]), (1, [(1, True), (0, False)])], 1: [(1, [(1, True)]), (0, [(0, True), (1, False)])]}
FAR_TILES = {0: [(1, [0, 1])], 1: [(1, [0]), (0, [0])]}


def set_masks(idx, bias, bias_n, query_dim):
    clean, level = idx[2], idx[4]
    qi = lax.shift_right_logical(lax.broadcasted_iota(jnp.int32, (HALF, HALF), query_dim), level)
    ki = lax.shift_right_logical(lax.broadcasted_iota(jnp.int32, (HALF, HALF), 1 - query_dim), level)
    bias[...] = jnp.where(ki < qi + clean, 0.0, MASKED)
    same = jnp.where(ki == qi, 0, 1) + clean
    bias_n[...] = jnp.where(same[:128, :128] == 0, 0.0, MASKED)


def lanes(rows):
    return lax.broadcasted_iota(jnp.int32, (rows, 128), 1)


def one_head(v, side):
    low_lane = lanes(v.shape[0]) < 64
    return jnp.where(low_lane if side == 0 else jnp.logical_not(low_lane), v, jnp.zeros_like(v))


def pair_cols(hp):
    off = pl.multiple_of(hp * 128, 128)
    return pl.ds(off, 128), pl.ds(pl.multiple_of(D + off, 128), 128)


def row_max(s):
    return jnp.max(s, axis=-1, keepdims=True)


def with_ones(v):
    return jnp.concatenate([v, jnp.ones_like(v)], axis=1)


def half_rows(half):
    return slice(HALF * half, HALF * (half + 1))


def attend_near_body(idx, q, own, near, acc, tops, counts, kvn, kvc, bias, bias_n, sems):
    waits = load_near(idx, own, near, kvn, kvc, sems)
    set_masks(idx, bias, bias_n, 0)
    tops[...] = jnp.zeros_like(tops)
    counts[...] = jnp.ones_like(counts)
    for copy in waits:
        copy.wait()

    def run(tiles):
        def pair(hp, carry):
            cols, vcols = pair_cols(hp)
            lane = lanes(HALF)
            for half, sources in tiles:
                rows = half_rows(half)
                q2 = q[rows, cols]
                sides = []
                for side in range(2):
                    qm = one_head(q2, side)
                    scores = []
                    for kh, diagonal in sources:
                        s = dot_nt(qm, kvc[half_rows(kh), cols])
                        scores.append(s + bias[...] if diagonal else s)
                    blocks = [slice(HALF * half + 128 * t, HALF * half + 128 * (t + 1)) for t in range(2)]
                    parts = [slice(128 * t, 128 * (t + 1)) for t in range(2)]
                    mine = [dot_nt(qm[part], kvn[block, cols]) + bias_n[...] for part, block in zip(parts, blocks)]
                    top = jnp.concatenate([row_max(s) for s in mine], axis=0)
                    for s in scores:
                        top = jnp.maximum(top, row_max(s))
                    total = jnp.concatenate(
                        [
                            dot(jnp.exp(s - top[part]).astype(BF), with_ones(kvn[block, vcols]))
                            for s, part, block in zip(mine, parts, blocks)
                        ],
                        axis=0,
                    )
                    for s, (kh, diagonal) in zip(scores, sources):
                        total = total + dot(jnp.exp(s - top).astype(BF), with_ones(kvc[half_rows(kh), vcols]))
                    sides.append((total[:, :128], top, total[:, 128:]))
                acc[rows, cols] = jnp.where(lane < 64, sides[0][0], sides[1][0])
                for target, at in ((tops, 1), (counts, 2)):
                    target[rows] = jnp.where(
                        lane == 2 * hp, sides[0][at], jnp.where(lane == 2 * hp + 1, sides[1][at], target[rows])
                    )
            return carry

        lax.fori_loop(0, 6, pair, 0)

    for zl in range(2):
        pl.when(idx[3] == zl)(functools.partial(run, NEAR_TILES[zl]))


def attend_near(idx, q, own, near):
    return kernel_call(
        attend_near_body,
        [smem_spec(), vmem_spec()] + [any_spec()] * 2,
        [sds((ROWS, D), F32), sds((ROWS, 128), F32), sds((ROWS, 128), F32)],
        [vmem_spec()] * 3,
        [
            pltpu.VMEM((ROWS, 2 * D), BF),
            pltpu.VMEM((ROWS, 2 * D), BF),
            pltpu.VMEM((HALF, HALF), F32),
            pltpu.VMEM((128, 128), F32),
            pltpu.SemaphoreType.DMA((2,)),
        ],
        (idx, q, own, near),
        8e9,
        6e6,
        name="attend_near",
    )


def attend_far_body(idx, q, far, far_near, acc, tops, counts, o, lse, kvr, last, sem):
    copy = load_far(idx, far, far_near, kvr, sem)
    last[...] = tops[...] + jnp.log(counts[...])
    copy.wait()

    def column(values, head):
        return jnp.sum(jnp.where(lanes(HALF) == head, values, 0.0), axis=-1, keepdims=True)

    def run(tiles):
        covered = [half for half, _ in tiles]

        def pair(hp, carry):
            cols, vcols = pair_cols(hp)
            lane = lanes(HALF)
            for half in range(2):
                rows = half_rows(half)
                if half in covered:
                    sources = dict(tiles)[half]
                    q2 = q[rows, cols]
                    sides = []
                    for side in range(2):
                        qm = one_head(q2, side)
                        scores = [dot_nt(qm, kvr[half_rows(kh), cols]) for kh in sources]
                        before = column(tops[rows], 2 * hp + side)
                        top = before
                        for s in scores:
                            top = jnp.maximum(top, row_max(s))
                        shrink = jnp.exp(before - top)
                        total = None
                        for s, kh in zip(scores, sources):
                            part = dot(jnp.exp(s - top).astype(BF), with_ones(kvr[half_rows(kh), vcols]))
                            total = part if total is None else total + part
                        count = column(counts[rows], 2 * hp + side) * shrink + total[:, 128:]
                        value = (acc[rows, cols] * shrink + total[:, :128]) / count
                        sides.append((value, top + jnp.log(count)))
                    last[rows] = jnp.where(
                        lane == 2 * hp, sides[0][1], jnp.where(lane == 2 * hp + 1, sides[1][1], last[rows])
                    )
                else:
                    sides = [(acc[rows, cols] / column(counts[rows], 2 * hp + side),) for side in range(2)]
                o[rows, cols] = jnp.where(lane < 64, sides[0][0], sides[1][0]).astype(BF)
            return carry

        lax.fori_loop(0, 6, pair, 0)

    for zl in range(2):
        pl.when(idx[3] == zl)(functools.partial(run, FAR_TILES[zl]))
    across = jnp.transpose(last[...])
    for head in range(12):
        lse[head] = across[head : head + 1]


def attend_far(idx, q, far, far_near, state):
    return kernel_call(
        attend_far_body,
        [smem_spec(), vmem_spec()] + [any_spec()] * 2 + [vmem_spec()] * 3,
        [sds((ROWS, D), BF), sds((12, 1, ROWS), F32)],
        [vmem_spec()] * 2,
        [
            pltpu.VMEM((ROWS, 2 * D), BF),
            pltpu.VMEM((ROWS, 128), F32),
            pltpu.SemaphoreType.DMA,
        ],
        (idx, q, far, far_near, *state),
        5e9,
        6e6,
        name="attend_far",
    )


def feed_body(idx, x, o, gain, shift, out_bias, down_bias, up_bias, *rest):
    pieces, (x2, x1, h2, g, gp, ups, downs, packed, outw, sems, sems_o) = rest[:8], rest[8:]
    first = packed_copies(pieces, idx, sems_o, packed)
    later = up_down_copies(pieces, idx, sems, ups, downs)
    for copy in first + later:
        copy.start()
    for copy in first:
        copy.wait()
    unpack_output(packed, outw)
    x1[...] = x[...] + (dot(o[...], outw[...]) + out_bias[...])

    def norm_rows(i, carry):
        rows = rows_at(i * 128, 128, 128)
        unit, _ = norm_parts(x1[rows])
        h2[rows] = (unit * gain[...] + shift[...]).astype(BF)
        x2[rows] = x1[rows] + down_bias[...]
        return carry

    lax.fori_loop(0, 4, norm_rows, 0)
    for copy in later:
        copy.wait()

    def hidden(k, carry):
        for n in range(3):
            cols = slice(256 * n, 256 * (n + 1))
            u = dot(h2[...], ups[k, :, cols]) + up_bias[k, :, cols]
            uu = u * u
            t = jnp.tanh(0.7978845608028654 * u * (1.0 + 0.044715 * uu))
            half_t = 0.5 + 0.5 * t
            g[k, :, cols] = (u * half_t).astype(BF)
            slope = half_t + (0.5 * 0.7978845608028654) * u * (1.0 - t * t) * (1.0 + 0.134145 * uu)
            gp[k, :, cols] = slope.astype(BF)
        x2[...] += dot(g[k], downs[k])
        return carry

    lax.fori_loop(0, QUARTERS, hidden, 0)


WEIGHT_SCRATCH = [
    ((QUARTERS, D, D), BF),
    ((QUARTERS, D, D), BF),
    ((QUARTERS, 8, 32, D), BF),
    ((D, D), BF),
]


def feed(idx, x, o, gain, shift, out_bias, down_bias, up_bias, pieces):
    return kernel_call(
        feed_body,
        [smem_spec()] + [vmem_spec()] * 7 + [any_spec()] * 8,
        [
            sds((ROWS, D), F32),
            sds((ROWS, D), F32),
            sds((ROWS, D), BF),
            sds((QUARTERS, ROWS, D), BF),
            sds((QUARTERS, ROWS, D), BF),
        ],
        [vmem_spec()] * 5,
        [pltpu.VMEM(s, t) for s, t in WEIGHT_SCRATCH]
        + [pltpu.SemaphoreType.DMA((64,)), pltpu.SemaphoreType.DMA((32,))],
        (idx, x, o, gain, shift, out_bias, down_bias, up_bias, *pieces),
        2 * ROWS * D * D * 9,
        25e6,
        name="feed",
    )


def feed_back_body(idx, e, x1, gp, gain, *rest):
    pieces, (dm, dz, e1, da, do, small, ups, downs, packed, outw, dh2, hidden_sums, sems, sems_o) = rest[:8], rest[8:]
    first = packed_copies(pieces, idx, sems_o, packed)
    later = up_down_copies(pieces, idx, sems, ups, downs)
    for copy in later + first:
        copy.start()
    dm[...] = e[...].astype(BF)
    small[4:5] = jnp.sum(dm[...].astype(F32), axis=0, keepdims=True)
    dh2[...] = jnp.zeros_like(dh2)
    for copy in later:
        copy.wait()

    def hidden(k, carry):
        zq = idx[1] ^ k
        for n in range(3):
            cols = slice(256 * n, 256 * (n + 1))
            part = (dot_nt(dm[...], downs[k, cols]) * gp[k, :, cols].astype(F32)).astype(BF)
            dz[k, :, cols] = part
            hidden_sums[zq, :, cols] = jnp.sum(part.astype(F32), axis=0, keepdims=True)
        dh2[...] += dot_nt(dz[k], ups[k])
        return carry

    lax.fori_loop(0, QUARTERS, hidden, 0)
    for copy in first:
        copy.wait()
    unpack_output(packed, outw)
    for zq in range(QUARTERS):
        small[zq : zq + 1] = hidden_sums[zq]
    small[5:8] = jnp.zeros((3, D), F32)

    def norm_rows(i, carry):
        rows = rows_at(i * 128, 128, 128)
        unit, inverse = norm_parts(x1[rows])
        grad = dh2[rows]
        up = e[rows] + norm_backward(grad, unit, inverse, gain[...])
        e1[rows] = up
        low = up.astype(BF)
        da[rows] = low
        small[5:6] += jnp.sum(low.astype(F32), axis=0, keepdims=True)
        small[6:7] += jnp.sum(grad * unit, axis=0, keepdims=True)
        small[7:8] += jnp.sum(grad, axis=0, keepdims=True)
        return carry

    lax.fori_loop(0, 4, norm_rows, 0)
    do[...] = dot_nt(da[...], outw[...]).astype(BF)


def feed_back(idx, e, x1, gp, gain, pieces):
    return kernel_call(
        feed_back_body,
        [smem_spec()] + [vmem_spec()] * 4 + [any_spec()] * 8,
        [
            sds((ROWS, D), BF),
            sds((QUARTERS, ROWS, D), BF),
            sds((ROWS, D), F32),
            sds((ROWS, D), BF),
            sds((ROWS, D), BF),
            sds((8, D), F32),
        ],
        [vmem_spec()] * 6,
        [pltpu.VMEM(s, t) for s, t in WEIGHT_SCRATCH]
        + [pltpu.VMEM((ROWS, D), F32), pltpu.VMEM((QUARTERS, 1, D), F32), pltpu.SemaphoreType.DMA((64,)), pltpu.SemaphoreType.DMA((32,))],
        (idx, e, x1, gp, gain, *pieces),
        2 * ROWS * D * D * 9,
        25e6,
        name="feed_back",
    )


def spread(idx, keep, send, source, k, wq, rows, sem):
    w8, mine = idx[0], idx[2]
    j = (wq >> 1) ^ (w8 >> 1)
    turned = ((j & 1) << 1) | (j >> 1)
    at = ((k & 1) << 1) | (k >> 1)
    here, there = jnp.where(mine == 1, j, turned), jnp.where(mine == 1, turned, j)
    a = pltpu.make_async_copy(source, keep.at[here, at, rows], sem)
    b = pltpu.make_async_copy(source, send.at[there, at, rows], sem)
    pl.when((wq & 1) == mine)(a.start)
    pl.when((wq & 1) != mine)(b.start)
    return a


def feed_grads_body(idx, g, dm, h2, dz, o, da, keep, send, flipped, turned, d_up, d_down, d_out, sems):
    waits = []
    flipped[...] = jnp.transpose(o[...])
    turned[...] = dot(flipped[...], da[...]).astype(BF)
    for zq in range(QUARTERS):
        for chip in range(4):
            for part in range(2):
                for s in range(4):
                    rows, cols = slice(16 * (s // 2), 16 * (s // 2) + 16), slice(384 * (s % 2), 384 * (s % 2) + 384)
                    if s == 3:
                        block = jnp.zeros((16, 384), BF)
                    else:
                        row = HEADS_COLS * zq + 48 * chip + 16 * s
                        block = turned[row : row + 16, 384 * part : 384 * part + 384]
                    d_out[zq, 2 * chip + part, rows, cols] = block
    for zq in range(QUARTERS):
        k = idx[1] ^ zq
        for wq in range(8):
            sem = sems.at[len(waits)]
            waits.append(spread(idx, keep, send, d_out.at[zq, wq], k, wq, pl.ds(2 * PIECE, 32), sem))
    for k in range(QUARTERS):
        flipped[...] = jnp.transpose(g[k])
        d_down[k] = dot(flipped[...], dm[...]).astype(BF)
        for wq in range(8):
            sem = sems.at[len(waits)]
            source = d_down.at[k, pl.ds(PIECE * wq, PIECE)]
            waits.append(spread(idx, keep, send, source, k, wq, pl.ds(PIECE, PIECE), sem))
    flipped[...] = jnp.transpose(h2[...])
    for k in range(QUARTERS):
        d_up[k] = dot(flipped[...], dz[k]).astype(BF)
        for wq in range(8):
            sem = sems.at[len(waits)]
            source = d_up.at[k, pl.ds(PIECE * wq, PIECE)]
            waits.append(spread(idx, keep, send, source, k, wq, pl.ds(0, PIECE), sem))
    for copy in waits:
        copy.wait()


def feed_grads(idx, g, dm, h2, dz, o, da):
    return kernel_call(
        feed_grads_body,
        [smem_spec()] + [vmem_spec()] * 6,
        [sds((4, QUARTERS, PACK, D), BF)] * 2,
        [any_spec()] * 2,
        [
            pltpu.VMEM((D, ROWS), BF),
            pltpu.VMEM((D, D), BF),
            pltpu.VMEM((QUARTERS, D, D), BF),
            pltpu.VMEM((QUARTERS, D, D), BF),
            pltpu.VMEM((QUARTERS, 8, 32, D), BF),
            pltpu.SemaphoreType.DMA((96,)),
        ],
        (idx, g, dm, h2, dz, o, da),
        2 * ROWS * D * D * 9,
        25e6,
        name="feed_grads",
    )


def back_tile(q, do, lse, drow, cols, hp, k2, v2, qrow, n, bias_here):
    q2, g2 = q[qrow : qrow + n, cols], do[qrow : qrow + n, cols]
    sums = None
    for side in range(2):
        qm, gm, km = one_head(q2, side), one_head(g2, side), one_head(k2, side)
        head = 2 * hp + side
        s = dot_nt(k2, qm)
        if bias_here is not None:
            s = s + bias_here
        p = jnp.exp(s - lse[head, :, qrow : qrow + n])
        dp = dot_nt(v2, gm)
        ds = (p * (dp - drow[head, :, qrow : qrow + n])).astype(BF)
        parts = (dot(ds, qm), dot(p.astype(BF), gm), dot_tn(ds, km))
        sums = parts if sums is None else tuple(a + b for a, b in zip(sums, parts))
    return sums


def attend_back_far_body(idx, q, do, o, lse, far, far_near, dq, dr, drow, kvr, dcol, sem):
    copy = load_far(idx, far, far_near, kvr, sem)
    dcol[...] = jnp.zeros_like(dcol)

    def products(hp, carry):
        cols, _ = pair_cols(hp)
        lane = lanes(ROWS)
        both = do[:, cols].astype(F32) * o[:, cols].astype(F32)
        first = jnp.sum(jnp.where(lane < 64, both, 0.0), axis=-1, keepdims=True)
        second = jnp.sum(jnp.where(lane < 64, 0.0, both), axis=-1, keepdims=True)
        dcol[...] = jnp.where(lane == 2 * hp, first, jnp.where(lane == 2 * hp + 1, second, dcol[...]))
        return carry

    lax.fori_loop(0, 6, products, 0)
    across = jnp.transpose(dcol[...])
    for head in range(12):
        drow[head] = across[head : head + 1]
    copy.wait()

    def run(tiles):
        def pair(hp, carry):
            cols, vcols = pair_cols(hp)
            dq_half = [None, None]
            for kh in range(2):
                keys = half_rows(kh)
                total = None
                for half, sources in tiles:
                    if kh in sources:
                        parts = back_tile(
                            q, do, lse, drow, cols, hp, kvr[keys, cols], kvr[keys, vcols], HALF * half, HALF, None
                        )
                        total = parts[:2] if total is None else (total[0] + parts[0], total[1] + parts[1])
                        dq_half[half] = parts[2] if dq_half[half] is None else dq_half[half] + parts[2]
                if total is None:
                    total = (jnp.zeros((HALF, 128), F32),) * 2
                dr[keys, cols] = total[0].astype(BF)
                dr[keys, vcols] = total[1].astype(BF)
            for half in range(2):
                part = dq_half[half]
                dq[half_rows(half), cols] = jnp.zeros((HALF, 128), F32) if part is None else part
            return carry

        lax.fori_loop(0, 6, pair, 0)

    for zl in range(2):
        pl.when(idx[3] == zl)(functools.partial(run, FAR_TILES[zl]))


def attend_back_far(idx, q, do, o, lse, far, far_near):
    return kernel_call(
        attend_back_far_body,
        [smem_spec()] + [vmem_spec()] * 4 + [any_spec()] * 2,
        [sds((ROWS, D), F32), sds((ROWS, 2 * D), BF), sds((12, 1, ROWS), F32)],
        [vmem_spec()] * 3,
        [
            pltpu.VMEM((ROWS, 2 * D), BF),
            pltpu.VMEM((ROWS, 128), F32),
            pltpu.SemaphoreType.DMA,
        ],
        (idx, q, do, o, lse, far, far_near),
        12e9,
        8e6,
        name="attend_back_far",
    )


def attend_back_near_body(idx, q, do, lse, drow, dq_far, own, near, dq, dn, dc, kvn, kvc, bias, bias_n, sems):
    waits = load_near(idx, own, near, kvn, kvc, sems)
    set_masks(idx, bias, bias_n, 1)
    for copy in waits:
        copy.wait()

    def run(tiles):
        def pair(hp, carry):
            cols, vcols = pair_cols(hp)
            dq_half = [None, None]
            for half in range(2):
                pieces = []
                for t in range(2):
                    rows = slice(HALF * half + 128 * t, HALF * half + 128 * (t + 1))
                    dk, dv, dqs = back_tile(
                        q, do, lse, drow, cols, hp, kvn[rows, cols], kvn[rows, vcols], rows.start, 128, bias_n[...]
                    )
                    dn[rows, cols] = dk.astype(BF)
                    dn[rows, vcols] = dv.astype(BF)
                    pieces.append(dqs)
                dq_half[half] = dq_far[half_rows(half), cols] + jnp.concatenate(pieces, axis=0)
            for kh in range(2):
                keys = half_rows(kh)
                total = None
                for half, sources in tiles:
                    if kh in dict(sources):
                        parts = back_tile(
                            q,
                            do,
                            lse,
                            drow,
                            cols,
                            hp,
                            kvc[keys, cols],
                            kvc[keys, vcols],
                            HALF * half,
                            HALF,
                            bias[...] if dict(sources)[kh] else None,
                        )
                        total = parts[:2] if total is None else (total[0] + parts[0], total[1] + parts[1])
                        dq_half[half] = dq_half[half] + parts[2]
                dc[keys, cols] = total[0].astype(BF)
                dc[keys, vcols] = total[1].astype(BF)
            for half in range(2):
                dq[half_rows(half), cols] = dq_half[half] * 0.125
            return carry

        lax.fori_loop(0, 6, pair, 0)

    for zl in range(2):
        pl.when(idx[3] == zl)(functools.partial(run, NEAR_TILES[zl]))


def attend_back_near(idx, q, do, lse, drow, dq_far, own, near):
    return kernel_call(
        attend_back_near_body,
        [smem_spec()] + [vmem_spec()] * 5 + [any_spec()] * 2,
        [sds((ROWS, D), F32), sds((ROWS, 2 * D), BF), sds((ROWS, 2 * D), BF)],
        [vmem_spec()] * 3,
        [
            pltpu.VMEM((ROWS, 2 * D), BF),
            pltpu.VMEM((ROWS, 2 * D), BF),
            pltpu.VMEM((HALF, HALF), F32),
            pltpu.VMEM((128, 128), F32),
            pltpu.SemaphoreType.DMA((2,)),
        ],
        (idx, q, do, lse, drow, dq_far, own, near),
        18e9,
        12e6,
        name="attend_back_near",
    )


def project_back_body(idx, dq, dn, dcr, got, far, cosine, sine, x, e1, gain, *rest):
    pieces, (dpz, e, small, weights, wide, sems) = rest[:8], rest[8:]
    copies = mixer_copies(pieces, idx, sems, weights)
    for copy in copies:
        copy.start()
    noisy = idx[2] == 0
    for half in range(2):
        rows = slice(HALF * half, HALF * (half + 1))
        for j in range(6):
            cols = slice(128 * j, 128 * (j + 1))
            wide[rows, cols] = unrot(dq[rows, cols], cosine[rows], sine[rows])

        def total(cols, at=rows):
            summed = dcr[at, cols].astype(F32) + got[at, cols].astype(F32) + far[at, cols].astype(F32)
            return jnp.where(noisy, dn[at, cols].astype(F32), summed)

        for j in range(6):
            cols = slice(128 * j, 128 * (j + 1))
            wide[rows, D + 128 * j : D + 128 * (j + 1)] = unrot(total(cols), cosine[rows], sine[rows])
        wide[rows, 2 * D :] = total(slice(D, 2 * D))
    for copy in copies:
        copy.wait()
    small[...] = jnp.zeros_like(small)
    for zq in range(QUARTERS):
        for part in range(3):
            col = D * part + HEADS_COLS * zq
            dpz[zq, :, HEADS_COLS * part : HEADS_COLS * (part + 1)] = wide[:, col : col + HEADS_COLS].astype(BF)
        small[zq : zq + 1, :PARTS] = jnp.sum(dpz[zq].astype(F32), axis=0, keepdims=True)
        piece = dot_nt(dpz[zq], weights[zq])
        if zq == 0:
            e[...] = piece
        else:
            e[...] += piece

    def norm_rows(i, carry):
        rows = rows_at(i * 128, 128, 128)
        unit, inverse = norm_parts(x[rows])
        grad = e[rows]
        small[4:5] += jnp.sum(grad * unit, axis=0, keepdims=True)
        small[5:6] += jnp.sum(grad, axis=0, keepdims=True)
        e[rows] = e1[rows] + norm_backward(grad, unit, inverse, gain[...])
        return carry

    lax.fori_loop(0, 4, norm_rows, 0)


def project_back(idx, dq, dn, dcr, got, far, cosine, sine, x, e1, gain, pieces):
    return kernel_call(
        project_back_body,
        [smem_spec()] + [vmem_spec()] * 10 + [any_spec()] * 8,
        [sds((QUARTERS, ROWS, PARTS), BF), sds((ROWS, D), F32), sds((8, D), F32)],
        [vmem_spec()] * 3,
        [
            pltpu.VMEM((QUARTERS, D, PARTS), BF),
            pltpu.VMEM((ROWS, 3 * D), F32),
            pltpu.SemaphoreType.DMA((32,)),
        ],
        (idx, dq, dn, dcr, got, far, cosine, sine, x, e1, gain, *pieces),
        2 * ROWS * D * 3 * D,
        12e6,
        name="project_back",
    )


def project_grads_body(idx, h1, dpz, keep, send, flipped, stage, sems):
    waits = []
    flipped[...] = jnp.transpose(h1[...])
    for zq in range(QUARTERS):
        k = idx[1] ^ zq
        stage[zq] = dot(flipped[...], dpz[zq]).astype(BF)
        for wq in range(8):
            sem = sems.at[len(waits)]
            source = stage.at[zq, pl.ds(PIECE * wq, PIECE)]
            waits.append(spread(idx, keep, send, source, k, wq, pl.ds(0, PIECE), sem))
    for copy in waits:
        copy.wait()


def project_grads(idx, h1, dpz):
    return kernel_call(
        project_grads_body,
        [smem_spec()] + [vmem_spec()] * 2,
        [sds((4, QUARTERS, PIECE, PARTS), BF)] * 2,
        [any_spec()] * 2,
        [
            pltpu.VMEM((D, ROWS), BF),
            pltpu.VMEM((QUARTERS, D, PARTS), BF),
            pltpu.SemaphoreType.DMA((32,)),
        ],
        (idx, h1, dpz),
        2 * ROWS * D * 3 * D,
        9e6,
        name="project_grads",
    )


def finish_mixer_body(layer, filled, idx, *rest):
    pieces, rest = rest[:8], rest[8:]
    if filled:
        rest = rest[1:]
    out, stage, sem = rest
    for flip, piece in zip(flips(idx), pieces):
        stage[rows_at((idx[0] ^ flip) * PIECE, PIECE, 32)] = piece[...].astype(F32)
    copy = pltpu.make_async_copy(stage, out.at[layer], sem)
    copy.start()
    copy.wait()


def finish_mixer(idx, layer, layers, pieces, before):
    filled = before is not None
    return kernel_call(
        functools.partial(finish_mixer_body, layer, filled),
        [smem_spec()] + [vmem_spec()] * 8 + [any_spec()] * filled,
        sds((layers, D, PARTS), F32),
        any_spec(),
        [pltpu.VMEM((D, PARTS), F32), pltpu.SemaphoreType.DMA],
        (idx, *pieces) + ((before,) if filled else ()),
        1e6,
        4e6,
        aliases={9: 0} if filled else None,
        name="finish_mixer",
    )


def finish_feed_body(layer, filled, idx, *rest):
    pieces, rest = rest[:8], rest[8:]
    if filled:
        rest = rest[3:]
    up, down, out, up_s, down_s, out_s, sems = rest
    for flip, piece in zip(flips(idx), pieces):
        wq = idx[0] ^ flip
        rows = rows_at(wq * PIECE, PIECE, 32)
        up_s[rows] = piece[:PIECE].astype(F32)
        down_s[rows] = piece[PIECE : 2 * PIECE].astype(F32)
        cols = pl.ds(pl.multiple_of((wq & 1) * 384, 128), 384)
        for s in range(3):
            row = 2 * PIECE + 16 * (s // 2)
            block = piece[row : row + 16, 384 * (s % 2) : 384 * (s % 2) + 384]
            out_s[rows_at((wq >> 1) * 48 + 16 * s, 16, 16), cols] = block.astype(F32)
    copies = [
        pltpu.make_async_copy(stage, whole.at[layer], sems.at[i])
        for i, (stage, whole) in enumerate(((up_s, up), (down_s, down), (out_s, out)))
    ]
    for copy in copies:
        copy.start()
    for copy in copies:
        copy.wait()


def finish_feed(idx, layer, layers, pieces, before):
    filled = before is not None
    return kernel_call(
        functools.partial(finish_feed_body, layer, filled),
        [smem_spec()] + [vmem_spec()] * 8 + [any_spec()] * (3 * filled),
        [sds((layers, D, D), F32), sds((layers, D, D), F32), sds((layers, HEADS_COLS, D), F32)],
        [any_spec()] * 3,
        [
            pltpu.VMEM((D, D), F32),
            pltpu.VMEM((D, D), F32),
            pltpu.VMEM((HEADS_COLS, D), F32),
            pltpu.SemaphoreType.DMA((3,)),
        ],
        (idx, *pieces) + (tuple(before) if filled else ()),
        1e6,
        8e6,
        aliases={9: 0, 10: 1, 11: 2} if filled else None,
        name="finish_feed",
    )


def pack_body(idx, ups, downs, outs, *rest):
    targets, (zeros, sems) = rest[:-2], rest[-2:]
    zeros[...] = jnp.zeros_like(zeros)
    rows = rows_at(idx[0] * PIECE, PIECE, 32)
    cols = pl.ds(pl.multiple_of(idx[2] * 384, 128), 384)
    copies = []
    for layer, target in enumerate(targets):
        moves = [
            (ups.at[layer, rows], target.at[pl.ds(0, PIECE)]),
            (downs.at[layer, rows], target.at[pl.ds(PIECE, PIECE)]),
        ]
        for s in range(4):
            place = target.at[pl.ds(2 * PIECE + 16 * (s // 2), 16), pl.ds(384 * (s % 2), 384)]
            if s == 3:
                moves.append((zeros, place))
            else:
                moves.append((outs.at[layer, rows_at((idx[0] >> 1) * 48 + 16 * s, 16, 16), cols], place))
        for source, place in moves:
            copies.append(pltpu.make_async_copy(source, place, sems.at[len(copies)]))
    for copy in copies:
        copy.start()
    for copy in copies:
        copy.wait()


def pack(idx, ups, downs, outs):
    layers = ups.shape[0]
    return kernel_call(
        pack_body,
        [smem_spec()] + [any_spec()] * 3,
        [sds((PACK, D), BF)] * layers,
        [vmem_spec()] * layers,
        [pltpu.VMEM((16, 384), BF), pltpu.SemaphoreType.DMA((6 * layers,))],
        (idx, ups, downs, outs),
        1e6,
        1e6,
        name="pack",
    )


def flip_wide(x, bit):
    return lax.ppermute(x, "wide", [(i, i ^ bit) for i in range(lax.axis_size("wide"))])


def flip_narrow(x, bit):
    return lax.ppermute(x, "narrow", [(i, i ^ bit) for i in range(QUARTERS)])


def first_axis(x):
    return lax.ppermute(x, "wide", [(i, i ^ (4 if i & 1 else 2)) for i in range(lax.axis_size("wide"))])


def second_axis(x):
    return lax.ppermute(x, "wide", [(i, i ^ (2 if i & 1 else 4)) for i in range(lax.axis_size("wide"))])


def gate_body(*refs):
    return None


def gate(tree):
    leaves, shape = jax.tree.flatten(tree)
    out = pl.pallas_call(
        gate_body,
        in_specs=[any_spec() for _ in leaves],
        out_specs=[any_spec() for _ in leaves],
        out_shape=[sds(x.shape, x.dtype) for x in leaves],
        input_output_aliases={i: i for i in range(len(leaves))},
        name="gate",
    )(*leaves)
    return jax.tree.unflatten(shape, out)


def gather_direct(piece):
    return [piece] + [flip_narrow(piece, k) for k in ORDER[1:]]


def gather_far(piece):
    return piece, flip_narrow(piece, 2)


def gather_near(pair):
    pair = jnp.stack(pair)
    return pair, flip_narrow(pair, 1)


def whole(parts):
    return jnp.stack(parts) if parts[0].ndim == 2 else jnp.concatenate(parts)


def gather_first(own):
    return own, first_axis(own)


def gather_second(parts):
    own, first = parts
    return [own, first, second_axis(own), second_axis(first)]


def gather_last(here):
    return here + [flip_wide(x, 1) for x in here]


def added(*terms):
    return functools.reduce(jnp.add, [t.astype(F32) for t in terms]).astype(BF)


def reduce_core(pair):
    keep, send = pair
    return keep, flip_wide(send, 1)


def reduce_first(pair):
    keep, got = pair
    return keep, got, first_axis(added(keep[2:], got[2:]))


def reduce_second(parts):
    keep, got, first = parts
    return keep, got, first, second_axis(added(keep[1], got[1], first[1]))


def reduce_near(parts):
    keep, got, first, second = parts
    total = added(keep[0], got[0], first[0], second)
    bit = 8
    while bit < lax.axis_size("wide"):
        total = added(total, flip_wide(total, bit))
        bit *= 2
    return total, flip_narrow(total[2:], 1)


def reduce_far(parts):
    total, near = parts
    return total, near, flip_narrow(added(total[1], near[1]), 2)


def both_axes(x):
    return flip_wide(x, 6)


def gather_plane(own):
    return [own, first_axis(own), second_axis(own), both_axes(own)]


def spread_first(parts):
    total, near, far = parts
    return gather_first(added(total[0], near[0], far))


def reduce_plane(pair):
    keep, got = pair
    moves = (second_axis, first_axis, both_axes)
    return [keep, got] + [move(added(keep[i + 1], got[i + 1])) for i, move in enumerate(moves)]


def reduce_narrow(parts):
    keep, got, *others = parts
    total = added(keep[0], got[0], *others)
    bit = 8
    while bit < lax.axis_size("wide"):
        total = added(total, flip_wide(total, bit))
        bit *= 2
    return [total] + [flip_narrow(total[i], ORDER[i]) for i in range(1, QUARTERS)]


def device_pairs(move):
    pairs = []
    for w in range(lax.axis_size("wide")):
        for z in range(QUARTERS):
            target = move(w, z)
            if target is not None:
                pairs.append((w * QUARTERS + z, target[0] * QUARTERS + target[1]))
    return pairs


BOTH = ("wide", "narrow")


def relocate(rows):
    first = device_pairs(lambda w, z: ((w & ~1) | (z >> 1), ((w & 1) << 1) | (z & 1)))
    second = device_pairs(lambda w, z: ((w & ~1) | (z >> 1), ((w & 1) << 1) | (1 - (z & 1))))
    return lax.ppermute(rows[:HALF], BOTH, first), lax.ppermute(rows[HALF:], BOTH, second)


def between_chips(x):
    pairs = device_pairs(lambda w, z: (w, z ^ 1) if w & 1 else None)
    return lax.ppermute(x, BOTH, pairs)


def within_chip(x, source):
    pairs = [(i, i ^ 1) for i in range(lax.axis_size("wide")) if (i & 1) == source]
    return lax.ppermute(x, "wide", pairs)


def per_device(
    tokens,
    block_size,
    norm_gain,
    norm_shift,
    mixer_weight,
    mixer_bias,
    output_weight,
    output_bias,
    up_weight,
    up_bias,
    down_weight,
    cotangent,
):
    layers = norm_gain.shape[0]
    w, z = lax.axis_index("wide"), lax.axis_index("narrow")
    w8, core, low = w & 7, w & 1, z & 1
    sizes = jnp.where((z >> 1) == core, block_size, flip_wide(block_size, 1))[0]
    level = 2 + (sizes >= 8).astype(jnp.int32) + (sizes >= 16).astype(jnp.int32)
    idx = jnp.stack([w8, z, core, low, level, w8, w8, w8]).astype(jnp.int32)

    bases = jnp.where(low == 0, jnp.array([0, 768]), jnp.array([512, 256]))
    position = (bases[:, None] + jnp.arange(HALF)[None, :]).reshape(ROWS).astype(F32)
    halfway = HEAD_DIM // 2
    frequency = jnp.exp(jnp.arange(halfway, dtype=F32) * (-math.log(10000.0) / halfway))
    angle = position[:, None] * frequency[None, :]
    cosine = jnp.tile(jnp.cos(angle), (1, 4))
    sine = jnp.sin(angle)
    sine = jnp.concatenate([-sine, sine, -sine, sine], axis=1)

    def bias_pieces(layer):
        return mixer_bias[layer].reshape(PARTS), up_bias[layer]

    biases = jnp.concatenate([t for layer in range(layers) for t in bias_pieces(layer)])
    width = PARTS + D

    def bias_of(layer, start, size):
        at = width * layer + start
        return jnp.stack([b[at : at + size] for b in biases])[:, None]

    def mixer_piece(layer):
        return lax.dynamic_slice_in_dim(mixer_weight[layer], w8 * PIECE, PIECE, 0).reshape(PIECE, PARTS)

    def run_project(layer, x, pieces):
        gain, shift = norm_gain[layer], norm_shift[layer]
        return project(idx, x, gain[0:1], shift[0:1], bias_of(layer, 0, PARTS), cosine, sine, pieces)

    def run_feed(layer, x, o, pieces):
        gain, shift, bias = norm_gain[layer], norm_shift[layer], output_bias[layer]
        return feed(
            idx, x, o, gain[1:2], shift[1:2], bias[0:1], bias[1:2], bias_of(layer, PARTS, D), pieces
        )

    mixer0 = gather_direct(mixer_piece(0))
    feed0, feed1 = pack(idx, up_weight, down_weight, output_weight)
    biases = [biases] + [flip_narrow(biases, k) for k in (1, 2, 3)]
    mixer0, tokens, feed0, biases = gate((mixer0, tokens, feed0, biases))
    mixer0 = gather_first(whole(mixer0))
    rows = relocate(tokens)
    mixer0, feed0 = gate((mixer0, feed0))
    own, first = mixer0
    mixer0 = [own, first, second_axis(own), second_axis(first)]
    feed0 = gather_far(feed0)
    mixer0, rows, feed0 = gate((mixer0, rows, feed0))
    mixer0 = gather_last(mixer0)
    feed0 = gather_near(feed0)
    x0 = jnp.concatenate(rows).astype(F32)
    h1_0, q_0, kv = run_project(0, x0, mixer0)
    own_0, feed0 = gate((kv, feed0))
    near_0, far = within_chip(own_0, 1), between_chips(own_0)
    own, first = gather_first(whole(feed0))
    mixer1 = mixer_piece(1)
    state = attend_near(idx, q_0, own_0, near_0)
    state, far_0, own, first, mixer1, feed1 = gate((state, far, own, first, mixer1, feed1))
    far_near_0 = within_chip(far_0, 1)
    second = second_axis(own)
    mixer1 = gather_direct(mixer1)
    o_0, lse_0 = attend_far(idx, q_0, far_0, far_near_0, state)
    o_0, own, first, second, mixer1, feed1 = gate((o_0, own, first, second, mixer1, feed1))
    third = second_axis(first)
    others = [flip_wide(own, 1), flip_wide(first, 1), flip_wide(second, 1)]
    feed1 = gather_far(feed1)
    third, others, o_0, mixer1, feed1 = gate((third, others, o_0, mixer1, feed1))
    feed0 = [own, first, second, third] + others + [flip_wide(third, 1)]
    mixer1, feed1 = gather_plane(whole(mixer1)), gather_near(feed1)
    x1, x1_0, h2_0, g_0, gp_0 = run_feed(0, x0, o_0, feed0)
    x1, mixer1, feed1 = gate((x1, mixer1, feed1))
    mixer1 = gather_last(mixer1)
    own, first = gather_first(whole(feed1))
    h1_1, q_1, kv = run_project(1, x1, mixer1)
    own_1, own, first = gate((kv, own, first))
    near_1, far = within_chip(own_1, 1), between_chips(own_1)
    second = second_axis(own)
    state = attend_near(idx, q_1, own_1, near_1)
    state, far_1, own, first, second = gate((state, far, own, first, second))
    far_near_1 = within_chip(far_1, 1)
    third = second_axis(first)
    others = [flip_wide(own, 1), flip_wide(first, 1), flip_wide(second, 1)]
    o_1, lse_1 = attend_far(idx, q_1, far_1, far_near_1, state)
    o_1, third, others, cotangent = gate((o_1, third, others, cotangent))
    e = relocate(cotangent)
    feed1 = [own, first, second, third] + others + [flip_wide(third, 1)]
    x2, x1_1, h2_1, g_1, gp_1 = run_feed(1, x1, o_1, feed1)
    x2, e = gate((x2, e))
    x_out = relocate(x2.astype(BF))

    e = jnp.concatenate(e).astype(F32)
    dm, dz, e1, da, do, small_feed1 = feed_back(idx, e, x1_1, gp_1, norm_gain[1, 1:2], feed1)
    g_feed1 = feed_grads(idx, g_1, dm, h2_1, dz, o_1, da)
    do, x_out, g_feed1 = gate((do, x_out, g_feed1))
    g_feed1 = reduce_core(g_feed1)
    dq, dr, drow = attend_back_far(idx, q_1, do, o_1, lse_1, far_1, far_near_1)
    dr, dq, g_feed1 = gate((dr, dq, g_feed1))
    far = between_chips(added(dr, within_chip(dr, 0)))
    g_feed1 = reduce_first(g_feed1)
    dq, dn, dc = attend_back_near(idx, q_1, do, lse_1, drow, dq, own_1, near_1)
    dc, far, g_feed1 = gate((dc, far, g_feed1))
    got = within_chip(dc, 0)
    g_feed1 = reduce_second(g_feed1)
    dpz, e, small_mixer1 = project_back(
        idx, dq, dn, dc, got, far, cosine, sine, x1, e1, norm_gain[1, 0:1], mixer1
    )
    dpz, e, g_feed1 = gate((dpz, e, g_feed1))
    g_feed1 = reduce_near(g_feed1)
    g_mixer1 = project_grads(idx, h1_1, dpz)
    e, g_mixer1 = gate((e, g_mixer1))
    g_mixer1 = reduce_core(g_mixer1)
    dm, dz, e1, da, do, small_feed0 = feed_back(idx, e, x1_0, gp_0, norm_gain[0, 1:2], feed0)
    dm, do, g_feed1, g_mixer1 = gate((dm, do, g_feed1, g_mixer1))
    g_feed1, g_mixer1 = reduce_far(g_feed1), reduce_plane(g_mixer1)
    g_feed0 = feed_grads(idx, g_0, dm, h2_0, dz, o_0, da)
    do, g_feed1, g_mixer1, g_feed0 = gate((do, g_feed1, g_mixer1, g_feed0))
    g_mixer1, g_feed0 = reduce_narrow(g_mixer1), reduce_core(g_feed0)
    g_feed1 = spread_first(g_feed1)
    dq, dr, drow = attend_back_far(idx, q_0, do, o_0, lse_0, far_0, far_near_0)
    dr, dq, g_feed1, g_mixer1, g_feed0 = gate((dr, dq, g_feed1, g_mixer1, g_feed0))
    far = between_chips(added(dr, within_chip(dr, 0)))
    g_feed0, g_feed1 = reduce_first(g_feed0), gather_second(g_feed1)
    dq, dn, dc = attend_back_near(idx, q_0, do, lse_0, drow, dq, own_0, near_0)
    dc, far, g_feed0, g_feed1 = gate((dc, far, g_feed0, g_feed1))
    got = within_chip(dc, 0)
    g_feed0 = reduce_second(g_feed0)
    total, *others = g_mixer1
    g_mixer1 = gather_first(added(total[0], *others))
    dpz, e, small_mixer0 = project_back(
        idx, dq, dn, dc, got, far, cosine, sine, x0, e1, norm_gain[0, 0:1], mixer0
    )
    e, dpz, g_feed0, g_mixer1 = gate((e, dpz, g_feed0, g_mixer1))
    g_feed0 = reduce_near(g_feed0)
    g_mixer0 = project_grads(idx, h1_0, dpz)
    smalls = jnp.concatenate([small_feed0, small_mixer0, small_feed1, small_mixer1])
    g_mixer0, smalls, g_feed0, g_feed1, g_mixer1, e = gate((g_mixer0, smalls, g_feed0, g_feed1, g_mixer1, e))
    g_mixer0 = reduce_core(g_mixer0)
    smalls = smalls, flip_wide(smalls, 1)
    g_mixer0, smalls, e = gate((g_mixer0, smalls, e))
    g_mixer0 = reduce_plane(g_mixer0)
    rows = relocate(e.astype(BF))
    smalls = smalls[0] + smalls[1]
    smalls = smalls, first_axis(smalls)
    g_feed1 = gather_last(g_feed1)
    feed_out = finish_feed(idx, 1, layers, g_feed1, None)
    g_mixer0, g_feed0, smalls, feed_out, rows, g_mixer1 = gate((g_mixer0, g_feed0, smalls, feed_out, rows, g_mixer1))
    keep, got, *others = g_mixer0
    total = added(keep[0], got[0], *others)
    bit = 8
    while bit < lax.axis_size("wide"):
        total = added(total, flip_wide(total, bit))
        bit *= 2
    g_mixer0 = total, flip_narrow(total[2:], 1)
    g_feed0 = reduce_far(g_feed0)
    smalls = smalls[0] + smalls[1]
    smalls = smalls, second_axis(smalls)
    g_mixer1 = gather_second(g_mixer1)
    g_mixer0, g_feed0, smalls, g_mixer1 = gate((g_mixer0, g_feed0, smalls, g_mixer1))
    g_mixer0, g_feed0 = reduce_far(g_mixer0), spread_first(g_feed0)
    smalls = smalls[0] + smalls[1]
    bit = 8
    while bit < lax.axis_size("wide"):
        smalls = smalls + flip_wide(smalls, bit)
        bit *= 2
    smalls = smalls, flip_narrow(smalls, 1)
    g_mixer1 = gather_last(g_mixer1)
    mixer_out = finish_mixer(idx, 1, layers, g_mixer1, None)
    g_mixer0, g_feed0, smalls, mixer_out = gate((g_mixer0, g_feed0, smalls, mixer_out))
    g_mixer0, g_feed0 = spread_first(g_mixer0), gather_second(g_feed0)
    smalls = smalls[0] + smalls[1]
    smalls = smalls, flip_narrow(smalls, 2)
    g_mixer0, g_feed0, smalls = gate((g_mixer0, g_feed0, smalls))
    g_mixer0 = gather_second(g_mixer0)
    smalls = smalls[0] + smalls[1]
    g_feed0 = gather_last(g_feed0)
    feed_out = finish_feed(idx, 0, layers, g_feed0, feed_out)
    g_mixer0, feed_out = gate((g_mixer0, feed_out))
    g_mixer0 = gather_last(g_mixer0)
    mixer_out = finish_mixer(idx, 0, layers, g_mixer0, mixer_out)
    tokens_grad = jnp.concatenate(rows)
    x_out = jnp.concatenate(x_out)

    small = smalls.reshape(layers, 16, D)
    up_bias_grad = lax.dynamic_index_in_dim(small[:, 0:4], z, 1, keepdims=False)
    mixer_bias_grad = lax.dynamic_index_in_dim(small[:, 8:12, :PARTS], z, 1, keepdims=False)
    return (
        x_out,
        tokens_grad,
        jnp.stack([small[:, 12], small[:, 6]], axis=1),
        jnp.stack([small[:, 13], small[:, 7]], axis=1),
        mixer_out.reshape(layers, D, 3, HEADS_COLS),
        mixer_bias_grad.reshape(layers, 3, HEADS_COLS),
        feed_out[2],
        jnp.stack([small[:, 5], small[:, 4]], axis=1),
        feed_out[0],
        up_bias_grad,
        feed_out[1],
    )


def solution(mesh):
    rows = P(("wide", "narrow"), None)
    quarters = (
        P(None, None, None, "narrow"),
        P(None, None, "narrow"),
        P(None, "narrow", None),
        P(),
        P(None, None, "narrow"),
        P(None, "narrow"),
        P(None, "narrow", None),
    )
    return jax.shard_map(
        per_device,
        mesh=mesh,
        in_specs=(rows, P("wide"), P(), P()) + quarters + (rows,),
        out_specs=(rows, rows, P(), P()) + quarters,
        check_vma=False,
    )
```

```python
import functools
import math

import jax
import jax.numpy as jnp
from jax import lax
from jax.experimental import pallas as pl
from jax.experimental.pallas import tpu as pltpu
from jax.sharding import PartitionSpec as P

HEAD_DIM = 64
LEN = 1024
EPSILON = 1e-05
D = 768
QUARTERS = 4
HALF = 256
ROWS = 512
PIECE = 96
HEADS_COLS = 192
PARTS = 576
PACK = 224
MASKED = -1e30
BF = jnp.bfloat16
F32 = jnp.float32
NT = (((1,), (1,)), ((), ()))
TN = (((0,), (0,)), ((), ()))
VMEM_LIMIT = 56 * 1024 * 1024


def dot(a, b):
    return jnp.dot(a, b, preferred_element_type=F32)


def dot_nt(a, b):
    return lax.dot_general(a, b, NT, preferred_element_type=F32)


def dot_tn(a, b):
    return lax.dot_general(a, b, TN, preferred_element_type=F32)


def norm_parts(values):
    center = values - jnp.mean(values, axis=-1, keepdims=True)
    inverse = lax.rsqrt(jnp.mean(center * center, axis=-1, keepdims=True) + EPSILON)
    return center * inverse, inverse


def norm_backward(grad_in, unit_rows, inverse, gain):
    scaled = grad_in * gain
    return inverse * (
        scaled
        - jnp.mean(scaled, axis=-1, keepdims=True)
        - unit_rows * jnp.mean(scaled * unit_rows, axis=-1, keepdims=True)
    )


def swap_halves(u):
    lane = lax.broadcasted_iota(jnp.int32, u.shape, 1)
    return jnp.where((lane & 63) < 32, pltpu.roll(u, 96, axis=1), pltpu.roll(u, 32, axis=1))


def rot(u, cosine, sine):
    return u * cosine + swap_halves(u) * sine


def unrot(u, cosine, sine):
    return u * cosine - swap_halves(u) * sine


ORDER = (0, 2, 1, 3)


def flips(idx):
    first, second = 2 + 2 * idx[2], 4 - 2 * idx[2]
    return [0, first, second, 6, 1, 1 ^ second, 1 ^ first, 7]


def piece_copies(refs, idx, sems, place):
    copies = []
    for flip, ref in zip(flips(idx), refs):
        for at, k in enumerate(ORDER):
            for source, target in place(ref.at[at], k, idx[1] ^ k, idx[0] ^ flip):
                copies.append(pltpu.make_async_copy(source, target, sems.at[len(copies)]))
    return copies


def rows_at(start, size, unit):
    return pl.ds(pl.multiple_of(start, unit), size)


def mixer_copies(refs, idx, sems, weights):
    def place(src, k, zq, wq):
        return [(src, weights.at[zq, rows_at(wq * PIECE, PIECE, 32)])]

    return piece_copies(refs, idx, sems, place)


def up_down_copies(refs, idx, sems, ups, downs):
    def place(src, k, zq, wq):
        rows = rows_at(wq * PIECE, PIECE, 32)
        return [
            (src.at[pl.ds(0, PIECE)], ups.at[k, rows]),
            (src.at[pl.ds(PIECE, PIECE)], downs.at[k, rows]),
        ]

    return piece_copies(refs, idx, sems, place)


def packed_copies(refs, idx, sems, packed):
    def place(src, k, zq, wq):
        return [(src.at[pl.ds(2 * PIECE, 32)], packed.at[zq, wq])]

    return piece_copies(refs, idx, sems, place)


def unpack_output(packed, weights):
    for zq in range(QUARTERS):
        for chip in range(4):
            for part in range(2):
                for s in range(3):
                    row = HEADS_COLS * zq + 48 * chip + 16 * s
                    weights[row : row + 16, 384 * part : 384 * part + 384] = packed[
                        zq, 2 * chip + part, 16 * (s // 2) : 16 * (s // 2) + 16, 384 * (s % 2) : 384 * (s % 2) + 384
                    ]


def any_spec():
    return pl.BlockSpec(memory_space=pl.ANY)


def vmem_spec():
    return pl.BlockSpec(memory_space=pltpu.VMEM)


def smem_spec():
    return pl.BlockSpec(memory_space=pltpu.SMEM)


def kernel_call(body, in_specs, out_shape, out_specs, scratch, args, flops, moved, aliases=None, name=None):
    return pl.pallas_call(
        body,
        in_specs=in_specs,
        out_specs=out_specs,
        out_shape=out_shape,
        scratch_shapes=scratch,
        input_output_aliases=aliases or {},
        compiler_params=pltpu.CompilerParams(vmem_limit_bytes=VMEM_LIMIT),
        cost_estimate=pl.CostEstimate(flops=1000, bytes_accessed=1000, transcendentals=0),
        name=name,
    )(*args)


def sds(shape, dtype):
    return jax.ShapeDtypeStruct(shape, dtype)


def project_body(idx, x, gain, shift, bias, cosine, sine, *rest):
    pieces, (h1, q, kv, weights, wide, sems) = rest[:8], rest[8:]
    copies = mixer_copies(pieces, idx, sems, weights)
    for copy in copies:
        copy.start()

    def norm_rows(i, carry):
        rows = rows_at(i * 128, 128, 128)
        unit, _ = norm_parts(x[rows])
        h1[rows] = (unit * gain[...] + shift[...]).astype(BF)
        return carry

    lax.fori_loop(0, 4, norm_rows, 0)
    for copy in copies:
        copy.wait()
    for zq in range(QUARTERS):
        p = dot(h1[...], weights[zq]) + bias[idx[1] ^ zq]
        for part in range(3):
            col = D * part + HEADS_COLS * zq
            wide[:, col : col + HEADS_COLS] = p[:, HEADS_COLS * part : HEADS_COLS * (part + 1)]
    for half in range(2):
        rows = slice(HALF * half, HALF * (half + 1))
        for j in range(6):
            cols = slice(128 * j, 128 * (j + 1))
            q[rows, cols] = (rot(wide[rows, cols], cosine[rows], sine[rows]) * 0.125).astype(BF)
            kcols = slice(D + 128 * j, D + 128 * (j + 1))
            kv[rows, cols] = rot(wide[rows, kcols], cosine[rows], sine[rows]).astype(BF)
        kv[rows, D:] = wide[rows, 2 * D :].astype(BF)


def project(idx, x, gain, shift, bias, cosine, sine, pieces):
    return kernel_call(
        project_body,
        [smem_spec()] + [vmem_spec()] * 6 + [any_spec()] * 8,
        [sds((ROWS, D), BF), sds((ROWS, D), BF), sds((ROWS, 2 * D), BF)],
        [vmem_spec()] * 3,
        [
            pltpu.VMEM((QUARTERS, D, PARTS), BF),
            pltpu.VMEM((ROWS, 3 * D), F32),
            pltpu.SemaphoreType.DMA((32,)),
        ],
        (idx, x, gain, shift, bias, cosine, sine, *pieces),
        2 * ROWS * D * 3 * D,
        8e6,
        name="project",
    )


def load_near(idx, own, near, kvn, kvc, sems):
    clean = idx[2] == 1
    copy = pltpu.make_async_copy(own, kvn, sems.at[0])
    copy.start()
    a = pltpu.make_async_copy(own, kvc, sems.at[1])
    b = pltpu.make_async_copy(near, kvc, sems.at[1])
    pl.when(clean)(a.start)
    pl.when(jnp.logical_not(clean))(b.start)
    return [copy, a]


def load_far(idx, far, far_near, kvr, sem):
    clean = idx[2] == 1
    a = pltpu.make_async_copy(far, kvr, sem)
    b = pltpu.make_async_copy(far_near, kvr, sem)
    pl.when(clean)(a.start)
    pl.when(jnp.logical_not(clean))(b.start)
    return a


NEAR_TILES = {0: [(0, [(0, True)]), (1, [(1, True), (0, False)])], 1: [(1, [(1, True)]), (0, [(0, True), (1, False)])]}
FAR_TILES = {0: [(1, [0, 1])], 1: [(1, [0]), (0, [0])]}


def set_masks(idx, bias, bias_n, query_dim):
    clean, level = idx[2], idx[4]
    qi = lax.shift_right_logical(lax.broadcasted_iota(jnp.int32, (HALF, HALF), query_dim), level)
    ki = lax.shift_right_logical(lax.broadcasted_iota(jnp.int32, (HALF, HALF), 1 - query_dim), level)
    allowed = jnp.where(ki < qi + clean, 0.0, MASKED)
    bias[...] = jnp.concatenate([allowed, allowed], axis=query_dim)
    same = (jnp.where(ki == qi, 0, 1) + clean)[:128, :128]
    own = jnp.where(same == 0, 0.0, MASKED)
    bias_n[...] = jnp.concatenate([own, own], axis=query_dim)


def lanes(rows):
    return lax.broadcasted_iota(jnp.int32, (rows, 128), 1)


def one_head(v, side):
    low_lane = lanes(v.shape[0]) < 64
    return jnp.where(low_lane if side == 0 else jnp.logical_not(low_lane), v, jnp.zeros_like(v))


def both_heads(v):
    return jnp.concatenate([one_head(v, 0), one_head(v, 1)], axis=0)


def pair_lanes(v):
    n = v.shape[0] // 2
    return jnp.where(lanes(n) < 64, v[:n], v[n:])


def pair_cols(hp):
    off = pl.multiple_of(hp * 128, 128)
    return pl.ds(off, 128), pl.ds(pl.multiple_of(D + off, 128), 128)


def row_max(s):
    return jnp.max(s, axis=-1, keepdims=True)


def with_ones(v):
    return jnp.concatenate([v, jnp.ones_like(v)], axis=1)


def half_rows(half):
    return slice(HALF * half, HALF * (half + 1))


def attend_near_body(idx, q, own, near, acc, tops, counts, kvn, kvc, bias, bias_n, sems):
    waits = load_near(idx, own, near, kvn, kvc, sems)
    set_masks(idx, bias, bias_n, 0)
    tops[...] = jnp.zeros_like(tops)
    counts[...] = jnp.ones_like(counts)
    for copy in waits:
        copy.wait()

    def run(tiles):
        def pair(hp, carry):
            cols, vcols = pair_cols(hp)
            lane = lanes(HALF)
            for half, sources in tiles:
                rows = half_rows(half)
                qs = both_heads(q[rows, cols])
                scores = []
                for kh, diagonal in sources:
                    s = dot_nt(qs, kvc[half_rows(kh), cols])
                    scores.append(s + bias[...] if diagonal else s)
                blocks = [slice(HALF * half + 128 * t, HALF * half + 128 * (t + 1)) for t in range(2)]

                def of_block(v, t):
                    return jnp.concatenate([v[128 * t : 128 * (t + 1)], v[HALF + 128 * t : HALF + 128 * (t + 1)]], axis=0)

                def of_heads(a, b):
                    return jnp.concatenate([a[:128], b[:128], a[128:], b[128:]], axis=0)

                mine = [dot_nt(of_block(qs, t), kvn[blocks[t], cols]) + bias_n[...] for t in range(2)]
                top = of_heads(*[row_max(s) for s in mine])
                for s in scores:
                    top = jnp.maximum(top, row_max(s))
                total = of_heads(
                    *[
                        dot(jnp.exp(mine[t] - of_block(top, t)).astype(BF), with_ones(kvn[blocks[t], vcols]))
                        for t in range(2)
                    ]
                )
                for s, (kh, diagonal) in zip(scores, sources):
                    total = total + dot(jnp.exp(s - top).astype(BF), with_ones(kvc[half_rows(kh), vcols]))
                acc[rows, cols] = pair_lanes(total[:, :128])
                for target, value in ((tops, top), (counts, total[:, 128:])):
                    target[rows] = jnp.where(
                        lane == 2 * hp, value[:HALF], jnp.where(lane == 2 * hp + 1, value[HALF:], target[rows])
                    )
            return carry

        lax.fori_loop(0, 6, pair, 0)

    for zl in range(2):
        pl.when(idx[3] == zl)(functools.partial(run, NEAR_TILES[zl]))


def attend_near(idx, q, own, near):
    return kernel_call(
        attend_near_body,
        [smem_spec(), vmem_spec()] + [any_spec()] * 2,
        [sds((ROWS, D), F32), sds((ROWS, 128), F32), sds((ROWS, 128), F32)],
        [vmem_spec()] * 3,
        [
            pltpu.VMEM((ROWS, 2 * D), BF),
            pltpu.VMEM((ROWS, 2 * D), BF),
            pltpu.VMEM((2 * HALF, HALF), F32),
            pltpu.VMEM((HALF, 128), F32),
            pltpu.SemaphoreType.DMA((2,)),
        ],
        (idx, q, own, near),
        8e9,
        6e6,
        name="attend_near",
    )


def attend_far_body(idx, q, far, far_near, acc, tops, counts, o, lse, kvr, last, sem):
    copy = load_far(idx, far, far_near, kvr, sem)
    last[...] = tops[...] + jnp.log(counts[...])
    copy.wait()

    def column(values, head):
        return jnp.sum(jnp.where(lanes(HALF) == head, values, 0.0), axis=-1, keepdims=True)

    def run(tiles):
        covered = [half for half, _ in tiles]

        def pair(hp, carry):
            cols, vcols = pair_cols(hp)
            lane = lanes(HALF)
            for half in range(2):
                rows = half_rows(half)
                if half in covered:
                    sources = dict(tiles)[half]
                    q2 = q[rows, cols]
                    sides = []
                    for side in range(2):
                        qm = one_head(q2, side)
                        scores = [dot_nt(qm, kvr[half_rows(kh), cols]) for kh in sources]
                        before = column(tops[rows], 2 * hp + side)
                        top = before
                        for s in scores:
                            top = jnp.maximum(top, row_max(s))
                        shrink = jnp.exp(before - top)
                        total = None
                        for s, kh in zip(scores, sources):
                            part = dot(jnp.exp(s - top).astype(BF), with_ones(kvr[half_rows(kh), vcols]))
                            total = part if total is None else total + part
                        count = column(counts[rows], 2 * hp + side) * shrink + total[:, 128:]
                        value = (acc[rows, cols] * shrink + total[:, :128]) / count
                        sides.append((value, top + jnp.log(count)))
                    last[rows] = jnp.where(
                        lane == 2 * hp, sides[0][1], jnp.where(lane == 2 * hp + 1, sides[1][1], last[rows])
                    )
                else:
                    sides = [(acc[rows, cols] / column(counts[rows], 2 * hp + side),) for side in range(2)]
                o[rows, cols] = jnp.where(lane < 64, sides[0][0], sides[1][0]).astype(BF)
            return carry

        lax.fori_loop(0, 6, pair, 0)

    for zl in range(2):
        pl.when(idx[3] == zl)(functools.partial(run, FAR_TILES[zl]))
    across = jnp.transpose(last[...])
    for head in range(12):
        lse[head] = across[head : head + 1]


def attend_far(idx, q, far, far_near, state):
    return kernel_call(
        attend_far_body,
        [smem_spec(), vmem_spec()] + [any_spec()] * 2 + [vmem_spec()] * 3,
        [sds((ROWS, D), BF), sds((12, 1, ROWS), F32)],
        [vmem_spec()] * 2,
        [
            pltpu.VMEM((ROWS, 2 * D), BF),
            pltpu.VMEM((ROWS, 128), F32),
            pltpu.SemaphoreType.DMA,
        ],
        (idx, q, far, far_near, *state),
        5e9,
        6e6,
        name="attend_far",
    )


def feed_body(idx, x, o, gain, shift, out_bias, down_bias, up_bias, *rest):
    pieces, (x2, x1, h2, g, gp, ups, downs, packed, outw, sems, sems_o) = rest[:8], rest[8:]
    first = packed_copies(pieces, idx, sems_o, packed)
    later = up_down_copies(pieces, idx, sems, ups, downs)
    for copy in first + later:
        copy.start()
    for copy in first:
        copy.wait()
    unpack_output(packed, outw)
    x1[...] = x[...] + (dot(o[...], outw[...]) + out_bias[...])

    def norm_rows(i, carry):
        rows = rows_at(i * 128, 128, 128)
        unit, _ = norm_parts(x1[rows])
        h2[rows] = (unit * gain[...] + shift[...]).astype(BF)
        x2[rows] = x1[rows] + down_bias[...]
        return carry

    lax.fori_loop(0, 4, norm_rows, 0)
    for copy in later:
        copy.wait()

    def hidden(k, carry):
        for n in range(3):
            cols = slice(256 * n, 256 * (n + 1))
            u = dot(h2[...], ups[k, :, cols]) + up_bias[k, :, cols]
            uu = u * u
            t = jnp.tanh(0.7978845608028654 * u * (1.0 + 0.044715 * uu))
            half_t = 0.5 + 0.5 * t
            g[k, :, cols] = (u * half_t).astype(BF)
            slope = half_t + (0.5 * 0.7978845608028654) * u * (1.0 - t * t) * (1.0 + 0.134145 * uu)
            gp[k, :, cols] = slope.astype(BF)
        x2[...] += dot(g[k], downs[k])
        return carry

    lax.fori_loop(0, QUARTERS, hidden, 0)


WEIGHT_SCRATCH = [
    ((QUARTERS, D, D), BF),
    ((QUARTERS, D, D), BF),
    ((QUARTERS, 8, 32, D), BF),
    ((D, D), BF),
]


def feed(idx, x, o, gain, shift, out_bias, down_bias, up_bias, pieces):
    return kernel_call(
        feed_body,
        [smem_spec()] + [vmem_spec()] * 7 + [any_spec()] * 8,
        [
            sds((ROWS, D), F32),
            sds((ROWS, D), F32),
            sds((ROWS, D), BF),
            sds((QUARTERS, ROWS, D), BF),
            sds((QUARTERS, ROWS, D), BF),
        ],
        [vmem_spec()] * 5,
        [pltpu.VMEM(s, t) for s, t in WEIGHT_SCRATCH]
        + [pltpu.SemaphoreType.DMA((64,)), pltpu.SemaphoreType.DMA((32,))],
        (idx, x, o, gain, shift, out_bias, down_bias, up_bias, *pieces),
        2 * ROWS * D * D * 9,
        25e6,
        name="feed",
    )


def feed_back_body(idx, e, x1, gp, gain, *rest):
    pieces, (dm, dz, e1, da, do, small, ups, downs, packed, outw, dh2, hidden_sums, sems, sems_o) = rest[:8], rest[8:]
    first = packed_copies(pieces, idx, sems_o, packed)
    later = up_down_copies(pieces, idx, sems, ups, downs)
    for copy in later + first:
        copy.start()
    dm[...] = e[...].astype(BF)
    small[4:5] = jnp.sum(dm[...].astype(F32), axis=0, keepdims=True)
    dh2[...] = jnp.zeros_like(dh2)
    for copy in later:
        copy.wait()

    def hidden(k, carry):
        zq = idx[1] ^ k
        for n in range(3):
            cols = slice(256 * n, 256 * (n + 1))
            part = (dot_nt(dm[...], downs[k, cols]) * gp[k, :, cols].astype(F32)).astype(BF)
            dz[k, :, cols] = part
            hidden_sums[zq, :, cols] = jnp.sum(part.astype(F32), axis=0, keepdims=True)
        dh2[...] += dot_nt(dz[k], ups[k])
        return carry

    lax.fori_loop(0, QUARTERS, hidden, 0)
    for copy in first:
        copy.wait()
    unpack_output(packed, outw)
    for zq in range(QUARTERS):
        small[zq : zq + 1] = hidden_sums[zq]
    small[5:8] = jnp.zeros((3, D), F32)

    def norm_rows(i, carry):
        rows = rows_at(i * 128, 128, 128)
        unit, inverse = norm_parts(x1[rows])
        grad = dh2[rows]
        up = e[rows] + norm_backward(grad, unit, inverse, gain[...])
        e1[rows] = up
        low = up.astype(BF)
        da[rows] = low
        small[5:6] += jnp.sum(low.astype(F32), axis=0, keepdims=True)
        small[6:7] += jnp.sum(grad * unit, axis=0, keepdims=True)
        small[7:8] += jnp.sum(grad, axis=0, keepdims=True)
        return carry

    lax.fori_loop(0, 4, norm_rows, 0)
    do[...] = dot_nt(da[...], outw[...]).astype(BF)


def feed_back(idx, e, x1, gp, gain, pieces):
    return kernel_call(
        feed_back_body,
        [smem_spec()] + [vmem_spec()] * 4 + [any_spec()] * 8,
        [
            sds((ROWS, D), BF),
            sds((QUARTERS, ROWS, D), BF),
            sds((ROWS, D), F32),
            sds((ROWS, D), BF),
            sds((ROWS, D), BF),
            sds((8, D), F32),
        ],
        [vmem_spec()] * 6,
        [pltpu.VMEM(s, t) for s, t in WEIGHT_SCRATCH]
        + [pltpu.VMEM((ROWS, D), F32), pltpu.VMEM((QUARTERS, 1, D), F32), pltpu.SemaphoreType.DMA((64,)), pltpu.SemaphoreType.DMA((32,))],
        (idx, e, x1, gp, gain, *pieces),
        2 * ROWS * D * D * 9,
        25e6,
        name="feed_back",
    )


def spread(idx, keep, send, source, k, wq, rows, sem):
    w8, mine = idx[0], idx[2]
    j = (wq >> 1) ^ (w8 >> 1)
    turned = ((j & 1) << 1) | (j >> 1)
    at = ((k & 1) << 1) | (k >> 1)
    here, there = jnp.where(mine == 1, j, turned), jnp.where(mine == 1, turned, j)
    a = pltpu.make_async_copy(source, keep.at[here, at, rows], sem)
    b = pltpu.make_async_copy(source, send.at[there, at, rows], sem)
    pl.when((wq & 1) == mine)(a.start)
    pl.when((wq & 1) != mine)(b.start)
    return a


def feed_grads_body(idx, g, dm, h2, dz, o, da, keep, send, flipped, turned, d_up, d_down, d_out, sems):
    waits = []
    flipped[...] = jnp.transpose(o[...])
    turned[...] = dot(flipped[...], da[...]).astype(BF)
    for zq in range(QUARTERS):
        for chip in range(4):
            for part in range(2):
                for s in range(4):
                    rows, cols = slice(16 * (s // 2), 16 * (s // 2) + 16), slice(384 * (s % 2), 384 * (s % 2) + 384)
                    if s == 3:
                        block = jnp.zeros((16, 384), BF)
                    else:
                        row = HEADS_COLS * zq + 48 * chip + 16 * s
                        block = turned[row : row + 16, 384 * part : 384 * part + 384]
                    d_out[zq, 2 * chip + part, rows, cols] = block
    for zq in range(QUARTERS):
        k = idx[1] ^ zq
        for wq in range(8):
            sem = sems.at[len(waits)]
            waits.append(spread(idx, keep, send, d_out.at[zq, wq], k, wq, pl.ds(2 * PIECE, 32), sem))
    for k in range(QUARTERS):
        flipped[...] = jnp.transpose(g[k])
        d_down[k] = dot(flipped[...], dm[...]).astype(BF)
        for wq in range(8):
            sem = sems.at[len(waits)]
            source = d_down.at[k, pl.ds(PIECE * wq, PIECE)]
            waits.append(spread(idx, keep, send, source, k, wq, pl.ds(PIECE, PIECE), sem))
    flipped[...] = jnp.transpose(h2[...])
    for k in range(QUARTERS):
        d_up[k] = dot(flipped[...], dz[k]).astype(BF)
        for wq in range(8):
            sem = sems.at[len(waits)]
            source = d_up.at[k, pl.ds(PIECE * wq, PIECE)]
            waits.append(spread(idx, keep, send, source, k, wq, pl.ds(0, PIECE), sem))
    for copy in waits:
        copy.wait()


def feed_grads(idx, g, dm, h2, dz, o, da):
    return kernel_call(
        feed_grads_body,
        [smem_spec()] + [vmem_spec()] * 6,
        [sds((4, QUARTERS, PACK, D), BF)] * 2,
        [any_spec()] * 2,
        [
            pltpu.VMEM((D, ROWS), BF),
            pltpu.VMEM((D, D), BF),
            pltpu.VMEM((QUARTERS, D, D), BF),
            pltpu.VMEM((QUARTERS, D, D), BF),
            pltpu.VMEM((QUARTERS, 8, 32, D), BF),
            pltpu.SemaphoreType.DMA((96,)),
        ],
        (idx, g, dm, h2, dz, o, da),
        2 * ROWS * D * D * 9,
        25e6,
        name="feed_grads",
    )


def back_tile(q, do, lse, drow, cols, hp, k2, v2, qrow, n, bias_here):
    qs, gs = both_heads(q[qrow : qrow + n, cols]), both_heads(do[qrow : qrow + n, cols])

    def of_heads(ref):
        return jnp.concatenate([ref[2 * hp + side, :, qrow : qrow + n] for side in range(2)], axis=1)

    s = dot_nt(k2, qs)
    if bias_here is not None:
        s = s + bias_here
    p = jnp.exp(s - of_heads(lse))
    ds = (p * (dot_nt(v2, gs) - of_heads(drow))).astype(BF)
    return dot(ds, qs), dot(p.astype(BF), gs), pair_lanes(dot_tn(ds, k2))


def attend_back_far_body(idx, q, do, o, lse, far, far_near, dq, dr, drow, kvr, dcol, sem):
    copy = load_far(idx, far, far_near, kvr, sem)
    dcol[...] = jnp.zeros_like(dcol)

    def products(hp, carry):
        cols, _ = pair_cols(hp)
        lane = lanes(ROWS)
        both = do[:, cols].astype(F32) * o[:, cols].astype(F32)
        first = jnp.sum(jnp.where(lane < 64, both, 0.0), axis=-1, keepdims=True)
        second = jnp.sum(jnp.where(lane < 64, 0.0, both), axis=-1, keepdims=True)
        dcol[...] = jnp.where(lane == 2 * hp, first, jnp.where(lane == 2 * hp + 1, second, dcol[...]))
        return carry

    lax.fori_loop(0, 6, products, 0)
    across = jnp.transpose(dcol[...])
    for head in range(12):
        drow[head] = across[head : head + 1]
    copy.wait()

    def run(tiles):
        def pair(hp, carry):
            cols, vcols = pair_cols(hp)
            dq_half = [None, None]
            for kh in range(2):
                keys = half_rows(kh)
                total = None
                for half, sources in tiles:
                    if kh in sources:
                        parts = back_tile(
                            q, do, lse, drow, cols, hp, kvr[keys, cols], kvr[keys, vcols], HALF * half, HALF, None
                        )
                        total = parts[:2] if total is None else (total[0] + parts[0], total[1] + parts[1])
                        dq_half[half] = parts[2] if dq_half[half] is None else dq_half[half] + parts[2]
                if total is None:
                    total = (jnp.zeros((HALF, 128), F32),) * 2
                dr[keys, cols] = total[0].astype(BF)
                dr[keys, vcols] = total[1].astype(BF)
            for half in range(2):
                part = dq_half[half]
                dq[half_rows(half), cols] = jnp.zeros((HALF, 128), F32) if part is None else part
            return carry

        lax.fori_loop(0, 6, pair, 0)

    for zl in range(2):
        pl.when(idx[3] == zl)(functools.partial(run, FAR_TILES[zl]))


def attend_back_far(idx, q, do, o, lse, far, far_near):
    return kernel_call(
        attend_back_far_body,
        [smem_spec()] + [vmem_spec()] * 4 + [any_spec()] * 2,
        [sds((ROWS, D), F32), sds((ROWS, 2 * D), BF), sds((12, 1, ROWS), F32)],
        [vmem_spec()] * 3,
        [
            pltpu.VMEM((ROWS, 2 * D), BF),
            pltpu.VMEM((ROWS, 128), F32),
            pltpu.SemaphoreType.DMA,
        ],
        (idx, q, do, o, lse, far, far_near),
        12e9,
        8e6,
        name="attend_back_far",
    )


def attend_back_near_body(idx, q, do, lse, drow, dq_far, own, near, dq, dn, dc, kvn, kvc, bias, bias_n, sems):
    waits = load_near(idx, own, near, kvn, kvc, sems)
    set_masks(idx, bias, bias_n, 1)
    for copy in waits:
        copy.wait()

    def run(tiles):
        def pair(hp, carry):
            cols, vcols = pair_cols(hp)
            dq_half = [None, None]
            for half in range(2):
                pieces = []
                for t in range(2):
                    rows = slice(HALF * half + 128 * t, HALF * half + 128 * (t + 1))
                    dk, dv, dqs = back_tile(
                        q, do, lse, drow, cols, hp, kvn[rows, cols], kvn[rows, vcols], rows.start, 128, bias_n[...]
                    )
                    dn[rows, cols] = dk.astype(BF)
                    dn[rows, vcols] = dv.astype(BF)
                    pieces.append(dqs)
                dq_half[half] = dq_far[half_rows(half), cols] + jnp.concatenate(pieces, axis=0)
            for kh in range(2):
                keys = half_rows(kh)
                total = None
                for half, sources in tiles:
                    if kh in dict(sources):
                        parts = back_tile(
                            q,
                            do,
                            lse,
                            drow,
                            cols,
                            hp,
                            kvc[keys, cols],
                            kvc[keys, vcols],
                            HALF * half,
                            HALF,
                            bias[...] if dict(sources)[kh] else None,
                        )
                        total = parts[:2] if total is None else (total[0] + parts[0], total[1] + parts[1])
                        dq_half[half] = dq_half[half] + parts[2]
                dc[keys, cols] = total[0].astype(BF)
                dc[keys, vcols] = total[1].astype(BF)
            for half in range(2):
                dq[half_rows(half), cols] = dq_half[half] * 0.125
            return carry

        lax.fori_loop(0, 6, pair, 0)

    for zl in range(2):
        pl.when(idx[3] == zl)(functools.partial(run, NEAR_TILES[zl]))


def attend_back_near(idx, q, do, lse, drow, dq_far, own, near):
    return kernel_call(
        attend_back_near_body,
        [smem_spec()] + [vmem_spec()] * 5 + [any_spec()] * 2,
        [sds((ROWS, D), F32), sds((ROWS, 2 * D), BF), sds((ROWS, 2 * D), BF)],
        [vmem_spec()] * 3,
        [
            pltpu.VMEM((ROWS, 2 * D), BF),
            pltpu.VMEM((ROWS, 2 * D), BF),
            pltpu.VMEM((HALF, 2 * HALF), F32),
            pltpu.VMEM((128, HALF), F32),
            pltpu.SemaphoreType.DMA((2,)),
        ],
        (idx, q, do, lse, drow, dq_far, own, near),
        18e9,
        12e6,
        name="attend_back_near",
    )


def project_back_body(idx, dq, dn, dcr, got, far, cosine, sine, x, e1, gain, *rest):
    pieces, (dpz, e, small, weights, wide, sems) = rest[:8], rest[8:]
    copies = mixer_copies(pieces, idx, sems, weights)
    for copy in copies:
        copy.start()
    noisy = idx[2] == 0
    for half in range(2):
        rows = slice(HALF * half, HALF * (half + 1))
        for j in range(6):
            cols = slice(128 * j, 128 * (j + 1))
            wide[rows, cols] = unrot(dq[rows, cols], cosine[rows], sine[rows])

        def total(cols, at=rows):
            summed = dcr[at, cols].astype(F32) + got[at, cols].astype(F32) + far[at, cols].astype(F32)
            return jnp.where(noisy, dn[at, cols].astype(F32), summed)

        for j in range(6):
            cols = slice(128 * j, 128 * (j + 1))
            wide[rows, D + 128 * j : D + 128 * (j + 1)] = unrot(total(cols), cosine[rows], sine[rows])
        wide[rows, 2 * D :] = total(slice(D, 2 * D))
    for copy in copies:
        copy.wait()
    small[...] = jnp.zeros_like(small)
    for zq in range(QUARTERS):
        for part in range(3):
            col = D * part + HEADS_COLS * zq
            dpz[zq, :, HEADS_COLS * part : HEADS_COLS * (part + 1)] = wide[:, col : col + HEADS_COLS].astype(BF)
        small[zq : zq + 1, :PARTS] = jnp.sum(dpz[zq].astype(F32), axis=0, keepdims=True)
        piece = dot_nt(dpz[zq], weights[zq])
        if zq == 0:
            e[...] = piece
        else:
            e[...] += piece

    def norm_rows(i, carry):
        rows = rows_at(i * 128, 128, 128)
        unit, inverse = norm_parts(x[rows])
        grad = e[rows]
        small[4:5] += jnp.sum(grad * unit, axis=0, keepdims=True)
        small[5:6] += jnp.sum(grad, axis=0, keepdims=True)
        e[rows] = e1[rows] + norm_backward(grad, unit, inverse, gain[...])
        return carry

    lax.fori_loop(0, 4, norm_rows, 0)


def project_back(idx, dq, dn, dcr, got, far, cosine, sine, x, e1, gain, pieces):
    return kernel_call(
        project_back_body,
        [smem_spec()] + [vmem_spec()] * 10 + [any_spec()] * 8,
        [sds((QUARTERS, ROWS, PARTS), BF), sds((ROWS, D), F32), sds((8, D), F32)],
        [vmem_spec()] * 3,
        [
            pltpu.VMEM((QUARTERS, D, PARTS), BF),
            pltpu.VMEM((ROWS, 3 * D), F32),
            pltpu.SemaphoreType.DMA((32,)),
        ],
        (idx, dq, dn, dcr, got, far, cosine, sine, x, e1, gain, *pieces),
        2 * ROWS * D * 3 * D,
        12e6,
        name="project_back",
    )


def project_grads_body(idx, h1, dpz, keep, send, flipped, stage, sems):
    waits = []
    flipped[...] = jnp.transpose(h1[...])
    for zq in range(QUARTERS):
        k = idx[1] ^ zq
        stage[zq] = dot(flipped[...], dpz[zq]).astype(BF)
        for wq in range(8):
            sem = sems.at[len(waits)]
            source = stage.at[zq, pl.ds(PIECE * wq, PIECE)]
            waits.append(spread(idx, keep, send, source, k, wq, pl.ds(0, PIECE), sem))
    for copy in waits:
        copy.wait()


def project_grads(idx, h1, dpz):
    return kernel_call(
        project_grads_body,
        [smem_spec()] + [vmem_spec()] * 2,
        [sds((4, QUARTERS, PIECE, PARTS), BF)] * 2,
        [any_spec()] * 2,
        [
            pltpu.VMEM((D, ROWS), BF),
            pltpu.VMEM((QUARTERS, D, PARTS), BF),
            pltpu.SemaphoreType.DMA((32,)),
        ],
        (idx, h1, dpz),
        2 * ROWS * D * 3 * D,
        9e6,
        name="project_grads",
    )


def finish_mixer_body(layer, filled, idx, *rest):
    pieces, rest = rest[:8], rest[8:]
    if filled:
        rest = rest[1:]
    out, stage, sem = rest
    for flip, piece in zip(flips(idx), pieces):
        stage[rows_at((idx[0] ^ flip) * PIECE, PIECE, 32)] = piece[...].astype(F32)
    copy = pltpu.make_async_copy(stage, out.at[layer], sem)
    copy.start()
    copy.wait()


def finish_mixer(idx, layer, layers, pieces, before):
    filled = before is not None
    return kernel_call(
        functools.partial(finish_mixer_body, layer, filled),
        [smem_spec()] + [vmem_spec()] * 8 + [any_spec()] * filled,
        sds((layers, D, PARTS), F32),
        any_spec(),
        [pltpu.VMEM((D, PARTS), F32), pltpu.SemaphoreType.DMA],
        (idx, *pieces) + ((before,) if filled else ()),
        1e6,
        4e6,
        aliases={9: 0} if filled else None,
        name="finish_mixer",
    )


def finish_feed_body(layer, filled, idx, *rest):
    pieces, rest = rest[:8], rest[8:]
    if filled:
        rest = rest[3:]
    up, down, out, up_s, down_s, out_s, sems = rest
    for flip, piece in zip(flips(idx), pieces):
        wq = idx[0] ^ flip
        rows = rows_at(wq * PIECE, PIECE, 32)
        up_s[rows] = piece[:PIECE].astype(F32)
        down_s[rows] = piece[PIECE : 2 * PIECE].astype(F32)
        cols = pl.ds(pl.multiple_of((wq & 1) * 384, 128), 384)
        for s in range(3):
            row = 2 * PIECE + 16 * (s // 2)
            block = piece[row : row + 16, 384 * (s % 2) : 384 * (s % 2) + 384]
            out_s[rows_at((wq >> 1) * 48 + 16 * s, 16, 16), cols] = block.astype(F32)
    copies = [
        pltpu.make_async_copy(stage, whole.at[layer], sems.at[i])
        for i, (stage, whole) in enumerate(((up_s, up), (down_s, down), (out_s, out)))
    ]
    for copy in copies:
        copy.start()
    for copy in copies:
        copy.wait()


def finish_feed(idx, layer, layers, pieces, before):
    filled = before is not None
    return kernel_call(
        functools.partial(finish_feed_body, layer, filled),
        [smem_spec()] + [vmem_spec()] * 8 + [any_spec()] * (3 * filled),
        [sds((layers, D, D), F32), sds((layers, D, D), F32), sds((layers, HEADS_COLS, D), F32)],
        [any_spec()] * 3,
        [
            pltpu.VMEM((D, D), F32),
            pltpu.VMEM((D, D), F32),
            pltpu.VMEM((HEADS_COLS, D), F32),
            pltpu.SemaphoreType.DMA((3,)),
        ],
        (idx, *pieces) + (tuple(before) if filled else ()),
        1e6,
        8e6,
        aliases={9: 0, 10: 1, 11: 2} if filled else None,
        name="finish_feed",
    )


def pack_body(idx, ups, downs, outs, *rest):
    targets, (zeros, sems) = rest[:-2], rest[-2:]
    zeros[...] = jnp.zeros_like(zeros)
    rows = rows_at(idx[0] * PIECE, PIECE, 32)
    cols = pl.ds(pl.multiple_of(idx[2] * 384, 128), 384)
    copies = []
    for layer, target in enumerate(targets):
        moves = [
            (ups.at[layer, rows], target.at[pl.ds(0, PIECE)]),
            (downs.at[layer, rows], target.at[pl.ds(PIECE, PIECE)]),
        ]
        for s in range(4):
            place = target.at[pl.ds(2 * PIECE + 16 * (s // 2), 16), pl.ds(384 * (s % 2), 384)]
            if s == 3:
                moves.append((zeros, place))
            else:
                moves.append((outs.at[layer, rows_at((idx[0] >> 1) * 48 + 16 * s, 16, 16), cols], place))
        for source, place in moves:
            copies.append(pltpu.make_async_copy(source, place, sems.at[len(copies)]))
    for copy in copies:
        copy.start()
    for copy in copies:
        copy.wait()


def pack(idx, ups, downs, outs):
    layers = ups.shape[0]
    return kernel_call(
        pack_body,
        [smem_spec()] + [any_spec()] * 3,
        [sds((PACK, D), BF)] * layers,
        [vmem_spec()] * layers,
        [pltpu.VMEM((16, 384), BF), pltpu.SemaphoreType.DMA((6 * layers,))],
        (idx, ups, downs, outs),
        1e6,
        1e6,
        name="pack",
    )


def flip_wide(x, bit):
    return lax.ppermute(x, "wide", [(i, i ^ bit) for i in range(lax.axis_size("wide"))])


def flip_narrow(x, bit):
    return lax.ppermute(x, "narrow", [(i, i ^ bit) for i in range(QUARTERS)])


def first_axis(x):
    return lax.ppermute(x, "wide", [(i, i ^ (4 if i & 1 else 2)) for i in range(lax.axis_size("wide"))])


def second_axis(x):
    return lax.ppermute(x, "wide", [(i, i ^ (2 if i & 1 else 4)) for i in range(lax.axis_size("wide"))])


def gate_body(*refs):
    return None


def gate(tree):
    leaves, shape = jax.tree.flatten(tree)
    out = pl.pallas_call(
        gate_body,
        in_specs=[any_spec() for _ in leaves],
        out_specs=[any_spec() for _ in leaves],
        out_shape=[sds(x.shape, x.dtype) for x in leaves],
        input_output_aliases={i: i for i in range(len(leaves))},
        name="gate",
    )(*leaves)
    return jax.tree.unflatten(shape, out)


def gather_direct(piece):
    return [piece] + [flip_narrow(piece, k) for k in ORDER[1:]]


def gather_far(piece):
    return piece, flip_narrow(piece, 2)


def gather_near(pair):
    pair = jnp.stack(pair)
    return pair, flip_narrow(pair, 1)


def whole(parts):
    return jnp.stack(parts) if parts[0].ndim == 2 else jnp.concatenate(parts)


def gather_first(own):
    return own, first_axis(own)


def gather_second(parts):
    own, first = parts
    return [own, first, second_axis(own), second_axis(first)]


def gather_last(here):
    return here + [flip_wide(x, 1) for x in here]


def added(*terms):
    return functools.reduce(jnp.add, [t.astype(F32) for t in terms]).astype(BF)


def reduce_core(pair):
    keep, send = pair
    return keep, flip_wide(send, 1)


def reduce_first_sums(pair):
    keep, got = pair
    return keep, got, added(keep[3], got[3]), added(keep[2], got[2])


def reduce_first(parts):
    keep, got, passed, stays = parts
    return keep, got, first_axis(passed), first_axis(stays)


def reduce_first_whole(pair):
    keep, got = pair
    return keep, got, first_axis(added(keep[2:], got[2:]))


def reduce_second(keep, got, passed):
    return second_axis(added(keep[1], got[1], passed))


def reduce_near(parts):
    total = added(parts[0][0], parts[1][0], *parts[2:])
    bit = 8
    while bit < lax.axis_size("wide"):
        total = added(total, flip_wide(total, bit))
        bit *= 2
    return total, flip_narrow(total[2:], 1)


def reduce_far(parts):
    total, near = parts
    return total, near, flip_narrow(added(total[1], near[1]), 2)


def both_axes(x):
    return flip_wide(x, 6)


def gather_plane(own):
    return [own, first_axis(own), second_axis(own), both_axes(own)]


def spread_first(parts):
    total, near, far = parts
    return gather_first(added(total[0], near[0], far))


def reduce_plane(pair):
    keep, got = pair
    moves = (second_axis, first_axis, both_axes)
    return [keep, got] + [move(added(keep[i + 1], got[i + 1])) for i, move in enumerate(moves)]


def reduce_narrow(parts):
    keep, got, *others = parts
    total = added(keep[0], got[0], *others)
    bit = 8
    while bit < lax.axis_size("wide"):
        total = added(total, flip_wide(total, bit))
        bit *= 2
    return [total] + [flip_narrow(total[i], ORDER[i]) for i in range(1, QUARTERS)]


def device_pairs(move):
    pairs = []
    for w in range(lax.axis_size("wide")):
        for z in range(QUARTERS):
            target = move(w, z)
            if target is not None:
                pairs.append((w * QUARTERS + z, target[0] * QUARTERS + target[1]))
    return pairs


BOTH = ("wide", "narrow")


def relocate_first(rows):
    pairs = device_pairs(lambda w, z: ((w & ~1) | (z >> 1), ((w & 1) << 1) | (z & 1)))
    return lax.ppermute(rows[:HALF], BOTH, pairs)


def relocate_second(rows):
    pairs = device_pairs(lambda w, z: ((w & ~1) | (z >> 1), ((w & 1) << 1) | (1 - (z & 1))))
    return lax.ppermute(rows[HALF:], BOTH, pairs)


def relocate(rows):
    return relocate_first(rows), relocate_second(rows)


def between_chips(x):
    pairs = device_pairs(lambda w, z: (w, z ^ 1) if w & 1 else None)
    return lax.ppermute(x, BOTH, pairs)


def within_chip(x, source):
    pairs = [(i, i ^ 1) for i in range(lax.axis_size("wide")) if (i & 1) == source]
    return lax.ppermute(x, "wide", pairs)


def per_device(
    tokens,
    block_size,
    norm_gain,
    norm_shift,
    mixer_weight,
    mixer_bias,
    output_weight,
    output_bias,
    up_weight,
    up_bias,
    down_weight,
    cotangent,
):
    layers = norm_gain.shape[0]
    w, z = lax.axis_index("wide"), lax.axis_index("narrow")
    w8, core, low = w & 7, w & 1, z & 1
    sizes = jnp.where((z >> 1) == core, block_size, flip_wide(block_size, 1))[0]
    level = 2 + (sizes >= 8).astype(jnp.int32) + (sizes >= 16).astype(jnp.int32)
    idx = jnp.stack([w8, z, core, low, level, w8, w8, w8]).astype(jnp.int32)

    bases = jnp.where(low == 0, jnp.array([0, 768]), jnp.array([512, 256]))
    position = (bases[:, None] + jnp.arange(HALF)[None, :]).reshape(ROWS).astype(F32)
    halfway = HEAD_DIM // 2
    frequency = jnp.exp(jnp.arange(halfway, dtype=F32) * (-math.log(10000.0) / halfway))
    angle = position[:, None] * frequency[None, :]
    cosine = jnp.tile(jnp.cos(angle), (1, 4))
    sine = jnp.sin(angle)
    sine = jnp.concatenate([-sine, sine, -sine, sine], axis=1)

    def bias_pieces(layer):
        return mixer_bias[layer].reshape(PARTS), up_bias[layer]

    biases = jnp.concatenate([t for layer in range(layers) for t in bias_pieces(layer)])
    width = PARTS + D

    def bias_of(layer, start, size):
        at = width * layer + start
        return jnp.stack([b[at : at + size] for b in biases])[:, None]

    def mixer_piece(layer):
        return lax.dynamic_slice_in_dim(mixer_weight[layer], w8 * PIECE, PIECE, 0).reshape(PIECE, PARTS)

    def run_project(layer, x, pieces):
        gain, shift = norm_gain[layer], norm_shift[layer]
        return project(idx, x, gain[0:1], shift[0:1], bias_of(layer, 0, PARTS), cosine, sine, pieces)

    def run_feed(layer, x, o, pieces):
        gain, shift, bias = norm_gain[layer], norm_shift[layer], output_bias[layer]
        return feed(
            idx, x, o, gain[1:2], shift[1:2], bias[0:1], bias[1:2], bias_of(layer, PARTS, D), pieces
        )

    mixer0 = gather_direct(mixer_piece(0))
    feed0, feed1 = pack(idx, up_weight, down_weight, output_weight)
    biases = [biases] + [flip_narrow(biases, k) for k in (1, 2, 3)]
    mixer0, tokens, feed0, biases = gate((mixer0, tokens, feed0, biases))
    mixer0 = gather_first(whole(mixer0))
    rows = relocate(tokens)
    mixer0, feed0 = gate((mixer0, feed0))
    own, first = mixer0
    mixer0 = [own, first, second_axis(own), second_axis(first)]
    feed0 = gather_far(feed0)
    mixer0, rows, feed0 = gate((mixer0, rows, feed0))
    mixer0 = gather_last(mixer0)
    feed0 = gather_near(feed0)
    x0 = jnp.concatenate(rows).astype(F32)
    h1_0, q_0, kv = run_project(0, x0, mixer0)
    own_0, feed0 = gate((kv, feed0))
    near_0, far = within_chip(own_0, 1), between_chips(own_0)
    own, first = gather_first(whole(feed0))
    mixer1 = mixer_piece(1)
    state = attend_near(idx, q_0, own_0, near_0)
    state, far_0, own, first, mixer1, feed1 = gate((state, far, own, first, mixer1, feed1))
    far_near_0 = within_chip(far_0, 1)
    second = second_axis(own)
    mixer1 = gather_direct(mixer1)
    o_0, lse_0 = attend_far(idx, q_0, far_0, far_near_0, state)
    o_0, own, first, second, mixer1, feed1 = gate((o_0, own, first, second, mixer1, feed1))
    third = second_axis(first)
    others = [flip_wide(own, 1), flip_wide(first, 1), flip_wide(second, 1)]
    feed1 = gather_far(feed1)
    third, others, o_0, mixer1, feed1 = gate((third, others, o_0, mixer1, feed1))
    feed0 = [own, first, second, third] + others + [flip_wide(third, 1)]
    mixer1, feed1 = gather_plane(whole(mixer1)), gather_near(feed1)
    x1, x1_0, h2_0, g_0, gp_0 = run_feed(0, x0, o_0, feed0)
    x1, mixer1, feed1 = gate((x1, mixer1, feed1))
    mixer1 = gather_last(mixer1)
    own, first = gather_first(whole(feed1))
    h1_1, q_1, kv = run_project(1, x1, mixer1)
    own_1, own, first = gate((kv, own, first))
    near_1, far = within_chip(own_1, 1), between_chips(own_1)
    second = second_axis(own)
    state = attend_near(idx, q_1, own_1, near_1)
    state, far_1, own, first, second = gate((state, far, own, first, second))
    far_near_1 = within_chip(far_1, 1)
    third = second_axis(first)
    others = [flip_wide(own, 1), flip_wide(first, 1), flip_wide(second, 1)]
    o_1, lse_1 = attend_far(idx, q_1, far_1, far_near_1, state)
    o_1, third, others, cotangent = gate((o_1, third, others, cotangent))
    e = relocate(cotangent)
    feed1 = [own, first, second, third] + others + [flip_wide(third, 1)]
    x2, x1_1, h2_1, g_1, gp_1 = run_feed(1, x1, o_1, feed1)
    x2, e = gate((x2, e))
    x_out = relocate(x2.astype(BF))

    e = jnp.concatenate(e).astype(F32)
    dm, dz, e1, da, do, small_feed1 = feed_back(idx, e, x1_1, gp_1, norm_gain[1, 1:2], feed1)
    g_feed1 = feed_grads(idx, g_1, dm, h2_1, dz, o_1, da)
    do, x_out, g_feed1 = gate((do, x_out, g_feed1))
    g_feed1 = reduce_core(g_feed1)
    dq, dr, drow = attend_back_far(idx, q_1, do, o_1, lse_1, far_1, far_near_1)
    dr, dq, g_feed1 = gate((dr, dq, g_feed1))
    dr, got, dq, g_feed1 = gate((dr, within_chip(dr, 0), dq, reduce_first_sums(g_feed1)))
    far = between_chips(added(dr, got))
    g_feed1 = reduce_first(g_feed1)
    dq, dn, dc = attend_back_near(idx, q_1, do, lse_1, drow, dq, own_1, near_1)
    keep, gained, passed, stays = g_feed1
    dc, far, keep, gained, passed = gate((dc, far, keep, gained, passed))
    got = within_chip(dc, 0)
    g_feed1 = keep, gained, stays, reduce_second(keep, gained, passed)
    dpz, e, small_mixer1 = project_back(
        idx, dq, dn, dc, got, far, cosine, sine, x1, e1, norm_gain[1, 0:1], mixer1
    )
    dpz, e, g_feed1 = gate((dpz, e, g_feed1))
    g_feed1 = reduce_near(g_feed1)
    g_mixer1 = project_grads(idx, h1_1, dpz)
    e, g_mixer1 = gate((e, g_mixer1))
    g_mixer1 = reduce_core(g_mixer1)
    dm, dz, e1, da, do, small_feed0 = feed_back(idx, e, x1_0, gp_0, norm_gain[0, 1:2], feed0)
    dm, do, g_feed1, g_mixer1 = gate((dm, do, g_feed1, g_mixer1))
    g_feed1, g_mixer1 = reduce_far(g_feed1), reduce_first_whole(g_mixer1)
    g_feed0 = feed_grads(idx, g_0, dm, h2_0, dz, o_0, da)
    do, g_feed1, g_mixer1, g_feed0 = gate((do, g_feed1, g_mixer1, g_feed0))
    keep1, gained1, both1 = g_mixer1
    second1, g_feed0 = reduce_second(keep1, gained1, both1[1]), reduce_core(g_feed0)
    g_feed1 = spread_first(g_feed1)
    dq, dr, drow = attend_back_far(idx, q_0, do, o_0, lse_0, far_0, far_near_0)
    dr, dq, g_feed1, second1, g_feed0 = gate((dr, dq, g_feed1, second1, g_feed0))
    dr, got, dq, g_feed0, g_feed1 = gate((dr, within_chip(dr, 0), dq, reduce_first_sums(g_feed0), g_feed1))
    far = between_chips(added(dr, got))
    g_feed0, g_feed1 = reduce_first(g_feed0), gather_second(g_feed1)
    dq, dn, dc = attend_back_near(idx, q_0, do, lse_0, drow, dq, own_0, near_0)
    keep, gained, passed, stays = g_feed0
    dc, far, keep, gained, passed, g_feed1 = gate((dc, far, keep, gained, passed, g_feed1))
    got = within_chip(dc, 0)
    g_feed0 = keep, gained, stays, reduce_second(keep, gained, passed)
    g_mixer1 = reduce_near((keep1, gained1, both1[0], second1))
    dpz, e, small_mixer0 = project_back(
        idx, dq, dn, dc, got, far, cosine, sine, x0, e1, norm_gain[0, 0:1], mixer0
    )
    e, dpz, g_feed0, g_mixer1 = gate((e, dpz, g_feed0, g_mixer1))
    g_feed0, g_mixer1 = reduce_near(g_feed0), reduce_far(g_mixer1)
    g_mixer0 = reduce_core(project_grads(idx, h1_0, dpz))
    smalls = jnp.concatenate([small_feed0, small_mixer0, small_feed1, small_mixer1])
    g_feed1 = gather_last(g_feed1)
    smalls = smalls, flip_wide(smalls, 1)
    g_mixer0, smalls, e, g_feed1, g_mixer1 = gate((g_mixer0, smalls, e, g_feed1, g_mixer1))
    g_mixer0 = reduce_plane(g_mixer0)
    early, e_late = relocate_first(e.astype(BF)), e
    feed_out = finish_feed(idx, 1, layers, g_feed1, None)
    g_mixer0, g_feed0, smalls, feed_out, early, e_late, g_mixer1 = gate(
        (g_mixer0, g_feed0, smalls, feed_out, early, e_late, g_mixer1)
    )
    keep, gained, *others = g_mixer0
    total = added(keep[0], gained[0], *others)
    bit = 8
    while bit < lax.axis_size("wide"):
        total = added(total, flip_wide(total, bit))
        bit *= 2
    g_mixer0 = total, flip_narrow(total[2:], 1)
    g_feed0 = reduce_far(g_feed0)
    smalls = smalls[0] + smalls[1]
    smalls = smalls, first_axis(smalls)
    g_mixer1 = spread_first(g_mixer1)
    g_mixer0, g_feed0, smalls, g_mixer1 = gate((g_mixer0, g_feed0, smalls, g_mixer1))
    g_mixer0, g_feed0 = reduce_far(g_mixer0), spread_first(g_feed0)
    smalls = smalls[0] + smalls[1]
    smalls = smalls, second_axis(smalls)
    g_mixer1 = gather_second(g_mixer1)
    g_mixer0, g_feed0, smalls, g_mixer1 = gate((g_mixer0, g_feed0, smalls, g_mixer1))
    g_mixer0, g_feed0 = spread_first(g_mixer0), gather_second(g_feed0)
    smalls = smalls[0] + smalls[1]
    bit = 8
    while bit < lax.axis_size("wide"):
        smalls = smalls + flip_wide(smalls, bit)
        bit *= 2
    smalls = smalls, flip_narrow(smalls, 1)
    g_mixer1 = gather_last(g_mixer1)
    mixer_out = finish_mixer(idx, 1, layers, g_mixer1, None)
    g_mixer0, g_feed0, smalls, e_late, mixer_out = gate((g_mixer0, g_feed0, smalls, e_late, mixer_out))
    g_mixer0, g_feed0 = gather_second(g_mixer0), gather_last(g_feed0)
    late = relocate_second(e_late.astype(BF))
    smalls = smalls[0] + smalls[1]
    smalls = smalls, flip_narrow(smalls, 2)
    feed_out = finish_feed(idx, 0, layers, g_feed0, feed_out)
    g_mixer0, smalls, late, feed_out = gate((g_mixer0, smalls, late, feed_out))
    smalls = smalls[0] + smalls[1]
    g_mixer0 = gather_last(g_mixer0)
    mixer_out = finish_mixer(idx, 0, layers, g_mixer0, mixer_out)
    tokens_grad = jnp.concatenate([early, late])
    x_out = jnp.concatenate(x_out)

    small = smalls.reshape(layers, 16, D)
    up_bias_grad = lax.dynamic_index_in_dim(small[:, 0:4], z, 1, keepdims=False)
    mixer_bias_grad = lax.dynamic_index_in_dim(small[:, 8:12, :PARTS], z, 1, keepdims=False)
    return (
        x_out,
        tokens_grad,
        jnp.stack([small[:, 12], small[:, 6]], axis=1),
        jnp.stack([small[:, 13], small[:, 7]], axis=1),
        mixer_out.reshape(layers, D, 3, HEADS_COLS),
        mixer_bias_grad.reshape(layers, 3, HEADS_COLS),
        feed_out[2],
        jnp.stack([small[:, 5], small[:, 4]], axis=1),
        feed_out[0],
        up_bias_grad,
        feed_out[1],
    )


def solution(mesh):
    rows = P(("wide", "narrow"), None)
    quarters = (
        P(None, None, None, "narrow"),
        P(None, None, "narrow"),
        P(None, "narrow", None),
        P(),
        P(None, None, "narrow"),
        P(None, "narrow"),
        P(None, "narrow", None),
    )
    return jax.shard_map(
        per_device,
        mesh=mesh,
        in_specs=(rows, P("wide"), P(), P()) + quarters + (rows,),
        out_specs=(rows, rows, P(), P()) + quarters,
        check_vma=False,
    )
```

```python
import functools
import math

import jax
import jax.numpy as jnp
from jax import lax
from jax.experimental import pallas as pl
from jax.experimental.pallas import tpu as pltpu
from jax.sharding import PartitionSpec as P

HEAD_DIM = 64
LEN = 1024
EPSILON = 1e-05
D = 768
QUARTERS = 4
HALF = 256
ROWS = 512
PIECE = 96
HEADS_COLS = 192
PARTS = 576
PACK = 224
MASKED = -1e30
BF = jnp.bfloat16
F32 = jnp.float32
NT = (((1,), (1,)), ((), ()))
TN = (((0,), (0,)), ((), ()))
VMEM_LIMIT = 56 * 1024 * 1024


def dot(a, b):
    return jnp.dot(a, b, preferred_element_type=F32)


def dot_nt(a, b):
    return lax.dot_general(a, b, NT, preferred_element_type=F32)


def dot_tn(a, b):
    return lax.dot_general(a, b, TN, preferred_element_type=F32)


def norm_parts(values):
    center = values - jnp.mean(values, axis=-1, keepdims=True)
    inverse = lax.rsqrt(jnp.mean(center * center, axis=-1, keepdims=True) + EPSILON)
    return center * inverse, inverse


def norm_backward(grad_in, unit_rows, inverse, gain):
    scaled = grad_in * gain
    return inverse * (
        scaled
        - jnp.mean(scaled, axis=-1, keepdims=True)
        - unit_rows * jnp.mean(scaled * unit_rows, axis=-1, keepdims=True)
    )


def swap_halves(u):
    lane = lax.broadcasted_iota(jnp.int32, u.shape, 1)
    return jnp.where((lane & 63) < 32, pltpu.roll(u, 96, axis=1), pltpu.roll(u, 32, axis=1))


def rot(u, cosine, sine):
    return u * cosine + swap_halves(u) * sine


def unrot(u, cosine, sine):
    return u * cosine - swap_halves(u) * sine


ORDER = (0, 2, 1, 3)


def flips(idx):
    first, second = 2 + 2 * idx[2], 4 - 2 * idx[2]
    return [0, first, second, 6, 1, 1 ^ second, 1 ^ first, 7]


def piece_copies(refs, idx, sems, place):
    copies = []
    for flip, ref in zip(flips(idx), refs):
        for at, k in enumerate(ORDER):
            for source, target in place(ref.at[at], k, idx[1] ^ k, idx[0] ^ flip):
                copies.append(pltpu.make_async_copy(source, target, sems.at[len(copies)]))
    return copies


def rows_at(start, size, unit):
    return pl.ds(pl.multiple_of(start, unit), size)


def mixer_copies(refs, idx, sems, weights):
    def place(src, k, zq, wq):
        return [(src, weights.at[zq, rows_at(wq * PIECE, PIECE, 32)])]

    return piece_copies(refs, idx, sems, place)


def up_down_copies(refs, idx, sems, ups, downs):
    def place(src, k, zq, wq):
        rows = rows_at(wq * PIECE, PIECE, 32)
        return [
            (src.at[pl.ds(0, PIECE)], ups.at[k, rows]),
            (src.at[pl.ds(PIECE, PIECE)], downs.at[k, rows]),
        ]

    return piece_copies(refs, idx, sems, place)


def packed_copies(refs, idx, sems, packed):
    def place(src, k, zq, wq):
        return [(src.at[pl.ds(2 * PIECE, 32)], packed.at[zq, wq])]

    return piece_copies(refs, idx, sems, place)


def unpack_output(packed, weights):
    for zq in range(QUARTERS):
        for chip in range(4):
            for part in range(2):
                for s in range(3):
                    row = HEADS_COLS * zq + 48 * chip + 16 * s
                    weights[row : row + 16, 384 * part : 384 * part + 384] = packed[
                        zq, 2 * chip + part, 16 * (s // 2) : 16 * (s // 2) + 16, 384 * (s % 2) : 384 * (s % 2) + 384
                    ]


def any_spec():
    return pl.BlockSpec(memory_space=pl.ANY)


def vmem_spec():
    return pl.BlockSpec(memory_space=pltpu.VMEM)


def smem_spec():
    return pl.BlockSpec(memory_space=pltpu.SMEM)


def kernel_call(body, in_specs, out_shape, out_specs, scratch, args, flops, moved, aliases=None, name=None):
    return pl.pallas_call(
        body,
        in_specs=in_specs,
        out_specs=out_specs,
        out_shape=out_shape,
        scratch_shapes=scratch,
        input_output_aliases=aliases or {},
        compiler_params=pltpu.CompilerParams(vmem_limit_bytes=VMEM_LIMIT),
        cost_estimate=pl.CostEstimate(flops=1000, bytes_accessed=1000, transcendentals=0),
        name=name,
    )(*args)


def sds(shape, dtype):
    return jax.ShapeDtypeStruct(shape, dtype)


def project_body(idx, x, gain, shift, bias, cosine, sine, *rest):
    pieces, (h1, q, kv, weights, wide, sems) = rest[:8], rest[8:]
    copies = mixer_copies(pieces, idx, sems, weights)
    for copy in copies:
        copy.start()

    def norm_rows(i, carry):
        rows = rows_at(i * 128, 128, 128)
        unit, _ = norm_parts(x[rows])
        h1[rows] = (unit * gain[...] + shift[...]).astype(BF)
        return carry

    lax.fori_loop(0, 4, norm_rows, 0)
    for copy in copies:
        copy.wait()
    for zq in range(QUARTERS):
        p = dot(h1[...], weights[zq]) + bias[idx[1] ^ zq]
        for part in range(3):
            col = D * part + HEADS_COLS * zq
            wide[:, col : col + HEADS_COLS] = p[:, HEADS_COLS * part : HEADS_COLS * (part + 1)]
    for half in range(2):
        rows = slice(HALF * half, HALF * (half + 1))
        for j in range(6):
            cols = slice(128 * j, 128 * (j + 1))
            q[rows, cols] = (rot(wide[rows, cols], cosine[rows], sine[rows]) * 0.125).astype(BF)
            kcols = slice(D + 128 * j, D + 128 * (j + 1))
            kv[rows, cols] = rot(wide[rows, kcols], cosine[rows], sine[rows]).astype(BF)
        kv[rows, D:] = wide[rows, 2 * D :].astype(BF)


def project(idx, x, gain, shift, bias, cosine, sine, pieces):
    return kernel_call(
        project_body,
        [smem_spec()] + [vmem_spec()] * 6 + [any_spec()] * 8,
        [sds((ROWS, D), BF), sds((ROWS, D), BF), sds((ROWS, 2 * D), BF)],
        [vmem_spec()] * 3,
        [
            pltpu.VMEM((QUARTERS, D, PARTS), BF),
            pltpu.VMEM((ROWS, 3 * D), F32),
            pltpu.SemaphoreType.DMA((32,)),
        ],
        (idx, x, gain, shift, bias, cosine, sine, *pieces),
        2 * ROWS * D * 3 * D,
        8e6,
        name="project",
    )


def load_near(idx, own, near, kvn, kvc, sems):
    clean = idx[2] == 1
    copy = pltpu.make_async_copy(own, kvn, sems.at[0])
    copy.start()
    a = pltpu.make_async_copy(own, kvc, sems.at[1])
    b = pltpu.make_async_copy(near, kvc, sems.at[1])
    pl.when(clean)(a.start)
    pl.when(jnp.logical_not(clean))(b.start)
    return [copy, a]


def load_far(idx, far, far_near, kvr, sem):
    clean = idx[2] == 1
    a = pltpu.make_async_copy(far, kvr, sem)
    b = pltpu.make_async_copy(far_near, kvr, sem)
    pl.when(clean)(a.start)
    pl.when(jnp.logical_not(clean))(b.start)
    return a


NEAR_TILES = {0: [(0, [(0, True)]), (1, [(1, True), (0, False)])], 1: [(1, [(1, True)]), (0, [(0, True), (1, False)])]}
FAR_TILES = {0: [(1, [0, 1])], 1: [(1, [0]), (0, [0])]}


def set_masks(idx, bias, bias_n, query_dim):
    clean, level = idx[2], idx[4]
    qi = lax.shift_right_logical(lax.broadcasted_iota(jnp.int32, (HALF, HALF), query_dim), level)
    ki = lax.shift_right_logical(lax.broadcasted_iota(jnp.int32, (HALF, HALF), 1 - query_dim), level)
    allowed = jnp.where(ki < qi + clean, 0.0, MASKED)
    bias[...] = jnp.concatenate([allowed, allowed], axis=query_dim)
    same = (jnp.where(ki == qi, 0, 1) + clean)[:128, :128]
    own = jnp.where(same == 0, 0.0, MASKED)
    bias_n[...] = jnp.concatenate([own, own], axis=query_dim)


def lanes(rows):
    return lax.broadcasted_iota(jnp.int32, (rows, 128), 1)


def one_head(v, side):
    low_lane = lanes(v.shape[0]) < 64
    return jnp.where(low_lane if side == 0 else jnp.logical_not(low_lane), v, jnp.zeros_like(v))


def both_heads(v):
    return jnp.concatenate([one_head(v, 0), one_head(v, 1)], axis=0)


def pair_lanes(v):
    n = v.shape[0] // 2
    return jnp.where(lanes(n) < 64, v[:n], v[n:])


def pair_cols(hp):
    off = pl.multiple_of(hp * 128, 128)
    return pl.ds(off, 128), pl.ds(pl.multiple_of(D + off, 128), 128)


def row_max(s):
    return jnp.max(s, axis=-1, keepdims=True)


def with_ones(v):
    return jnp.concatenate([v, jnp.ones_like(v)], axis=1)


def half_rows(half):
    return slice(HALF * half, HALF * (half + 1))


def attend_near_body(idx, q, own, near, acc, tops, counts, kvn, kvc, bias, bias_n, sems):
    waits = load_near(idx, own, near, kvn, kvc, sems)
    set_masks(idx, bias, bias_n, 0)
    tops[...] = jnp.zeros_like(tops)
    counts[...] = jnp.ones_like(counts)
    for copy in waits:
        copy.wait()

    def run(tiles):
        def pair(hp, carry):
            cols, vcols = pair_cols(hp)
            lane = lanes(HALF)
            for half, sources in tiles:
                rows = half_rows(half)
                qs = both_heads(q[rows, cols])
                scores = []
                for kh, diagonal in sources:
                    s = dot_nt(qs, kvc[half_rows(kh), cols])
                    scores.append(s + bias[...] if diagonal else s)
                blocks = [slice(HALF * half + 128 * t, HALF * half + 128 * (t + 1)) for t in range(2)]

                def of_block(v, t):
                    return jnp.concatenate([v[128 * t : 128 * (t + 1)], v[HALF + 128 * t : HALF + 128 * (t + 1)]], axis=0)

                def of_heads(a, b):
                    return jnp.concatenate([a[:128], b[:128], a[128:], b[128:]], axis=0)

                mine = [dot_nt(of_block(qs, t), kvn[blocks[t], cols]) + bias_n[...] for t in range(2)]
                top = of_heads(*[row_max(s) for s in mine])
                for s in scores:
                    top = jnp.maximum(top, row_max(s))
                total = of_heads(
                    *[
                        dot(jnp.exp(mine[t] - of_block(top, t)).astype(BF), with_ones(kvn[blocks[t], vcols]))
                        for t in range(2)
                    ]
                )
                for s, (kh, diagonal) in zip(scores, sources):
                    total = total + dot(jnp.exp(s - top).astype(BF), with_ones(kvc[half_rows(kh), vcols]))
                acc[rows, cols] = pair_lanes(total[:, :128])
                for target, value in ((tops, top), (counts, total[:, 128:])):
                    target[rows] = jnp.where(
                        lane == 2 * hp, value[:HALF], jnp.where(lane == 2 * hp + 1, value[HALF:], target[rows])
                    )
            return carry

        lax.fori_loop(0, 6, pair, 0)

    for zl in range(2):
        pl.when(idx[3] == zl)(functools.partial(run, NEAR_TILES[zl]))


def attend_near(idx, q, own, near):
    return kernel_call(
        attend_near_body,
        [smem_spec(), vmem_spec()] + [any_spec()] * 2,
        [sds((ROWS, D), F32), sds((ROWS, 128), F32), sds((ROWS, 128), F32)],
        [vmem_spec()] * 3,
        [
            pltpu.VMEM((ROWS, 2 * D), BF),
            pltpu.VMEM((ROWS, 2 * D), BF),
            pltpu.VMEM((2 * HALF, HALF), F32),
            pltpu.VMEM((HALF, 128), F32),
            pltpu.SemaphoreType.DMA((2,)),
        ],
        (idx, q, own, near),
        8e9,
        6e6,
        name="attend_near",
    )


def attend_far_body(idx, q, far, far_near, acc, tops, counts, o, lse, kvr, last, sem):
    copy = load_far(idx, far, far_near, kvr, sem)
    last[...] = tops[...] + jnp.log(counts[...])
    copy.wait()

    def column(values, head):
        return jnp.sum(jnp.where(lanes(HALF) == head, values, 0.0), axis=-1, keepdims=True)

    def run(tiles):
        covered = [half for half, _ in tiles]

        def pair(hp, carry):
            cols, vcols = pair_cols(hp)
            lane = lanes(HALF)
            for half in range(2):
                rows = half_rows(half)
                if half in covered:
                    sources = dict(tiles)[half]
                    q2 = q[rows, cols]
                    sides = []
                    for side in range(2):
                        qm = one_head(q2, side)
                        scores = [dot_nt(qm, kvr[half_rows(kh), cols]) for kh in sources]
                        before = column(tops[rows], 2 * hp + side)
                        top = before
                        for s in scores:
                            top = jnp.maximum(top, row_max(s))
                        shrink = jnp.exp(before - top)
                        total = None
                        for s, kh in zip(scores, sources):
                            part = dot(jnp.exp(s - top).astype(BF), with_ones(kvr[half_rows(kh), vcols]))
                            total = part if total is None else total + part
                        count = column(counts[rows], 2 * hp + side) * shrink + total[:, 128:]
                        value = (acc[rows, cols] * shrink + total[:, :128]) / count
                        sides.append((value, top + jnp.log(count)))
                    last[rows] = jnp.where(
                        lane == 2 * hp, sides[0][1], jnp.where(lane == 2 * hp + 1, sides[1][1], last[rows])
                    )
                else:
                    sides = [(acc[rows, cols] / column(counts[rows], 2 * hp + side),) for side in range(2)]
                o[rows, cols] = jnp.where(lane < 64, sides[0][0], sides[1][0]).astype(BF)
            return carry

        lax.fori_loop(0, 6, pair, 0)

    for zl in range(2):
        pl.when(idx[3] == zl)(functools.partial(run, FAR_TILES[zl]))
    across = jnp.transpose(last[...])
    for head in range(12):
        lse[head] = across[head : head + 1]


def attend_far(idx, q, far, far_near, state):
    return kernel_call(
        attend_far_body,
        [smem_spec(), vmem_spec()] + [any_spec()] * 2 + [vmem_spec()] * 3,
        [sds((ROWS, D), BF), sds((12, 1, ROWS), F32)],
        [vmem_spec()] * 2,
        [
            pltpu.VMEM((ROWS, 2 * D), BF),
            pltpu.VMEM((ROWS, 128), F32),
            pltpu.SemaphoreType.DMA,
        ],
        (idx, q, far, far_near, *state),
        5e9,
        6e6,
        name="attend_far",
    )


def feed_body(idx, x, o, gain, shift, out_bias, down_bias, up_bias, *rest):
    pieces, (x2, x1, h2, g, gp, ups, downs, packed, outw, sems, sems_o) = rest[:8], rest[8:]
    first = packed_copies(pieces, idx, sems_o, packed)
    later = up_down_copies(pieces, idx, sems, ups, downs)
    for copy in first + later:
        copy.start()
    for copy in first:
        copy.wait()
    unpack_output(packed, outw)
    x1[...] = x[...] + (dot(o[...], outw[...]) + out_bias[...])

    def norm_rows(i, carry):
        rows = rows_at(i * 128, 128, 128)
        unit, _ = norm_parts(x1[rows])
        h2[rows] = (unit * gain[...] + shift[...]).astype(BF)
        x2[rows] = x1[rows] + down_bias[...]
        return carry

    lax.fori_loop(0, 4, norm_rows, 0)
    for copy in later:
        copy.wait()

    def hidden(k, carry):
        for n in range(3):
            cols = slice(256 * n, 256 * (n + 1))
            u = dot(h2[...], ups[k, :, cols]) + up_bias[k, :, cols]
            uu = u * u
            t = jnp.tanh(0.7978845608028654 * u * (1.0 + 0.044715 * uu))
            half_t = 0.5 + 0.5 * t
            g[k, :, cols] = (u * half_t).astype(BF)
            slope = half_t + (0.5 * 0.7978845608028654) * u * (1.0 - t * t) * (1.0 + 0.134145 * uu)
            gp[k, :, cols] = slope.astype(BF)
        x2[...] += dot(g[k], downs[k])
        return carry

    lax.fori_loop(0, QUARTERS, hidden, 0)


WEIGHT_SCRATCH = [
    ((QUARTERS, D, D), BF),
    ((QUARTERS, D, D), BF),
    ((QUARTERS, 8, 32, D), BF),
    ((D, D), BF),
]


def feed(idx, x, o, gain, shift, out_bias, down_bias, up_bias, pieces):
    return kernel_call(
        feed_body,
        [smem_spec()] + [vmem_spec()] * 7 + [any_spec()] * 8,
        [
            sds((ROWS, D), F32),
            sds((ROWS, D), F32),
            sds((ROWS, D), BF),
            sds((QUARTERS, ROWS, D), BF),
            sds((QUARTERS, ROWS, D), BF),
        ],
        [vmem_spec()] * 5,
        [pltpu.VMEM(s, t) for s, t in WEIGHT_SCRATCH]
        + [pltpu.SemaphoreType.DMA((64,)), pltpu.SemaphoreType.DMA((32,))],
        (idx, x, o, gain, shift, out_bias, down_bias, up_bias, *pieces),
        2 * ROWS * D * D * 9,
        25e6,
        name="feed",
    )


def feed_back_body(idx, e, x1, gp, gain, *rest):
    pieces, (dm, dz, e1, da, do, small, ups, downs, packed, outw, dh2, hidden_sums, sems, sems_o) = rest[:8], rest[8:]
    first = packed_copies(pieces, idx, sems_o, packed)
    later = up_down_copies(pieces, idx, sems, ups, downs)
    for copy in later + first:
        copy.start()
    dm[...] = e[...].astype(BF)
    small[4:5] = jnp.sum(dm[...].astype(F32), axis=0, keepdims=True)
    dh2[...] = jnp.zeros_like(dh2)
    for copy in later:
        copy.wait()

    def hidden(k, carry):
        zq = idx[1] ^ k
        for n in range(3):
            cols = slice(256 * n, 256 * (n + 1))
            part = (dot_nt(dm[...], downs[k, cols]) * gp[k, :, cols].astype(F32)).astype(BF)
            dz[k, :, cols] = part
            hidden_sums[zq, :, cols] = jnp.sum(part.astype(F32), axis=0, keepdims=True)
        dh2[...] += dot_nt(dz[k], ups[k])
        return carry

    lax.fori_loop(0, QUARTERS, hidden, 0)
    for copy in first:
        copy.wait()
    unpack_output(packed, outw)
    for zq in range(QUARTERS):
        small[zq : zq + 1] = hidden_sums[zq]
    small[5:8] = jnp.zeros((3, D), F32)

    def norm_rows(i, carry):
        rows = rows_at(i * 128, 128, 128)
        unit, inverse = norm_parts(x1[rows])
        grad = dh2[rows]
        up = e[rows] + norm_backward(grad, unit, inverse, gain[...])
        e1[rows] = up
        low = up.astype(BF)
        da[rows] = low
        small[5:6] += jnp.sum(low.astype(F32), axis=0, keepdims=True)
        small[6:7] += jnp.sum(grad * unit, axis=0, keepdims=True)
        small[7:8] += jnp.sum(grad, axis=0, keepdims=True)
        return carry

    lax.fori_loop(0, 4, norm_rows, 0)
    do[...] = dot_nt(da[...], outw[...]).astype(BF)


def feed_back(idx, e, x1, gp, gain, pieces):
    return kernel_call(
        feed_back_body,
        [smem_spec()] + [vmem_spec()] * 4 + [any_spec()] * 8,
        [
            sds((ROWS, D), BF),
            sds((QUARTERS, ROWS, D), BF),
            sds((ROWS, D), F32),
            sds((ROWS, D), BF),
            sds((ROWS, D), BF),
            sds((8, D), F32),
        ],
        [vmem_spec()] * 6,
        [pltpu.VMEM(s, t) for s, t in WEIGHT_SCRATCH]
        + [pltpu.VMEM((ROWS, D), F32), pltpu.VMEM((QUARTERS, 1, D), F32), pltpu.SemaphoreType.DMA((64,)), pltpu.SemaphoreType.DMA((32,))],
        (idx, e, x1, gp, gain, *pieces),
        2 * ROWS * D * D * 9,
        25e6,
        name="feed_back",
    )


def spread(idx, keep, send, source, k, wq, rows, sem):
    w8, mine = idx[0], idx[2]
    j = (wq >> 1) ^ (w8 >> 1)
    turned = ((j & 1) << 1) | (j >> 1)
    at = ((k & 1) << 1) | (k >> 1)
    here, there = jnp.where(mine == 1, j, turned), jnp.where(mine == 1, turned, j)
    a = pltpu.make_async_copy(source, keep.at[here, at, rows], sem)
    b = pltpu.make_async_copy(source, send.at[there, at, rows], sem)
    pl.when((wq & 1) == mine)(a.start)
    pl.when((wq & 1) != mine)(b.start)
    return a


def feed_grads_body(idx, g, dm, h2, dz, o, da, keep, send, flipped, turned, d_up, d_down, d_out, sems):
    waits = []
    flipped[...] = jnp.transpose(o[...])
    turned[...] = dot(flipped[...], da[...]).astype(BF)
    for zq in range(QUARTERS):
        for chip in range(4):
            for part in range(2):
                for s in range(4):
                    rows, cols = slice(16 * (s // 2), 16 * (s // 2) + 16), slice(384 * (s % 2), 384 * (s % 2) + 384)
                    if s == 3:
                        block = jnp.zeros((16, 384), BF)
                    else:
                        row = HEADS_COLS * zq + 48 * chip + 16 * s
                        block = turned[row : row + 16, 384 * part : 384 * part + 384]
                    d_out[zq, 2 * chip + part, rows, cols] = block
    for zq in range(QUARTERS):
        k = idx[1] ^ zq
        for wq in range(8):
            sem = sems.at[len(waits)]
            waits.append(spread(idx, keep, send, d_out.at[zq, wq], k, wq, pl.ds(2 * PIECE, 32), sem))
    for k in range(QUARTERS):
        flipped[...] = jnp.transpose(g[k])
        d_down[k] = dot(flipped[...], dm[...]).astype(BF)
        for wq in range(8):
            sem = sems.at[len(waits)]
            source = d_down.at[k, pl.ds(PIECE * wq, PIECE)]
            waits.append(spread(idx, keep, send, source, k, wq, pl.ds(PIECE, PIECE), sem))
    flipped[...] = jnp.transpose(h2[...])
    for k in range(QUARTERS):
        d_up[k] = dot(flipped[...], dz[k]).astype(BF)
        for wq in range(8):
            sem = sems.at[len(waits)]
            source = d_up.at[k, pl.ds(PIECE * wq, PIECE)]
            waits.append(spread(idx, keep, send, source, k, wq, pl.ds(0, PIECE), sem))
    for copy in waits:
        copy.wait()


def feed_grads(idx, g, dm, h2, dz, o, da):
    return kernel_call(
        feed_grads_body,
        [smem_spec()] + [vmem_spec()] * 6,
        [sds((4, QUARTERS, PACK, D), BF)] * 2,
        [any_spec()] * 2,
        [
            pltpu.VMEM((D, ROWS), BF),
            pltpu.VMEM((D, D), BF),
            pltpu.VMEM((QUARTERS, D, D), BF),
            pltpu.VMEM((QUARTERS, D, D), BF),
            pltpu.VMEM((QUARTERS, 8, 32, D), BF),
            pltpu.SemaphoreType.DMA((96,)),
        ],
        (idx, g, dm, h2, dz, o, da),
        2 * ROWS * D * D * 9,
        25e6,
        name="feed_grads",
    )


def back_tile(q, do, lse, drow, cols, hp, k2, v2, qrow, n, bias_here):
    qs, gs = both_heads(q[qrow : qrow + n, cols]), both_heads(do[qrow : qrow + n, cols])

    def of_heads(ref):
        return jnp.concatenate([ref[2 * hp + side, :, qrow : qrow + n] for side in range(2)], axis=1)

    s = dot_nt(k2, qs)
    if bias_here is not None:
        s = s + bias_here
    p = jnp.exp(s - of_heads(lse))
    ds = (p * (dot_nt(v2, gs) - of_heads(drow))).astype(BF)
    return dot(ds, qs), dot(p.astype(BF), gs), pair_lanes(dot_tn(ds, k2))


def attend_back_far_body(idx, q, do, o, lse, far, far_near, dq, dr, drow, kvr, dcol, sem):
    copy = load_far(idx, far, far_near, kvr, sem)
    dcol[...] = jnp.zeros_like(dcol)

    def products(hp, carry):
        cols, _ = pair_cols(hp)
        lane = lanes(ROWS)
        both = do[:, cols].astype(F32) * o[:, cols].astype(F32)
        first = jnp.sum(jnp.where(lane < 64, both, 0.0), axis=-1, keepdims=True)
        second = jnp.sum(jnp.where(lane < 64, 0.0, both), axis=-1, keepdims=True)
        dcol[...] = jnp.where(lane == 2 * hp, first, jnp.where(lane == 2 * hp + 1, second, dcol[...]))
        return carry

    lax.fori_loop(0, 6, products, 0)
    across = jnp.transpose(dcol[...])
    for head in range(12):
        drow[head] = across[head : head + 1]
    copy.wait()

    def run(tiles):
        def pair(hp, carry):
            cols, vcols = pair_cols(hp)
            dq_half = [None, None]
            for kh in range(2):
                keys = half_rows(kh)
                total = None
                for half, sources in tiles:
                    if kh in sources:
                        parts = back_tile(
                            q, do, lse, drow, cols, hp, kvr[keys, cols], kvr[keys, vcols], HALF * half, HALF, None
                        )
                        total = parts[:2] if total is None else (total[0] + parts[0], total[1] + parts[1])
                        dq_half[half] = parts[2] if dq_half[half] is None else dq_half[half] + parts[2]
                if total is None:
                    total = (jnp.zeros((HALF, 128), F32),) * 2
                dr[keys, cols] = total[0].astype(BF)
                dr[keys, vcols] = total[1].astype(BF)
            for half in range(2):
                part = dq_half[half]
                dq[half_rows(half), cols] = jnp.zeros((HALF, 128), F32) if part is None else part
            return carry

        lax.fori_loop(0, 6, pair, 0)

    for zl in range(2):
        pl.when(idx[3] == zl)(functools.partial(run, FAR_TILES[zl]))


def attend_back_far(idx, q, do, o, lse, far, far_near):
    return kernel_call(
        attend_back_far_body,
        [smem_spec()] + [vmem_spec()] * 4 + [any_spec()] * 2,
        [sds((ROWS, D), F32), sds((ROWS, 2 * D), BF), sds((12, 1, ROWS), F32)],
        [vmem_spec()] * 3,
        [
            pltpu.VMEM((ROWS, 2 * D), BF),
            pltpu.VMEM((ROWS, 128), F32),
            pltpu.SemaphoreType.DMA,
        ],
        (idx, q, do, o, lse, far, far_near),
        12e9,
        8e6,
        name="attend_back_far",
    )


def attend_back_near_body(idx, q, do, lse, drow, dq_far, own, near, dq, dn, dc, kvn, kvc, bias, bias_n, sems):
    waits = load_near(idx, own, near, kvn, kvc, sems)
    set_masks(idx, bias, bias_n, 1)
    for copy in waits:
        copy.wait()

    def run(tiles):
        def pair(hp, carry):
            cols, vcols = pair_cols(hp)
            dq_half = [None, None]
            for half in range(2):
                pieces = []
                for t in range(2):
                    rows = slice(HALF * half + 128 * t, HALF * half + 128 * (t + 1))
                    dk, dv, dqs = back_tile(
                        q, do, lse, drow, cols, hp, kvn[rows, cols], kvn[rows, vcols], rows.start, 128, bias_n[...]
                    )
                    dn[rows, cols] = dk.astype(BF)
                    dn[rows, vcols] = dv.astype(BF)
                    pieces.append(dqs)
                dq_half[half] = dq_far[half_rows(half), cols] + jnp.concatenate(pieces, axis=0)
            for kh in range(2):
                keys = half_rows(kh)
                total = None
                for half, sources in tiles:
                    if kh in dict(sources):
                        parts = back_tile(
                            q,
                            do,
                            lse,
                            drow,
                            cols,
                            hp,
                            kvc[keys, cols],
                            kvc[keys, vcols],
                            HALF * half,
                            HALF,
                            bias[...] if dict(sources)[kh] else None,
                        )
                        total = parts[:2] if total is None else (total[0] + parts[0], total[1] + parts[1])
                        dq_half[half] = dq_half[half] + parts[2]
                dc[keys, cols] = total[0].astype(BF)
                dc[keys, vcols] = total[1].astype(BF)
            for half in range(2):
                dq[half_rows(half), cols] = dq_half[half] * 0.125
            return carry

        lax.fori_loop(0, 6, pair, 0)

    for zl in range(2):
        pl.when(idx[3] == zl)(functools.partial(run, NEAR_TILES[zl]))


def attend_back_near(idx, q, do, lse, drow, dq_far, own, near):
    return kernel_call(
        attend_back_near_body,
        [smem_spec()] + [vmem_spec()] * 5 + [any_spec()] * 2,
        [sds((ROWS, D), F32), sds((ROWS, 2 * D), BF), sds((ROWS, 2 * D), BF)],
        [vmem_spec()] * 3,
        [
            pltpu.VMEM((ROWS, 2 * D), BF),
            pltpu.VMEM((ROWS, 2 * D), BF),
            pltpu.VMEM((HALF, 2 * HALF), F32),
            pltpu.VMEM((128, HALF), F32),
            pltpu.SemaphoreType.DMA((2,)),
        ],
        (idx, q, do, lse, drow, dq_far, own, near),
        18e9,
        12e6,
        name="attend_back_near",
    )


def project_back_body(idx, dq, dn, dcr, got, far, cosine, sine, x, e1, gain, *rest):
    pieces, (dpz, e, small, weights, wide, sems) = rest[:8], rest[8:]
    copies = mixer_copies(pieces, idx, sems, weights)
    for copy in copies:
        copy.start()
    noisy = idx[2] == 0
    for half in range(2):
        rows = slice(HALF * half, HALF * (half + 1))
        for j in range(6):
            cols = slice(128 * j, 128 * (j + 1))
            wide[rows, cols] = unrot(dq[rows, cols], cosine[rows], sine[rows])

        def total(cols, at=rows):
            summed = dcr[at, cols].astype(F32) + got[at, cols].astype(F32) + far[at, cols].astype(F32)
            return jnp.where(noisy, dn[at, cols].astype(F32), summed)

        for j in range(6):
            cols = slice(128 * j, 128 * (j + 1))
            wide[rows, D + 128 * j : D + 128 * (j + 1)] = unrot(total(cols), cosine[rows], sine[rows])
        wide[rows, 2 * D :] = total(slice(D, 2 * D))
    for copy in copies:
        copy.wait()
    small[...] = jnp.zeros_like(small)
    for zq in range(QUARTERS):
        for part in range(3):
            col = D * part + HEADS_COLS * zq
            dpz[zq, :, HEADS_COLS * part : HEADS_COLS * (part + 1)] = wide[:, col : col + HEADS_COLS].astype(BF)
        small[zq : zq + 1, :PARTS] = jnp.sum(dpz[zq].astype(F32), axis=0, keepdims=True)
        piece = dot_nt(dpz[zq], weights[zq])
        if zq == 0:
            e[...] = piece
        else:
            e[...] += piece

    def norm_rows(i, carry):
        rows = rows_at(i * 128, 128, 128)
        unit, inverse = norm_parts(x[rows])
        grad = e[rows]
        small[4:5] += jnp.sum(grad * unit, axis=0, keepdims=True)
        small[5:6] += jnp.sum(grad, axis=0, keepdims=True)
        e[rows] = e1[rows] + norm_backward(grad, unit, inverse, gain[...])
        return carry

    lax.fori_loop(0, 4, norm_rows, 0)


def project_back(idx, dq, dn, dcr, got, far, cosine, sine, x, e1, gain, pieces):
    return kernel_call(
        project_back_body,
        [smem_spec()] + [vmem_spec()] * 10 + [any_spec()] * 8,
        [sds((QUARTERS, ROWS, PARTS), BF), sds((ROWS, D), F32), sds((8, D), F32)],
        [vmem_spec()] * 3,
        [
            pltpu.VMEM((QUARTERS, D, PARTS), BF),
            pltpu.VMEM((ROWS, 3 * D), F32),
            pltpu.SemaphoreType.DMA((32,)),
        ],
        (idx, dq, dn, dcr, got, far, cosine, sine, x, e1, gain, *pieces),
        2 * ROWS * D * 3 * D,
        12e6,
        name="project_back",
    )


def project_grads_body(idx, h1, dpz, keep, send, flipped, stage, sems):
    waits = []
    flipped[...] = jnp.transpose(h1[...])
    for zq in range(QUARTERS):
        k = idx[1] ^ zq
        stage[zq] = dot(flipped[...], dpz[zq]).astype(BF)
        for wq in range(8):
            sem = sems.at[len(waits)]
            source = stage.at[zq, pl.ds(PIECE * wq, PIECE)]
            waits.append(spread(idx, keep, send, source, k, wq, pl.ds(0, PIECE), sem))
    for copy in waits:
        copy.wait()


def project_grads(idx, h1, dpz):
    return kernel_call(
        project_grads_body,
        [smem_spec()] + [vmem_spec()] * 2,
        [sds((4, QUARTERS, PIECE, PARTS), BF)] * 2,
        [any_spec()] * 2,
        [
            pltpu.VMEM((D, ROWS), BF),
            pltpu.VMEM((QUARTERS, D, PARTS), BF),
            pltpu.SemaphoreType.DMA((32,)),
        ],
        (idx, h1, dpz),
        2 * ROWS * D * 3 * D,
        9e6,
        name="project_grads",
    )


def finish_mixer_body(layer, filled, idx, *rest):
    pieces, rest = rest[:8], rest[8:]
    if filled:
        rest = rest[1:]
    out, stage, sem = rest
    for flip, piece in zip(flips(idx), pieces):
        stage[rows_at((idx[0] ^ flip) * PIECE, PIECE, 32)] = piece[...].astype(F32)
    copy = pltpu.make_async_copy(stage, out.at[layer], sem)
    copy.start()
    copy.wait()


def finish_mixer(idx, layer, layers, pieces, before):
    filled = before is not None
    return kernel_call(
        functools.partial(finish_mixer_body, layer, filled),
        [smem_spec()] + [vmem_spec()] * 8 + [any_spec()] * filled,
        sds((layers, D, PARTS), F32),
        any_spec(),
        [pltpu.VMEM((D, PARTS), F32), pltpu.SemaphoreType.DMA],
        (idx, *pieces) + ((before,) if filled else ()),
        1e6,
        4e6,
        aliases={9: 0} if filled else None,
        name="finish_mixer",
    )


def finish_feed_body(layer, filled, idx, *rest):
    pieces, rest = rest[:8], rest[8:]
    if filled:
        rest = rest[3:]
    up, down, out, up_s, down_s, out_s, sems = rest
    for flip, piece in zip(flips(idx), pieces):
        wq = idx[0] ^ flip
        rows = rows_at(wq * PIECE, PIECE, 32)
        up_s[rows] = piece[:PIECE].astype(F32)
        down_s[rows] = piece[PIECE : 2 * PIECE].astype(F32)
        cols = pl.ds(pl.multiple_of((wq & 1) * 384, 128), 384)
        for s in range(3):
            row = 2 * PIECE + 16 * (s // 2)
            block = piece[row : row + 16, 384 * (s % 2) : 384 * (s % 2) + 384]
            out_s[rows_at((wq >> 1) * 48 + 16 * s, 16, 16), cols] = block.astype(F32)
    copies = [
        pltpu.make_async_copy(stage, whole.at[layer], sems.at[i])
        for i, (stage, whole) in enumerate(((up_s, up), (down_s, down), (out_s, out)))
    ]
    for copy in copies:
        copy.start()
    for copy in copies:
        copy.wait()


def finish_feed(idx, layer, layers, pieces, before):
    filled = before is not None
    return kernel_call(
        functools.partial(finish_feed_body, layer, filled),
        [smem_spec()] + [vmem_spec()] * 8 + [any_spec()] * (3 * filled),
        [sds((layers, D, D), F32), sds((layers, D, D), F32), sds((layers, HEADS_COLS, D), F32)],
        [any_spec()] * 3,
        [
            pltpu.VMEM((D, D), F32),
            pltpu.VMEM((D, D), F32),
            pltpu.VMEM((HEADS_COLS, D), F32),
            pltpu.SemaphoreType.DMA((3,)),
        ],
        (idx, *pieces) + (tuple(before) if filled else ()),
        1e6,
        8e6,
        aliases={9: 0, 10: 1, 11: 2} if filled else None,
        name="finish_feed",
    )


def pack_body(idx, ups, downs, outs, *rest):
    targets, (zeros, sems) = rest[:-2], rest[-2:]
    zeros[...] = jnp.zeros_like(zeros)
    rows = rows_at(idx[0] * PIECE, PIECE, 32)
    cols = pl.ds(pl.multiple_of(idx[2] * 384, 128), 384)
    copies = []
    for layer, target in enumerate(targets):
        moves = [
            (ups.at[layer, rows], target.at[pl.ds(0, PIECE)]),
            (downs.at[layer, rows], target.at[pl.ds(PIECE, PIECE)]),
        ]
        for s in range(4):
            place = target.at[pl.ds(2 * PIECE + 16 * (s // 2), 16), pl.ds(384 * (s % 2), 384)]
            if s == 3:
                moves.append((zeros, place))
            else:
                moves.append((outs.at[layer, rows_at((idx[0] >> 1) * 48 + 16 * s, 16, 16), cols], place))
        for source, place in moves:
            copies.append(pltpu.make_async_copy(source, place, sems.at[len(copies)]))
    for copy in copies:
        copy.start()
    for copy in copies:
        copy.wait()


def pack(idx, ups, downs, outs):
    layers = ups.shape[0]
    return kernel_call(
        pack_body,
        [smem_spec()] + [any_spec()] * 3,
        [sds((PACK, D), BF)] * layers,
        [vmem_spec()] * layers,
        [pltpu.VMEM((16, 384), BF), pltpu.SemaphoreType.DMA((6 * layers,))],
        (idx, ups, downs, outs),
        1e6,
        1e6,
        name="pack",
    )


def flip_wide(x, bit):
    return lax.ppermute(x, "wide", [(i, i ^ bit) for i in range(lax.axis_size("wide"))])


def flip_narrow(x, bit):
    return lax.ppermute(x, "narrow", [(i, i ^ bit) for i in range(QUARTERS)])


def first_axis(x):
    return lax.ppermute(x, "wide", [(i, i ^ (4 if i & 1 else 2)) for i in range(lax.axis_size("wide"))])


def second_axis(x):
    return lax.ppermute(x, "wide", [(i, i ^ (2 if i & 1 else 4)) for i in range(lax.axis_size("wide"))])


def gate_body(*refs):
    return None


def gate(tree):
    leaves, shape = jax.tree.flatten(tree)
    out = pl.pallas_call(
        gate_body,
        in_specs=[any_spec() for _ in leaves],
        out_specs=[any_spec() for _ in leaves],
        out_shape=[sds(x.shape, x.dtype) for x in leaves],
        input_output_aliases={i: i for i in range(len(leaves))},
        name="gate",
    )(*leaves)
    return jax.tree.unflatten(shape, out)


def gather_direct(piece):
    return [piece] + [flip_narrow(piece, k) for k in ORDER[1:]]


def gather_far(piece):
    return piece, flip_narrow(piece, 2)


def gather_near(pair):
    pair = jnp.stack(pair)
    return pair, flip_narrow(pair, 1)


def whole(parts):
    return jnp.stack(parts) if parts[0].ndim == 2 else jnp.concatenate(parts)


def gather_first(own):
    return own, first_axis(own)


def gather_second(parts):
    own, first = parts
    return [own, first, second_axis(own), second_axis(first)]


def gather_last(here):
    return here + [flip_wide(x, 1) for x in here]


def added(*terms):
    return functools.reduce(jnp.add, [t.astype(F32) for t in terms]).astype(BF)


def reduce_core(pair):
    keep, send = pair
    return keep, flip_wide(send, 1)


def reduce_first_sums(pair):
    keep, got = pair
    return keep, got, added(keep[3], got[3]), added(keep[2], got[2])


def reduce_first(parts):
    keep, got, passed, stays = parts
    return keep, got, first_axis(passed), first_axis(stays)


def reduce_first_whole(pair):
    keep, got = pair
    return keep, got, first_axis(added(keep[2:], got[2:]))


def reduce_second(keep, got, passed):
    return second_axis(added(keep[1], got[1], passed))


def reduce_near(parts):
    total = added(parts[0][0], parts[1][0], *parts[2:])
    bit = 8
    while bit < lax.axis_size("wide"):
        total = added(total, flip_wide(total, bit))
        bit *= 2
    return total, flip_narrow(total[2:], 1)


def reduce_far(parts):
    total, near = parts
    return total, near, flip_narrow(added(total[1], near[1]), 2)


def both_axes(x):
    return flip_wide(x, 6)


def gather_plane(own):
    return [own, first_axis(own), second_axis(own), both_axes(own)]


def spread_first(parts):
    total, near, far = parts
    return gather_first(added(total[0], near[0], far))


def reduce_plane(pair):
    keep, got = pair
    moves = (second_axis, first_axis, both_axes)
    return [keep, got] + [move(added(keep[i + 1], got[i + 1])) for i, move in enumerate(moves)]


def reduce_narrow(parts):
    keep, got, *others = parts
    total = added(keep[0], got[0], *others)
    bit = 8
    while bit < lax.axis_size("wide"):
        total = added(total, flip_wide(total, bit))
        bit *= 2
    return [total] + [flip_narrow(total[i], ORDER[i]) for i in range(1, QUARTERS)]


def device_pairs(move):
    pairs = []
    for w in range(lax.axis_size("wide")):
        for z in range(QUARTERS):
            target = move(w, z)
            if target is not None:
                pairs.append((w * QUARTERS + z, target[0] * QUARTERS + target[1]))
    return pairs


BOTH = ("wide", "narrow")


def relocate_first(rows):
    pairs = device_pairs(lambda w, z: ((w & ~1) | (z >> 1), ((w & 1) << 1) | (z & 1)))
    return lax.ppermute(rows, BOTH, pairs)


def relocate_second(rows):
    pairs = device_pairs(lambda w, z: ((w & ~1) | (z >> 1), ((w & 1) << 1) | (1 - (z & 1))))
    return lax.ppermute(rows, BOTH, pairs)


def relocate(rows):
    return relocate_halves((rows[:HALF], rows[HALF:]))


def relocate_halves(halves):
    return relocate_first(halves[0]), relocate_second(halves[1])


def between_chips(x):
    pairs = device_pairs(lambda w, z: (w, z ^ 1) if w & 1 else None)
    return lax.ppermute(x, BOTH, pairs)


def within_chip(x, source):
    pairs = [(i, i ^ 1) for i in range(lax.axis_size("wide")) if (i & 1) == source]
    return lax.ppermute(x, "wide", pairs)


def per_device(
    tokens,
    block_size,
    norm_gain,
    norm_shift,
    mixer_weight,
    mixer_bias,
    output_weight,
    output_bias,
    up_weight,
    up_bias,
    down_weight,
    cotangent,
):
    layers = norm_gain.shape[0]
    w, z = lax.axis_index("wide"), lax.axis_index("narrow")
    w8, core, low = w & 7, w & 1, z & 1
    sizes = jnp.where((z >> 1) == core, block_size, flip_wide(block_size, 1))[0]
    level = 2 + (sizes >= 8).astype(jnp.int32) + (sizes >= 16).astype(jnp.int32)
    idx = jnp.stack([w8, z, core, low, level, w8, w8, w8]).astype(jnp.int32)

    bases = jnp.where(low == 0, jnp.array([0, 768]), jnp.array([512, 256]))
    position = (bases[:, None] + jnp.arange(HALF)[None, :]).reshape(ROWS).astype(F32)
    halfway = HEAD_DIM // 2
    frequency = jnp.exp(jnp.arange(halfway, dtype=F32) * (-math.log(10000.0) / halfway))
    angle = position[:, None] * frequency[None, :]
    cosine = jnp.tile(jnp.cos(angle), (1, 4))
    sine = jnp.sin(angle)
    sine = jnp.concatenate([-sine, sine, -sine, sine], axis=1)

    def bias_pieces(layer):
        return mixer_bias[layer].reshape(PARTS), up_bias[layer]

    biases = jnp.concatenate([t for layer in range(layers) for t in bias_pieces(layer)])
    width = PARTS + D

    def bias_of(layer, start, size):
        at = width * layer + start
        return jnp.stack([b[at : at + size] for b in biases])[:, None]

    def mixer_piece(layer):
        return lax.dynamic_slice_in_dim(mixer_weight[layer], w8 * PIECE, PIECE, 0).reshape(PIECE, PARTS)

    def run_project(layer, x, pieces):
        gain, shift = norm_gain[layer], norm_shift[layer]
        return project(idx, x, gain[0:1], shift[0:1], bias_of(layer, 0, PARTS), cosine, sine, pieces)

    def run_feed(layer, x, o, pieces):
        gain, shift, bias = norm_gain[layer], norm_shift[layer], output_bias[layer]
        return feed(
            idx, x, o, gain[1:2], shift[1:2], bias[0:1], bias[1:2], bias_of(layer, PARTS, D), pieces
        )

    mixer0 = gather_direct(mixer_piece(0))
    feed0, feed1 = pack(idx, up_weight, down_weight, output_weight)
    biases = [biases] + [flip_narrow(biases, k) for k in (1, 2, 3)]
    halves = tokens[:HALF], tokens[HALF:]
    mixer0, halves, feed0, biases = gate((mixer0, halves, feed0, biases))
    mixer0 = gather_first(whole(mixer0))
    feed0 = gather_far(feed0)
    mixer0, feed0, halves, mixer1 = gate((mixer0, feed0, halves, mixer_piece(1)))
    own, first = mixer0
    mixer0 = [own, first, second_axis(own), second_axis(first)]
    rows = relocate_halves(halves)
    feed0 = gather_near(feed0)
    mixer0, rows, feed0, mixer1 = gate((mixer0, rows, feed0, mixer1))
    mixer0 = gather_last(mixer0)
    own, first = gather_first(whole(feed0))
    mixer1 = gather_far(mixer1)
    x0 = jnp.concatenate(rows).astype(F32)
    h1_0, q_0, kv = run_project(0, x0, mixer0)
    own_0, own, first, mixer1 = gate((kv, own, first, mixer1))
    near_0, far = within_chip(own_0, 1), between_chips(own_0)
    second = second_axis(own)
    others = [flip_wide(own, 1), flip_wide(first, 1)]
    state = attend_near(idx, q_0, own_0, near_0)
    state, far_0, first, second, others, mixer1, feed1 = gate((state, far, first, second, others, mixer1, feed1))
    far_near_0 = within_chip(far_0, 1)
    third = second_axis(first)
    others = others + [flip_wide(second, 1)]
    mixer1, feed1 = gather_near(mixer1), gather_far(feed1)
    o_0, lse_0 = attend_far(idx, q_0, far_0, far_near_0, state)
    o_0, third, others, mixer1, feed1 = gate((o_0, third, others, mixer1, feed1))
    feed0 = [own, first, second, third] + others + [flip_wide(third, 1)]
    mixer1, feed1 = gather_plane(whole(mixer1)), gather_near(feed1)
    x1, x1_0, h2_0, g_0, gp_0 = run_feed(0, x0, o_0, feed0)
    x1, mixer1, feed1 = gate((x1, mixer1, feed1))
    mixer1 = gather_last(mixer1)
    own, first = gather_first(whole(feed1))
    h1_1, q_1, kv = run_project(1, x1, mixer1)
    own_1, own, first = gate((kv, own, first))
    near_1, far = within_chip(own_1, 1), between_chips(own_1)
    second = second_axis(own)
    state = attend_near(idx, q_1, own_1, near_1)
    state, far_1, own, first, second = gate((state, far, own, first, second))
    far_near_1 = within_chip(far_1, 1)
    third = second_axis(first)
    others = [flip_wide(own, 1), flip_wide(first, 1), flip_wide(second, 1)]
    o_1, lse_1 = attend_far(idx, q_1, far_1, far_near_1, state)
    o_1, third, others, halves = gate((o_1, third, others, (cotangent[:HALF], cotangent[HALF:])))
    e = relocate_halves(halves)
    feed1 = [own, first, second, third] + others + [flip_wide(third, 1)]
    x2, x1_1, h2_1, g_1, gp_1 = run_feed(1, x1, o_1, feed1)
    x2, e = gate((x2, e))
    x_out = relocate(x2.astype(BF))

    e = jnp.concatenate(e).astype(F32)
    dm, dz, e1, da, do, small_feed1 = feed_back(idx, e, x1_1, gp_1, norm_gain[1, 1:2], feed1)
    g_feed1 = feed_grads(idx, g_1, dm, h2_1, dz, o_1, da)
    do, x_out, g_feed1 = gate((do, x_out, g_feed1))
    g_feed1 = reduce_core(g_feed1)
    dq, dr, drow = attend_back_far(idx, q_1, do, o_1, lse_1, far_1, far_near_1)
    dr, dq, g_feed1 = gate((dr, dq, g_feed1))
    dr, got, dq, g_feed1 = gate((dr, within_chip(dr, 0), dq, reduce_first_sums(g_feed1)))
    far = between_chips(added(dr, got))
    g_feed1 = reduce_first(g_feed1)
    dq, dn, dc = attend_back_near(idx, q_1, do, lse_1, drow, dq, own_1, near_1)
    keep, gained, passed, stays = g_feed1
    dc, far, keep, gained, passed = gate((dc, far, keep, gained, passed))
    got = within_chip(dc, 0)
    g_feed1 = keep, gained, stays, reduce_second(keep, gained, passed)
    dpz, e, small_mixer1 = project_back(
        idx, dq, dn, dc, got, far, cosine, sine, x1, e1, norm_gain[1, 0:1], mixer1
    )
    dpz, e, g_feed1 = gate((dpz, e, g_feed1))
    g_feed1 = reduce_near(g_feed1)
    g_mixer1 = project_grads(idx, h1_1, dpz)
    e, g_mixer1 = gate((e, g_mixer1))
    g_mixer1 = reduce_core(g_mixer1)
    dm, dz, e1, da, do, small_feed0 = feed_back(idx, e, x1_0, gp_0, norm_gain[0, 1:2], feed0)
    dm, do, g_feed1, g_mixer1 = gate((dm, do, g_feed1, g_mixer1))
    g_feed1, g_mixer1 = reduce_far(g_feed1), reduce_first_whole(g_mixer1)
    g_feed0 = feed_grads(idx, g_0, dm, h2_0, dz, o_0, da)
    do, g_feed1, g_mixer1, g_feed0 = gate((do, g_feed1, g_mixer1, g_feed0))
    keep1, gained1, both1 = g_mixer1
    second1, g_feed0 = reduce_second(keep1, gained1, both1[1]), reduce_core(g_feed0)
    g_feed1 = spread_first(g_feed1)
    dq, dr, drow = attend_back_far(idx, q_0, do, o_0, lse_0, far_0, far_near_0)
    dr, dq, g_feed1, second1, g_feed0 = gate((dr, dq, g_feed1, second1, g_feed0))
    dr, got, dq, g_feed0, g_feed1 = gate((dr, within_chip(dr, 0), dq, reduce_first_sums(g_feed0), g_feed1))
    far = between_chips(added(dr, got))
    g_feed0, g_feed1 = reduce_first(g_feed0), gather_second(g_feed1)
    dq, dn, dc = attend_back_near(idx, q_0, do, lse_0, drow, dq, own_0, near_0)
    keep, gained, passed, stays = g_feed0
    dc, far, keep, gained, passed, g_feed1 = gate((dc, far, keep, gained, passed, g_feed1))
    got = within_chip(dc, 0)
    g_feed0 = keep, gained, stays, reduce_second(keep, gained, passed)
    g_mixer1 = reduce_near((keep1, gained1, both1[0], second1))
    dpz, e, small_mixer0 = project_back(
        idx, dq, dn, dc, got, far, cosine, sine, x0, e1, norm_gain[0, 0:1], mixer0
    )
    e, dpz, g_feed0, g_mixer1 = gate((e, dpz, g_feed0, g_mixer1))
    g_feed0, g_mixer1 = reduce_near(g_feed0), reduce_far(g_mixer1)
    g_mixer0 = reduce_core(project_grads(idx, h1_0, dpz))
    smalls = jnp.concatenate([small_feed0, small_mixer0, small_feed1, small_mixer1])
    g_feed1 = gather_last(g_feed1)
    smalls = smalls, flip_wide(smalls, 1)
    g_mixer0, smalls, e, g_feed1, g_mixer1 = gate((g_mixer0, smalls, e, g_feed1, g_mixer1))
    g_mixer0 = reduce_plane(g_mixer0)
    early, e_late = relocate_first(e[:HALF].astype(BF)), e
    feed_out = finish_feed(idx, 1, layers, g_feed1, None)
    g_mixer0, g_feed0, smalls, feed_out, early, e_late, g_mixer1 = gate(
        (g_mixer0, g_feed0, smalls, feed_out, early, e_late, g_mixer1)
    )
    keep, gained, *others = g_mixer0
    total = added(keep[0], gained[0], *others)
    bit = 8
    while bit < lax.axis_size("wide"):
        total = added(total, flip_wide(total, bit))
        bit *= 2
    g_mixer0 = total, flip_narrow(total[2:], 1)
    g_feed0 = reduce_far(g_feed0)
    smalls = smalls[0] + smalls[1]
    smalls = smalls, first_axis(smalls)
    g_mixer1 = spread_first(g_mixer1)
    g_mixer0, g_feed0, smalls, g_mixer1, e_late = gate((g_mixer0, g_feed0, smalls, g_mixer1, e_late))
    g_mixer0, g_feed0 = reduce_far(g_mixer0), spread_first(g_feed0)
    smalls = smalls[0] + smalls[1]
    smalls = smalls, second_axis(smalls)
    own, first = g_mixer1
    both = second_axis(jnp.stack([own, first]))
    late = relocate_second(e_late[HALF:].astype(BF))
    g_mixer0, g_feed0, smalls, own, first, both, late = gate((g_mixer0, g_feed0, smalls, own, first, both, late))
    g_mixer1 = [own, first, both[0], both[1]]
    g_mixer0, g_feed0 = spread_first(g_mixer0), gather_second(g_feed0)
    smalls = smalls[0] + smalls[1]
    bit = 8
    while bit < lax.axis_size("wide"):
        smalls = smalls + flip_wide(smalls, bit)
        bit *= 2
    smalls = smalls, flip_narrow(smalls, 1)
    g_mixer1 = gather_last(g_mixer1)
    mixer_out = finish_mixer(idx, 1, layers, g_mixer1, None)
    g_mixer0, g_feed0, smalls, mixer_out = gate((g_mixer0, g_feed0, smalls, mixer_out))
    g_mixer0, g_feed0 = gather_second(g_mixer0), gather_last(g_feed0)
    smalls = smalls[0] + smalls[1]
    smalls = smalls, flip_narrow(smalls, 2)
    feed_out = finish_feed(idx, 0, layers, g_feed0, feed_out)
    g_mixer0, smalls, feed_out = gate((g_mixer0, smalls, feed_out))
    smalls = smalls[0] + smalls[1]
    g_mixer0 = gather_last(g_mixer0)
    mixer_out = finish_mixer(idx, 0, layers, g_mixer0, mixer_out)
    tokens_grad = jnp.concatenate([early, late])
    x_out = jnp.concatenate(x_out)

    small = smalls.reshape(layers, 16, D)
    up_bias_grad = lax.dynamic_index_in_dim(small[:, 0:4], z, 1, keepdims=False)
    mixer_bias_grad = lax.dynamic_index_in_dim(small[:, 8:12, :PARTS], z, 1, keepdims=False)
    return (
        x_out,
        tokens_grad,
        jnp.stack([small[:, 12], small[:, 6]], axis=1),
        jnp.stack([small[:, 13], small[:, 7]], axis=1),
        mixer_out.reshape(layers, D, 3, HEADS_COLS),
        mixer_bias_grad.reshape(layers, 3, HEADS_COLS),
        feed_out[2],
        jnp.stack([small[:, 5], small[:, 4]], axis=1),
        feed_out[0],
        up_bias_grad,
        feed_out[1],
    )


def solution(mesh):
    rows = P(("wide", "narrow"), None)
    quarters = (
        P(None, None, None, "narrow"),
        P(None, None, "narrow"),
        P(None, "narrow", None),
        P(),
        P(None, None, "narrow"),
        P(None, "narrow"),
        P(None, "narrow", None),
    )
    return jax.shard_map(
        per_device,
        mesh=mesh,
        in_specs=(rows, P("wide"), P(), P()) + quarters + (rows,),
        out_specs=(rows, rows, P(), P()) + quarters,
        check_vma=False,
    )
```

```python
import functools
import math

import jax
import jax.numpy as jnp
from jax import lax
from jax.experimental import pallas as pl
from jax.experimental.pallas import tpu as pltpu
from jax.sharding import PartitionSpec as P

HEAD_DIM = 64
LEN = 1024
EPSILON = 1e-05
D = 768
QUARTERS = 4
HALF = 256
ROWS = 512
PIECE = 96
HEADS_COLS = 192
PARTS = 576
PACK = 224
MASKED = -1e30
BF = jnp.bfloat16
F32 = jnp.float32
NT = (((1,), (1,)), ((), ()))
TN = (((0,), (0,)), ((), ()))
VMEM_LIMIT = 56 * 1024 * 1024


def dot(a, b):
    return jnp.dot(a, b, preferred_element_type=F32)


def dot_nt(a, b):
    return lax.dot_general(a, b, NT, preferred_element_type=F32)


def dot_tn(a, b):
    return lax.dot_general(a, b, TN, preferred_element_type=F32)


def norm_parts(values):
    center = values - jnp.mean(values, axis=-1, keepdims=True)
    inverse = lax.rsqrt(jnp.mean(center * center, axis=-1, keepdims=True) + EPSILON)
    return center * inverse, inverse


def norm_backward(grad_in, unit_rows, inverse, gain):
    scaled = grad_in * gain
    return inverse * (
        scaled
        - jnp.mean(scaled, axis=-1, keepdims=True)
        - unit_rows * jnp.mean(scaled * unit_rows, axis=-1, keepdims=True)
    )


def swap_halves(u):
    lane = lax.broadcasted_iota(jnp.int32, u.shape, 1)
    return jnp.where((lane & 63) < 32, pltpu.roll(u, 96, axis=1), pltpu.roll(u, 32, axis=1))


def rot(u, cosine, sine):
    return u * cosine + swap_halves(u) * sine


def unrot(u, cosine, sine):
    return u * cosine - swap_halves(u) * sine


ORDER = (0, 2, 1, 3)


def flips(idx):
    first, second = 2 + 2 * idx[2], 4 - 2 * idx[2]
    return [0, first, second, 6, 1, 1 ^ second, 1 ^ first, 7]


def piece_copies(refs, idx, sems, place):
    copies = []
    for flip, ref in zip(flips(idx), refs):
        for at, k in enumerate(ORDER):
            for source, target in place(ref.at[at], k, idx[1] ^ k, idx[0] ^ flip):
                copies.append(pltpu.make_async_copy(source, target, sems.at[len(copies)]))
    return copies


def rows_at(start, size, unit):
    return pl.ds(pl.multiple_of(start, unit), size)


def mixer_copies(refs, idx, sems, weights):
    def place(src, k, zq, wq):
        return [(src, weights.at[zq, rows_at(wq * PIECE, PIECE, 32)])]

    return piece_copies(refs, idx, sems, place)


def up_down_copies(refs, idx, sems, ups, downs):
    groups = []
    for k in range(QUARTERS):
        up, down = [], []
        for i, (flip, ref) in enumerate(zip(flips(idx), refs)):
            rows = rows_at((idx[0] ^ flip) * PIECE, PIECE, 32)
            src = ref.at[ORDER.index(k)]
            up.append(pltpu.make_async_copy(src.at[pl.ds(0, PIECE)], ups.at[k, rows], sems.at[16 * k + i]))
            down.append(pltpu.make_async_copy(src.at[pl.ds(PIECE, PIECE)], downs.at[k, rows], sems.at[16 * k + 8 + i]))
        groups.append((up, down))
    return groups


def begin(copies):
    for copy in copies:
        copy.start()


def finish(copies):
    for copy in copies:
        copy.wait()


def packed_copies(refs, idx, sems, packed):
    def place(src, k, zq, wq):
        return [(src.at[pl.ds(2 * PIECE, 32)], packed.at[zq, wq])]

    return piece_copies(refs, idx, sems, place)


def unpack_output(packed, weights):
    for zq in range(QUARTERS):
        for chip in range(4):
            for part in range(2):
                for s in range(3):
                    row = HEADS_COLS * zq + 48 * chip + 16 * s
                    weights[row : row + 16, 384 * part : 384 * part + 384] = packed[
                        zq, 2 * chip + part, 16 * (s // 2) : 16 * (s // 2) + 16, 384 * (s % 2) : 384 * (s % 2) + 384
                    ]


def any_spec():
    return pl.BlockSpec(memory_space=pl.ANY)


def vmem_spec():
    return pl.BlockSpec(memory_space=pltpu.VMEM)


def smem_spec():
    return pl.BlockSpec(memory_space=pltpu.SMEM)


def kernel_call(body, in_specs, out_shape, out_specs, scratch, args, flops, moved, aliases=None, name=None):
    return pl.pallas_call(
        body,
        in_specs=in_specs,
        out_specs=out_specs,
        out_shape=out_shape,
        scratch_shapes=scratch,
        input_output_aliases=aliases or {},
        compiler_params=pltpu.CompilerParams(vmem_limit_bytes=VMEM_LIMIT),
        cost_estimate=pl.CostEstimate(flops=1000, bytes_accessed=1000, transcendentals=0),
        name=name,
    )(*args)


def sds(shape, dtype):
    return jax.ShapeDtypeStruct(shape, dtype)


def project_body(idx, x, gain, shift, bias, cosine, sine, *rest):
    pieces, (h1, q, kv, weights, wide, sems) = rest[:8], rest[8:]
    copies = mixer_copies(pieces, idx, sems, weights)
    for copy in copies:
        copy.start()

    def norm_rows(i, carry):
        rows = rows_at(i * 128, 128, 128)
        unit, _ = norm_parts(x[rows])
        h1[rows] = (unit * gain[...] + shift[...]).astype(BF)
        return carry

    lax.fori_loop(0, 4, norm_rows, 0)
    for copy in copies:
        copy.wait()
    for zq in range(QUARTERS):
        p = dot(h1[...], weights[zq]) + bias[idx[1] ^ zq]
        for part in range(3):
            col = D * part + HEADS_COLS * zq
            wide[:, col : col + HEADS_COLS] = p[:, HEADS_COLS * part : HEADS_COLS * (part + 1)]
    for half in range(2):
        rows = slice(HALF * half, HALF * (half + 1))
        for j in range(6):
            cols = slice(128 * j, 128 * (j + 1))
            q[rows, cols] = (rot(wide[rows, cols], cosine[rows], sine[rows]) * 0.125).astype(BF)
            kcols = slice(D + 128 * j, D + 128 * (j + 1))
            kv[rows, cols] = rot(wide[rows, kcols], cosine[rows], sine[rows]).astype(BF)
        kv[rows, D:] = wide[rows, 2 * D :].astype(BF)


def project(idx, x, gain, shift, bias, cosine, sine, pieces):
    return kernel_call(
        project_body,
        [smem_spec()] + [vmem_spec()] * 6 + [any_spec()] * 8,
        [sds((ROWS, D), BF), sds((ROWS, D), BF), sds((ROWS, 2 * D), BF)],
        [vmem_spec()] * 3,
        [
            pltpu.VMEM((QUARTERS, D, PARTS), BF),
            pltpu.VMEM((ROWS, 3 * D), F32),
            pltpu.SemaphoreType.DMA((32,)),
        ],
        (idx, x, gain, shift, bias, cosine, sine, *pieces),
        2 * ROWS * D * 3 * D,
        8e6,
        name="project",
    )


def load_near(idx, own, near, kvn, kvc, sems):
    clean = idx[2] == 1
    copy = pltpu.make_async_copy(own, kvn, sems.at[0])
    copy.start()
    a = pltpu.make_async_copy(own, kvc, sems.at[1])
    b = pltpu.make_async_copy(near, kvc, sems.at[1])
    pl.when(clean)(a.start)
    pl.when(jnp.logical_not(clean))(b.start)
    return [copy, a]


def load_far(idx, far, far_near, kvr, sem):
    clean = idx[2] == 1
    a = pltpu.make_async_copy(far, kvr, sem)
    b = pltpu.make_async_copy(far_near, kvr, sem)
    pl.when(clean)(a.start)
    pl.when(jnp.logical_not(clean))(b.start)
    return a


NEAR_TILES = {0: [(0, [(0, True)]), (1, [(1, True), (0, False)])], 1: [(1, [(1, True)]), (0, [(0, True), (1, False)])]}
FAR_TILES = {0: [(1, [0, 1])], 1: [(1, [0]), (0, [0])]}


def set_masks(idx, bias, bias_n, query_dim):
    clean, level = idx[2], idx[4]
    qi = lax.shift_right_logical(lax.broadcasted_iota(jnp.int32, (HALF, HALF), query_dim), level)
    ki = lax.shift_right_logical(lax.broadcasted_iota(jnp.int32, (HALF, HALF), 1 - query_dim), level)
    allowed = jnp.where(ki < qi + clean, 0.0, MASKED)
    bias[...] = jnp.concatenate([allowed, allowed], axis=query_dim)
    same = (jnp.where(ki == qi, 0, 1) + clean)[:128, :128]
    own = jnp.where(same == 0, 0.0, MASKED)
    bias_n[...] = jnp.concatenate([own, own], axis=query_dim)


def lanes(rows):
    return lax.broadcasted_iota(jnp.int32, (rows, 128), 1)


def one_head(v, side):
    low_lane = lanes(v.shape[0]) < 64
    return jnp.where(low_lane if side == 0 else jnp.logical_not(low_lane), v, jnp.zeros_like(v))


def both_heads(v):
    return jnp.concatenate([one_head(v, 0), one_head(v, 1)], axis=0)


def pair_lanes(v):
    n = v.shape[0] // 2
    return jnp.where(lanes(n) < 64, v[:n], v[n:])


def pair_cols(hp):
    off = pl.multiple_of(hp * 128, 128)
    return pl.ds(off, 128), pl.ds(pl.multiple_of(D + off, 128), 128)


def row_max(s):
    return jnp.max(s, axis=-1, keepdims=True)


def with_ones(v):
    return jnp.concatenate([v, jnp.ones_like(v)], axis=1)


def half_rows(half):
    return slice(HALF * half, HALF * (half + 1))


def attend_near_body(idx, q, own, near, acc, tops, counts, kvn, kvc, bias, bias_n, sems):
    waits = load_near(idx, own, near, kvn, kvc, sems)
    set_masks(idx, bias, bias_n, 0)
    tops[...] = jnp.zeros_like(tops)
    counts[...] = jnp.ones_like(counts)
    for copy in waits:
        copy.wait()

    def run(tiles):
        def pair(hp, carry):
            cols, vcols = pair_cols(hp)
            lane = lanes(HALF)
            for half, sources in tiles:
                rows = half_rows(half)
                qs = both_heads(q[rows, cols])
                scores = []
                for kh, diagonal in sources:
                    s = dot_nt(qs, kvc[half_rows(kh), cols])
                    scores.append(s + bias[...] if diagonal else s)
                blocks = [slice(HALF * half + 128 * t, HALF * half + 128 * (t + 1)) for t in range(2)]

                def of_block(v, t):
                    return jnp.concatenate([v[128 * t : 128 * (t + 1)], v[HALF + 128 * t : HALF + 128 * (t + 1)]], axis=0)

                def of_heads(a, b):
                    return jnp.concatenate([a[:128], b[:128], a[128:], b[128:]], axis=0)

                mine = [dot_nt(of_block(qs, t), kvn[blocks[t], cols]) + bias_n[...] for t in range(2)]
                top = of_heads(*[row_max(s) for s in mine])
                for s in scores:
                    top = jnp.maximum(top, row_max(s))
                total = of_heads(
                    *[
                        dot(jnp.exp(mine[t] - of_block(top, t)).astype(BF), with_ones(kvn[blocks[t], vcols]))
                        for t in range(2)
                    ]
                )
                for s, (kh, diagonal) in zip(scores, sources):
                    total = total + dot(jnp.exp(s - top).astype(BF), with_ones(kvc[half_rows(kh), vcols]))
                acc[rows, cols] = pair_lanes(total[:, :128])
                for target, value in ((tops, top), (counts, total[:, 128:])):
                    target[rows] = jnp.where(
                        lane == 2 * hp, value[:HALF], jnp.where(lane == 2 * hp + 1, value[HALF:], target[rows])
                    )
            return carry

        lax.fori_loop(0, 6, pair, 0)

    for zl in range(2):
        pl.when(idx[3] == zl)(functools.partial(run, NEAR_TILES[zl]))


def attend_near(idx, q, own, near):
    return kernel_call(
        attend_near_body,
        [smem_spec(), vmem_spec()] + [any_spec()] * 2,
        [sds((ROWS, D), F32), sds((ROWS, 128), F32), sds((ROWS, 128), F32)],
        [vmem_spec()] * 3,
        [
            pltpu.VMEM((ROWS, 2 * D), BF),
            pltpu.VMEM((ROWS, 2 * D), BF),
            pltpu.VMEM((2 * HALF, HALF), F32),
            pltpu.VMEM((HALF, 128), F32),
            pltpu.SemaphoreType.DMA((2,)),
        ],
        (idx, q, own, near),
        8e9,
        6e6,
        name="attend_near",
    )


def attend_far_body(idx, q, far, far_near, acc, tops, counts, o, lse, kvr, last, sem):
    copy = load_far(idx, far, far_near, kvr, sem)
    last[...] = tops[...] + jnp.log(counts[...])
    copy.wait()

    def column(values, head):
        return jnp.sum(jnp.where(lanes(HALF) == head, values, 0.0), axis=-1, keepdims=True)

    def run(tiles):
        covered = [half for half, _ in tiles]

        def pair(hp, carry):
            cols, vcols = pair_cols(hp)
            lane = lanes(HALF)
            for half in range(2):
                rows = half_rows(half)
                if half in covered:
                    sources = dict(tiles)[half]
                    q2 = q[rows, cols]
                    sides = []
                    for side in range(2):
                        qm = one_head(q2, side)
                        scores = [dot_nt(qm, kvr[half_rows(kh), cols]) for kh in sources]
                        before = column(tops[rows], 2 * hp + side)
                        top = before
                        for s in scores:
                            top = jnp.maximum(top, row_max(s))
                        shrink = jnp.exp(before - top)
                        total = None
                        for s, kh in zip(scores, sources):
                            part = dot(jnp.exp(s - top).astype(BF), with_ones(kvr[half_rows(kh), vcols]))
                            total = part if total is None else total + part
                        count = column(counts[rows], 2 * hp + side) * shrink + total[:, 128:]
                        value = (acc[rows, cols] * shrink + total[:, :128]) / count
                        sides.append((value, top + jnp.log(count)))
                    last[rows] = jnp.where(
                        lane == 2 * hp, sides[0][1], jnp.where(lane == 2 * hp + 1, sides[1][1], last[rows])
                    )
                else:
                    sides = [(acc[rows, cols] / column(counts[rows], 2 * hp + side),) for side in range(2)]
                o[rows, cols] = jnp.where(lane < 64, sides[0][0], sides[1][0]).astype(BF)
            return carry

        lax.fori_loop(0, 6, pair, 0)

    for zl in range(2):
        pl.when(idx[3] == zl)(functools.partial(run, FAR_TILES[zl]))
    across = jnp.transpose(last[...])
    for head in range(12):
        lse[head] = across[head : head + 1]


def attend_far(idx, q, far, far_near, state):
    return kernel_call(
        attend_far_body,
        [smem_spec(), vmem_spec()] + [any_spec()] * 2 + [vmem_spec()] * 3,
        [sds((ROWS, D), BF), sds((12, 1, ROWS), F32)],
        [vmem_spec()] * 2,
        [
            pltpu.VMEM((ROWS, 2 * D), BF),
            pltpu.VMEM((ROWS, 128), F32),
            pltpu.SemaphoreType.DMA,
        ],
        (idx, q, far, far_near, *state),
        5e9,
        6e6,
        name="attend_far",
    )


def feed_body(idx, x_in, o_in, gain, shift, out_bias, down_bias, up_bias, *rest):
    pieces, (x2_out, x1_out, h2_out, g_out, gp_out), rest = rest[:8], rest[8:13], rest[13:]
    ups, downs, packed, outw, x, o, x2, x1, h2, g, gp, sems, sems_o, sems_io = rest
    first = packed_copies(pieces, idx, sems_o, packed)
    loads = [pltpu.make_async_copy(o_in, o, sems_io.at[0]), pltpu.make_async_copy(x_in, x, sems_io.at[1])]
    later = up_down_copies(pieces, idx, sems, ups, downs)
    begin(first + loads + later[0][0])
    finish(first)
    unpack_output(packed, outw)
    finish(loads)
    begin(later[0][1])
    x1[...] = x[...] + (dot(o[...], outw[...]) + out_bias[...])
    stores = [pltpu.make_async_copy(x1, x1_out, sems_io.at[2])]
    begin(stores)

    def norm_rows(i, carry):
        rows = rows_at(i * 128, 128, 128)
        unit, _ = norm_parts(x1[rows])
        h2[rows] = (unit * gain[...] + shift[...]).astype(BF)
        x2[rows] = x1[rows] + down_bias[...]
        return carry

    lax.fori_loop(0, 4, norm_rows, 0)
    stores.append(pltpu.make_async_copy(h2, h2_out, sems_io.at[3]))
    begin(stores[-1:])
    for k, (up, down) in enumerate(later):
        finish(up)
        if k + 1 < QUARTERS:
            begin(later[k + 1][0] + later[k + 1][1])
        for n in range(3):
            cols = slice(256 * n, 256 * (n + 1))
            u = dot(h2[...], ups[k, :, cols]) + up_bias[k, :, cols]
            uu = u * u
            t = jnp.tanh(u * (0.7978845608028654 + (0.7978845608028654 * 0.044715) * uu))
            half_t = 0.5 + 0.5 * t
            g[k, :, cols] = (u * half_t).astype(BF)
            inner = (0.5 * 0.7978845608028654) + (0.5 * 0.7978845608028654 * 0.134145) * uu
            gp[k, :, cols] = (half_t + u * inner * (1.0 - t * t)).astype(BF)
        ends = [
            pltpu.make_async_copy(g.at[k], g_out.at[k], sems_io.at[4 + 2 * k]),
            pltpu.make_async_copy(gp.at[k], gp_out.at[k], sems_io.at[5 + 2 * k]),
        ]
        begin(ends)
        stores += ends
        finish(down)
        x2[...] += dot(g[k], downs[k])
    stores.append(pltpu.make_async_copy(x2, x2_out, sems_io.at[12]))
    begin(stores[-1:])
    finish(stores)


WEIGHT_SCRATCH = [
    ((QUARTERS, D, D), BF),
    ((QUARTERS, D, D), BF),
    ((QUARTERS, 8, 32, D), BF),
    ((D, D), BF),
]


def feed(idx, x, o, gain, shift, out_bias, down_bias, up_bias, pieces):
    return kernel_call(
        feed_body,
        [smem_spec()] + [any_spec()] * 2 + [vmem_spec()] * 5 + [any_spec()] * 8,
        [
            sds((ROWS, D), F32),
            sds((ROWS, D), F32),
            sds((ROWS, D), BF),
            sds((QUARTERS, ROWS, D), BF),
            sds((QUARTERS, ROWS, D), BF),
        ],
        [any_spec()] * 5,
        [pltpu.VMEM(s, t) for s, t in WEIGHT_SCRATCH]
        + [pltpu.VMEM((ROWS, D), t) for t in (F32, BF, F32, F32, BF)]
        + [pltpu.VMEM((QUARTERS, ROWS, D), BF)] * 2
        + [pltpu.SemaphoreType.DMA((64,)), pltpu.SemaphoreType.DMA((32,)), pltpu.SemaphoreType.DMA((13,))],
        (idx, x, o, gain, shift, out_bias, down_bias, up_bias, *pieces),
        2 * ROWS * D * D * 9,
        25e6,
        name="feed",
    )


def feed_back_body(idx, e_in, x1_in, gp_in, gain, *rest):
    pieces, (dm_out, dz_out, e1_out, da_out, do_out, small), rest = rest[:8], rest[8:14], rest[14:]
    ups, downs, packed, outw, e, x1, gp, dm, dz, da, do, dh2, hidden_sums, sems, sems_o, sems_io = rest
    load_e = pltpu.make_async_copy(e_in, e, sems_io.at[0])
    load_x1 = pltpu.make_async_copy(x1_in, x1, sems_io.at[1])
    load_gp = [pltpu.make_async_copy(gp_in.at[k], gp.at[k], sems_io.at[2 + k]) for k in range(QUARTERS)]
    last = packed_copies(pieces, idx, sems_o, packed)
    weights = up_down_copies(pieces, idx, sems, ups, downs)
    begin([load_e] + weights[0][1] + [load_gp[0]])
    load_e.wait()
    begin(weights[0][0])
    dm[...] = e[...].astype(BF)
    stores = [pltpu.make_async_copy(dm, dm_out, sems_io.at[6])]
    begin(stores)
    small[4:5] = jnp.sum(dm[...].astype(F32), axis=0, keepdims=True)
    for k, (up, down) in enumerate(weights):
        finish(down + [load_gp[k]])
        if k + 1 < QUARTERS:
            begin(weights[k + 1][1] + [load_gp[k + 1]] + weights[k + 1][0])
        else:
            begin(last + [load_x1])
        for n in range(3):
            cols = slice(256 * n, 256 * (n + 1))
            part = (dot_nt(dm[...], downs[k, cols]) * gp[k, :, cols].astype(F32)).astype(BF)
            dz[k, :, cols] = part
            hidden_sums[idx[1] ^ k, :, cols] = jnp.sum(part.astype(F32), axis=0, keepdims=True)
        stores.append(pltpu.make_async_copy(dz.at[k], dz_out.at[k], sems_io.at[7 + k]))
        begin(stores[-1:])
        finish(up)
        grown = dot_nt(dz[k], ups[k])
        if k == 0:
            dh2[...] = grown
        else:
            dh2[...] += grown
    for zq in range(QUARTERS):
        small[zq : zq + 1] = hidden_sums[zq]
    finish(last + [load_x1])
    unpack_output(packed, outw)
    small[5:8] = jnp.zeros((3, D), F32)

    def norm_rows(i, carry):
        rows = rows_at(i * 128, 128, 128)
        unit, inverse = norm_parts(x1[rows])
        grad = dh2[rows]
        up = e[rows] + norm_backward(grad, unit, inverse, gain[...])
        e[rows] = up
        low = up.astype(BF)
        da[rows] = low
        small[5:6] += jnp.sum(low.astype(F32), axis=0, keepdims=True)
        small[6:7] += jnp.sum(grad * unit, axis=0, keepdims=True)
        small[7:8] += jnp.sum(grad, axis=0, keepdims=True)
        return carry

    lax.fori_loop(0, 4, norm_rows, 0)
    ends = [pltpu.make_async_copy(e, e1_out, sems_io.at[11]), pltpu.make_async_copy(da, da_out, sems_io.at[12])]
    begin(ends)
    do[...] = dot_nt(da[...], outw[...]).astype(BF)
    ends.append(pltpu.make_async_copy(do, do_out, sems_io.at[13]))
    begin(ends[-1:])
    finish(stores + ends)


def feed_back(idx, e, x1, gp, gain, pieces):
    return kernel_call(
        feed_back_body,
        [smem_spec()] + [any_spec()] * 3 + [vmem_spec()] + [any_spec()] * 8,
        [
            sds((ROWS, D), BF),
            sds((QUARTERS, ROWS, D), BF),
            sds((ROWS, D), F32),
            sds((ROWS, D), BF),
            sds((ROWS, D), BF),
            sds((8, D), F32),
        ],
        [any_spec()] * 5 + [vmem_spec()],
        [pltpu.VMEM(s, t) for s, t in WEIGHT_SCRATCH]
        + [
            pltpu.VMEM((ROWS, D), F32),
            pltpu.VMEM((ROWS, D), F32),
            pltpu.VMEM((QUARTERS, ROWS, D), BF),
            pltpu.VMEM((ROWS, D), BF),
            pltpu.VMEM((QUARTERS, ROWS, D), BF),
            pltpu.VMEM((ROWS, D), BF),
            pltpu.VMEM((ROWS, D), BF),
            pltpu.VMEM((ROWS, D), F32),
            pltpu.VMEM((QUARTERS, 1, D), F32),
            pltpu.SemaphoreType.DMA((64,)),
            pltpu.SemaphoreType.DMA((32,)),
            pltpu.SemaphoreType.DMA((14,)),
        ],
        (idx, e, x1, gp, gain, *pieces),
        2 * ROWS * D * D * 9,
        25e6,
        name="feed_back",
    )


def spread(idx, keep, send, source, k, wq, rows, sem):
    w8, mine = idx[0], idx[2]
    j = (wq >> 1) ^ (w8 >> 1)
    turned = ((j & 1) << 1) | (j >> 1)
    at = ((k & 1) << 1) | (k >> 1)
    here, there = jnp.where(mine == 1, j, turned), jnp.where(mine == 1, turned, j)
    a = pltpu.make_async_copy(source, keep.at[here, at, rows], sem)
    b = pltpu.make_async_copy(source, send.at[there, at, rows], sem)
    pl.when((wq & 1) == mine)(a.start)
    pl.when((wq & 1) != mine)(b.start)
    return a


def feed_grads_body(idx, g, dm, h2, dz, o, da, keep, send, flipped, turned, d_up, d_down, d_out, sems):
    waits = []
    flipped[...] = jnp.transpose(o[...])
    turned[...] = dot(flipped[...], da[...]).astype(BF)
    for zq in range(QUARTERS):
        for chip in range(4):
            for part in range(2):
                for s in range(4):
                    rows, cols = slice(16 * (s // 2), 16 * (s // 2) + 16), slice(384 * (s % 2), 384 * (s % 2) + 384)
                    if s == 3:
                        block = jnp.zeros((16, 384), BF)
                    else:
                        row = HEADS_COLS * zq + 48 * chip + 16 * s
                        block = turned[row : row + 16, 384 * part : 384 * part + 384]
                    d_out[zq, 2 * chip + part, rows, cols] = block
    for zq in range(QUARTERS):
        k = idx[1] ^ zq
        for wq in range(8):
            sem = sems.at[len(waits)]
            waits.append(spread(idx, keep, send, d_out.at[zq, wq], k, wq, pl.ds(2 * PIECE, 32), sem))
    for k in range(QUARTERS):
        flipped[...] = jnp.transpose(g[k])
        d_down[k] = dot(flipped[...], dm[...]).astype(BF)
        for wq in range(8):
            sem = sems.at[len(waits)]
            source = d_down.at[k, pl.ds(PIECE * wq, PIECE)]
            waits.append(spread(idx, keep, send, source, k, wq, pl.ds(PIECE, PIECE), sem))
    flipped[...] = jnp.transpose(h2[...])
    for k in range(QUARTERS):
        d_up[k] = dot(flipped[...], dz[k]).astype(BF)
        for wq in range(8):
            sem = sems.at[len(waits)]
            source = d_up.at[k, pl.ds(PIECE * wq, PIECE)]
            waits.append(spread(idx, keep, send, source, k, wq, pl.ds(0, PIECE), sem))
    for copy in waits:
        copy.wait()


def feed_grads(idx, g, dm, h2, dz, o, da):
    return kernel_call(
        feed_grads_body,
        [smem_spec()] + [vmem_spec()] * 6,
        [sds((4, QUARTERS, PACK, D), BF)] * 2,
        [any_spec()] * 2,
        [
            pltpu.VMEM((D, ROWS), BF),
            pltpu.VMEM((D, D), BF),
            pltpu.VMEM((QUARTERS, D, D), BF),
            pltpu.VMEM((QUARTERS, D, D), BF),
            pltpu.VMEM((QUARTERS, 8, 32, D), BF),
            pltpu.SemaphoreType.DMA((96,)),
        ],
        (idx, g, dm, h2, dz, o, da),
        2 * ROWS * D * D * 9,
        25e6,
        name="feed_grads",
    )


def back_tile(q, do, lse, drow, cols, hp, k2, v2, qrow, n, bias_here):
    qs, gs = both_heads(q[qrow : qrow + n, cols]), both_heads(do[qrow : qrow + n, cols])

    def of_heads(ref):
        return jnp.concatenate([ref[2 * hp + side, :, qrow : qrow + n] for side in range(2)], axis=1)

    s = dot_nt(k2, qs)
    if bias_here is not None:
        s = s + bias_here
    p = jnp.exp(s - of_heads(lse))
    ds = (p * (dot_nt(v2, gs) - of_heads(drow))).astype(BF)
    return dot(ds, qs), dot(p.astype(BF), gs), pair_lanes(dot_tn(ds, k2))


def attend_back_far_body(idx, q, do, o, lse, far, far_near, dq, dr, drow, kvr, dcol, sem):
    copy = load_far(idx, far, far_near, kvr, sem)
    dcol[...] = jnp.zeros_like(dcol)

    def products(hp, carry):
        cols, _ = pair_cols(hp)
        lane = lanes(ROWS)
        both = do[:, cols].astype(F32) * o[:, cols].astype(F32)
        first = jnp.sum(jnp.where(lane < 64, both, 0.0), axis=-1, keepdims=True)
        second = jnp.sum(jnp.where(lane < 64, 0.0, both), axis=-1, keepdims=True)
        dcol[...] = jnp.where(lane == 2 * hp, first, jnp.where(lane == 2 * hp + 1, second, dcol[...]))
        return carry

    lax.fori_loop(0, 6, products, 0)
    across = jnp.transpose(dcol[...])
    for head in range(12):
        drow[head] = across[head : head + 1]
    copy.wait()

    def run(tiles):
        def pair(hp, carry):
            cols, vcols = pair_cols(hp)
            dq_half = [None, None]
            for kh in range(2):
                keys = half_rows(kh)
                total = None
                for half, sources in tiles:
                    if kh in sources:
                        parts = back_tile(
                            q, do, lse, drow, cols, hp, kvr[keys, cols], kvr[keys, vcols], HALF * half, HALF, None
                        )
                        total = parts[:2] if total is None else (total[0] + parts[0], total[1] + parts[1])
                        dq_half[half] = parts[2] if dq_half[half] is None else dq_half[half] + parts[2]
                if total is None:
                    total = (jnp.zeros((HALF, 128), F32),) * 2
                dr[keys, cols] = total[0].astype(BF)
                dr[keys, vcols] = total[1].astype(BF)
            for half in range(2):
                part = dq_half[half]
                dq[half_rows(half), cols] = jnp.zeros((HALF, 128), F32) if part is None else part
            return carry

        lax.fori_loop(0, 6, pair, 0)

    for zl in range(2):
        pl.when(idx[3] == zl)(functools.partial(run, FAR_TILES[zl]))


def attend_back_far(idx, q, do, o, lse, far, far_near):
    return kernel_call(
        attend_back_far_body,
        [smem_spec()] + [vmem_spec()] * 4 + [any_spec()] * 2,
        [sds((ROWS, D), F32), sds((ROWS, 2 * D), BF), sds((12, 1, ROWS), F32)],
        [vmem_spec()] * 3,
        [
            pltpu.VMEM((ROWS, 2 * D), BF),
            pltpu.VMEM((ROWS, 128), F32),
            pltpu.SemaphoreType.DMA,
        ],
        (idx, q, do, o, lse, far, far_near),
        12e9,
        8e6,
        name="attend_back_far",
    )


def attend_back_near_body(idx, q, do, lse, drow, dq_far, own, near, dq, dn, dc, kvn, kvc, bias, bias_n, sems):
    waits = load_near(idx, own, near, kvn, kvc, sems)
    set_masks(idx, bias, bias_n, 1)
    for copy in waits:
        copy.wait()

    def run(tiles):
        def pair(hp, carry):
            cols, vcols = pair_cols(hp)
            dq_half = [None, None]
            for half in range(2):
                pieces = []
                for t in range(2):
                    rows = slice(HALF * half + 128 * t, HALF * half + 128 * (t + 1))
                    dk, dv, dqs = back_tile(
                        q, do, lse, drow, cols, hp, kvn[rows, cols], kvn[rows, vcols], rows.start, 128, bias_n[...]
                    )
                    dn[rows, cols] = dk.astype(BF)
                    dn[rows, vcols] = dv.astype(BF)
                    pieces.append(dqs)
                dq_half[half] = dq_far[half_rows(half), cols] + jnp.concatenate(pieces, axis=0)
            for kh in range(2):
                keys = half_rows(kh)
                total = None
                for half, sources in tiles:
                    if kh in dict(sources):
                        parts = back_tile(
                            q,
                            do,
                            lse,
                            drow,
                            cols,
                            hp,
                            kvc[keys, cols],
                            kvc[keys, vcols],
                            HALF * half,
                            HALF,
                            bias[...] if dict(sources)[kh] else None,
                        )
                        total = parts[:2] if total is None else (total[0] + parts[0], total[1] + parts[1])
                        dq_half[half] = dq_half[half] + parts[2]
                dc[keys, cols] = total[0].astype(BF)
                dc[keys, vcols] = total[1].astype(BF)
            for half in range(2):
                dq[half_rows(half), cols] = dq_half[half] * 0.125
            return carry

        lax.fori_loop(0, 6, pair, 0)

    for zl in range(2):
        pl.when(idx[3] == zl)(functools.partial(run, NEAR_TILES[zl]))


def attend_back_near(idx, q, do, lse, drow, dq_far, own, near):
    return kernel_call(
        attend_back_near_body,
        [smem_spec()] + [vmem_spec()] * 5 + [any_spec()] * 2,
        [sds((ROWS, D), F32), sds((ROWS, 2 * D), BF), sds((ROWS, 2 * D), BF)],
        [vmem_spec()] * 3,
        [
            pltpu.VMEM((ROWS, 2 * D), BF),
            pltpu.VMEM((ROWS, 2 * D), BF),
            pltpu.VMEM((HALF, 2 * HALF), F32),
            pltpu.VMEM((128, HALF), F32),
            pltpu.SemaphoreType.DMA((2,)),
        ],
        (idx, q, do, lse, drow, dq_far, own, near),
        18e9,
        12e6,
        name="attend_back_near",
    )


def project_back_body(idx, dq, dn, dcr, got, far, cosine, sine, x, e1, gain, *rest):
    pieces, (dpz, e, small, weights, wide, sems) = rest[:8], rest[8:]
    copies = mixer_copies(pieces, idx, sems, weights)
    for copy in copies:
        copy.start()
    noisy = idx[2] == 0
    for half in range(2):
        rows = slice(HALF * half, HALF * (half + 1))
        for j in range(6):
            cols = slice(128 * j, 128 * (j + 1))
            wide[rows, cols] = unrot(dq[rows, cols], cosine[rows], sine[rows])

        def total(cols, at=rows):
            summed = dcr[at, cols].astype(F32) + got[at, cols].astype(F32) + far[at, cols].astype(F32)
            return jnp.where(noisy, dn[at, cols].astype(F32), summed)

        for j in range(6):
            cols = slice(128 * j, 128 * (j + 1))
            wide[rows, D + 128 * j : D + 128 * (j + 1)] = unrot(total(cols), cosine[rows], sine[rows])
        wide[rows, 2 * D :] = total(slice(D, 2 * D))
    for copy in copies:
        copy.wait()
    small[...] = jnp.zeros_like(small)
    for zq in range(QUARTERS):
        for part in range(3):
            col = D * part + HEADS_COLS * zq
            dpz[zq, :, HEADS_COLS * part : HEADS_COLS * (part + 1)] = wide[:, col : col + HEADS_COLS].astype(BF)
        small[zq : zq + 1, :PARTS] = jnp.sum(dpz[zq].astype(F32), axis=0, keepdims=True)
        piece = dot_nt(dpz[zq], weights[zq])
        if zq == 0:
            e[...] = piece
        else:
            e[...] += piece

    def norm_rows(i, carry):
        rows = rows_at(i * 128, 128, 128)
        unit, inverse = norm_parts(x[rows])
        grad = e[rows]
        small[4:5] += jnp.sum(grad * unit, axis=0, keepdims=True)
        small[5:6] += jnp.sum(grad, axis=0, keepdims=True)
        e[rows] = e1[rows] + norm_backward(grad, unit, inverse, gain[...])
        return carry

    lax.fori_loop(0, 4, norm_rows, 0)


def project_back(idx, dq, dn, dcr, got, far, cosine, sine, x, e1, gain, pieces):
    return kernel_call(
        project_back_body,
        [smem_spec()] + [vmem_spec()] * 10 + [any_spec()] * 8,
        [sds((QUARTERS, ROWS, PARTS), BF), sds((ROWS, D), F32), sds((8, D), F32)],
        [vmem_spec()] * 3,
        [
            pltpu.VMEM((QUARTERS, D, PARTS), BF),
            pltpu.VMEM((ROWS, 3 * D), F32),
            pltpu.SemaphoreType.DMA((32,)),
        ],
        (idx, dq, dn, dcr, got, far, cosine, sine, x, e1, gain, *pieces),
        2 * ROWS * D * 3 * D,
        12e6,
        name="project_back",
    )


def project_grads_body(idx, h1, dpz, keep, send, flipped, stage, sems):
    waits = []
    flipped[...] = jnp.transpose(h1[...])
    for zq in range(QUARTERS):
        k = idx[1] ^ zq
        stage[zq] = dot(flipped[...], dpz[zq]).astype(BF)
        for wq in range(8):
            sem = sems.at[len(waits)]
            source = stage.at[zq, pl.ds(PIECE * wq, PIECE)]
            waits.append(spread(idx, keep, send, source, k, wq, pl.ds(0, PIECE), sem))
    for copy in waits:
        copy.wait()


def project_grads(idx, h1, dpz):
    return kernel_call(
        project_grads_body,
        [smem_spec()] + [vmem_spec()] * 2,
        [sds((4, QUARTERS, PIECE, PARTS), BF)] * 2,
        [any_spec()] * 2,
        [
            pltpu.VMEM((D, ROWS), BF),
            pltpu.VMEM((QUARTERS, D, PARTS), BF),
            pltpu.SemaphoreType.DMA((32,)),
        ],
        (idx, h1, dpz),
        2 * ROWS * D * 3 * D,
        9e6,
        name="project_grads",
    )


def finish_mixer_body(layer, filled, idx, *rest):
    pieces, rest = rest[:8], rest[8:]
    if filled:
        rest = rest[1:]
    out, stage, sem = rest
    for flip, piece in zip(flips(idx), pieces):
        stage[rows_at((idx[0] ^ flip) * PIECE, PIECE, 32)] = piece[...].astype(F32)
    copy = pltpu.make_async_copy(stage, out.at[layer], sem)
    copy.start()
    copy.wait()


def finish_mixer(idx, layer, layers, pieces, before):
    filled = before is not None
    return kernel_call(
        functools.partial(finish_mixer_body, layer, filled),
        [smem_spec()] + [vmem_spec()] * 8 + [any_spec()] * filled,
        sds((layers, D, PARTS), F32),
        any_spec(),
        [pltpu.VMEM((D, PARTS), F32), pltpu.SemaphoreType.DMA],
        (idx, *pieces) + ((before,) if filled else ()),
        1e6,
        4e6,
        aliases={9: 0} if filled else None,
        name="finish_mixer",
    )


def finish_feed_body(layer, filled, idx, *rest):
    pieces, rest = rest[:8], rest[8:]
    if filled:
        rest = rest[3:]
    up, down, out, up_s, down_s, out_s, sems = rest
    for flip, piece in zip(flips(idx), pieces):
        wq = idx[0] ^ flip
        rows = rows_at(wq * PIECE, PIECE, 32)
        up_s[rows] = piece[:PIECE].astype(F32)
        down_s[rows] = piece[PIECE : 2 * PIECE].astype(F32)
        cols = pl.ds(pl.multiple_of((wq & 1) * 384, 128), 384)
        for s in range(3):
            row = 2 * PIECE + 16 * (s // 2)
            block = piece[row : row + 16, 384 * (s % 2) : 384 * (s % 2) + 384]
            out_s[rows_at((wq >> 1) * 48 + 16 * s, 16, 16), cols] = block.astype(F32)
    copies = [
        pltpu.make_async_copy(stage, whole.at[layer], sems.at[i])
        for i, (stage, whole) in enumerate(((up_s, up), (down_s, down), (out_s, out)))
    ]
    for copy in copies:
        copy.start()
    for copy in copies:
        copy.wait()


def finish_feed(idx, layer, layers, pieces, before):
    filled = before is not None
    return kernel_call(
        functools.partial(finish_feed_body, layer, filled),
        [smem_spec()] + [vmem_spec()] * 8 + [any_spec()] * (3 * filled),
        [sds((layers, D, D), F32), sds((layers, D, D), F32), sds((layers, HEADS_COLS, D), F32)],
        [any_spec()] * 3,
        [
            pltpu.VMEM((D, D), F32),
            pltpu.VMEM((D, D), F32),
            pltpu.VMEM((HEADS_COLS, D), F32),
            pltpu.SemaphoreType.DMA((3,)),
        ],
        (idx, *pieces) + (tuple(before) if filled else ()),
        1e6,
        8e6,
        aliases={9: 0, 10: 1, 11: 2} if filled else None,
        name="finish_feed",
    )


def pack_body(idx, ups, downs, outs, *rest):
    targets, (zeros, sems) = rest[:-2], rest[-2:]
    zeros[...] = jnp.zeros_like(zeros)
    rows = rows_at(idx[0] * PIECE, PIECE, 32)
    cols = pl.ds(pl.multiple_of(idx[2] * 384, 128), 384)
    copies = []
    for layer, target in enumerate(targets):
        moves = [
            (ups.at[layer, rows], target.at[pl.ds(0, PIECE)]),
            (downs.at[layer, rows], target.at[pl.ds(PIECE, PIECE)]),
        ]
        for s in range(4):
            place = target.at[pl.ds(2 * PIECE + 16 * (s // 2), 16), pl.ds(384 * (s % 2), 384)]
            if s == 3:
                moves.append((zeros, place))
            else:
                moves.append((outs.at[layer, rows_at((idx[0] >> 1) * 48 + 16 * s, 16, 16), cols], place))
        for source, place in moves:
            copies.append(pltpu.make_async_copy(source, place, sems.at[len(copies)]))
    for copy in copies:
        copy.start()
    for copy in copies:
        copy.wait()


def pack(idx, ups, downs, outs):
    layers = ups.shape[0]
    return kernel_call(
        pack_body,
        [smem_spec()] + [any_spec()] * 3,
        [sds((PACK, D), BF)] * layers,
        [vmem_spec()] * layers,
        [pltpu.VMEM((16, 384), BF), pltpu.SemaphoreType.DMA((6 * layers,))],
        (idx, ups, downs, outs),
        1e6,
        1e6,
        name="pack",
    )


def flip_wide(x, bit):
    return lax.ppermute(x, "wide", [(i, i ^ bit) for i in range(lax.axis_size("wide"))])


def flip_narrow(x, bit):
    return lax.ppermute(x, "narrow", [(i, i ^ bit) for i in range(QUARTERS)])


def first_axis(x):
    return lax.ppermute(x, "wide", [(i, i ^ (4 if i & 1 else 2)) for i in range(lax.axis_size("wide"))])


def second_axis(x):
    return lax.ppermute(x, "wide", [(i, i ^ (2 if i & 1 else 4)) for i in range(lax.axis_size("wide"))])


def gate_body(*refs):
    return None


def gate(tree):
    leaves, shape = jax.tree.flatten(tree)
    out = pl.pallas_call(
        gate_body,
        in_specs=[any_spec() for _ in leaves],
        out_specs=[any_spec() for _ in leaves],
        out_shape=[sds(x.shape, x.dtype) for x in leaves],
        input_output_aliases={i: i for i in range(len(leaves))},
        name="gate",
    )(*leaves)
    return jax.tree.unflatten(shape, out)


def gather_direct(piece):
    return [piece] + [flip_narrow(piece, k) for k in ORDER[1:]]


def gather_far(piece):
    return piece, flip_narrow(piece, 2)


def gather_near(pair):
    pair = jnp.stack(pair)
    return pair, flip_narrow(pair, 1)


def whole(parts):
    return jnp.stack(parts) if parts[0].ndim == 2 else jnp.concatenate(parts)


def gather_first(own):
    return own, first_axis(own)


def gather_second(parts):
    own, first = parts
    return [own, first, second_axis(own), second_axis(first)]


def gather_last(here):
    return here + [flip_wide(x, 1) for x in here]


def added(*terms):
    return functools.reduce(jnp.add, [t.astype(F32) for t in terms]).astype(BF)


def reduce_core(pair):
    keep, send = pair
    return keep, flip_wide(send, 1)


def reduce_first_sums(pair):
    keep, got = pair
    return keep, got, added(keep[3], got[3]), added(keep[2], got[2])


def reduce_first(parts):
    keep, got, passed, stays = parts
    return keep, got, first_axis(passed), first_axis(stays)


def reduce_first_whole(pair):
    keep, got = pair
    return keep, got, first_axis(added(keep[2:], got[2:]))


def reduce_second(keep, got, passed):
    return second_axis(added(keep[1], got[1], passed))


def reduce_near(parts):
    total = added(parts[0][0], parts[1][0], *parts[2:])
    bit = 8
    while bit < lax.axis_size("wide"):
        total = added(total, flip_wide(total, bit))
        bit *= 2
    return total, flip_narrow(total[2:], 1)


def reduce_far(parts):
    total, near = parts
    return total, near, flip_narrow(added(total[1], near[1]), 2)


def both_axes(x):
    return flip_wide(x, 6)


def gather_plane(own):
    return [own, first_axis(own), second_axis(own), both_axes(own)]


def spread_first(parts):
    total, near, far = parts
    return gather_first(added(total[0], near[0], far))


def reduce_plane(pair):
    keep, got = pair
    moves = (second_axis, first_axis, both_axes)
    return [keep, got] + [move(added(keep[i + 1], got[i + 1])) for i, move in enumerate(moves)]


def reduce_narrow(parts):
    keep, got, *others = parts
    total = added(keep[0], got[0], *others)
    bit = 8
    while bit < lax.axis_size("wide"):
        total = added(total, flip_wide(total, bit))
        bit *= 2
    return [total] + [flip_narrow(total[i], ORDER[i]) for i in range(1, QUARTERS)]


def device_pairs(move):
    pairs = []
    for w in range(lax.axis_size("wide")):
        for z in range(QUARTERS):
            target = move(w, z)
            if target is not None:
                pairs.append((w * QUARTERS + z, target[0] * QUARTERS + target[1]))
    return pairs


BOTH = ("wide", "narrow")


def relocate_first(rows):
    pairs = device_pairs(lambda w, z: ((w & ~1) | (z >> 1), ((w & 1) << 1) | (z & 1)))
    return lax.ppermute(rows, BOTH, pairs)


def relocate_second(rows):
    pairs = device_pairs(lambda w, z: ((w & ~1) | (z >> 1), ((w & 1) << 1) | (1 - (z & 1))))
    return lax.ppermute(rows, BOTH, pairs)


def relocate(rows):
    return relocate_halves((rows[:HALF], rows[HALF:]))


def relocate_halves(halves):
    return relocate_first(halves[0]), relocate_second(halves[1])


def between_chips(x):
    pairs = device_pairs(lambda w, z: (w, z ^ 1) if w & 1 else None)
    return lax.ppermute(x, BOTH, pairs)


def within_chip(x, source):
    pairs = [(i, i ^ 1) for i in range(lax.axis_size("wide")) if (i & 1) == source]
    return lax.ppermute(x, "wide", pairs)


def per_device(
    tokens,
    block_size,
    norm_gain,
    norm_shift,
    mixer_weight,
    mixer_bias,
    output_weight,
    output_bias,
    up_weight,
    up_bias,
    down_weight,
    cotangent,
):
    layers = norm_gain.shape[0]
    w, z = lax.axis_index("wide"), lax.axis_index("narrow")
    w8, core, low = w & 7, w & 1, z & 1
    sizes = jnp.where((z >> 1) == core, block_size, flip_wide(block_size, 1))[0]
    level = 2 + (sizes >= 8).astype(jnp.int32) + (sizes >= 16).astype(jnp.int32)
    idx = jnp.stack([w8, z, core, low, level, w8, w8, w8]).astype(jnp.int32)

    bases = jnp.where(low == 0, jnp.array([0, 768]), jnp.array([512, 256]))
    position = (bases[:, None] + jnp.arange(HALF)[None, :]).reshape(ROWS).astype(F32)
    halfway = HEAD_DIM // 2
    frequency = jnp.exp(jnp.arange(halfway, dtype=F32) * (-math.log(10000.0) / halfway))
    angle = position[:, None] * frequency[None, :]
    cosine = jnp.tile(jnp.cos(angle), (1, 4))
    sine = jnp.sin(angle)
    sine = jnp.concatenate([-sine, sine, -sine, sine], axis=1)

    def bias_pieces(layer):
        return mixer_bias[layer].reshape(PARTS), up_bias[layer]

    biases = jnp.concatenate([t for layer in range(layers) for t in bias_pieces(layer)])
    width = PARTS + D

    def bias_of(layer, start, size):
        at = width * layer + start
        return jnp.stack([b[at : at + size] for b in biases])[:, None]

    def mixer_piece(layer):
        return lax.dynamic_slice_in_dim(mixer_weight[layer], w8 * PIECE, PIECE, 0).reshape(PIECE, PARTS)

    def run_project(layer, x, pieces):
        gain, shift = norm_gain[layer], norm_shift[layer]
        return project(idx, x, gain[0:1], shift[0:1], bias_of(layer, 0, PARTS), cosine, sine, pieces)

    def run_feed(layer, x, o, pieces):
        gain, shift, bias = norm_gain[layer], norm_shift[layer], output_bias[layer]
        return feed(
            idx, x, o, gain[1:2], shift[1:2], bias[0:1], bias[1:2], bias_of(layer, PARTS, D), pieces
        )

    mixer0 = gather_direct(mixer_piece(0))
    feed0, feed1 = pack(idx, up_weight, down_weight, output_weight)
    biases = [biases] + [flip_narrow(biases, k) for k in (1, 2, 3)]
    halves = tokens[:HALF], tokens[HALF:]
    mixer0, halves, feed0, biases = gate((mixer0, halves, feed0, biases))
    mixer0 = gather_first(whole(mixer0))
    feed0 = gather_far(feed0)
    mixer0, feed0, halves, mixer1 = gate((mixer0, feed0, halves, mixer_piece(1)))
    own, first = mixer0
    mixer0 = [own, first, second_axis(own), second_axis(first)]
    rows = relocate_halves(halves)
    feed0 = gather_near(feed0)
    mixer0, rows, feed0, mixer1 = gate((mixer0, rows, feed0, mixer1))
    mixer0 = gather_last(mixer0)
    own, first = gather_first(whole(feed0))
    mixer1 = gather_far(mixer1)
    x0 = jnp.concatenate(rows).astype(F32)
    h1_0, q_0, kv = run_project(0, x0, mixer0)
    own_0, own, first, mixer1 = gate((kv, own, first, mixer1))
    near_0, far = within_chip(own_0, 1), between_chips(own_0)
    second = second_axis(own)
    others = [flip_wide(own, 1), flip_wide(first, 1)]
    state = attend_near(idx, q_0, own_0, near_0)
    state, far_0, first, second, others, mixer1, feed1 = gate((state, far, first, second, others, mixer1, feed1))
    far_near_0 = within_chip(far_0, 1)
    third = second_axis(first)
    others = others + [flip_wide(second, 1)]
    mixer1, feed1 = gather_near(mixer1), gather_far(feed1)
    o_0, lse_0 = attend_far(idx, q_0, far_0, far_near_0, state)
    o_0, third, others, mixer1, feed1 = gate((o_0, third, others, mixer1, feed1))
    feed0 = [own, first, second, third] + others + [flip_wide(third, 1)]
    mixer1, feed1 = gather_plane(whole(mixer1)), gather_near(feed1)
    x1, x1_0, h2_0, g_0, gp_0 = run_feed(0, x0, o_0, feed0)
    x1, mixer1, feed1 = gate((x1, mixer1, feed1))
    mixer1 = gather_last(mixer1)
    own, first = gather_first(whole(feed1))
    h1_1, q_1, kv = run_project(1, x1, mixer1)
    own_1, own, first = gate((kv, own, first))
    near_1, far = within_chip(own_1, 1), between_chips(own_1)
    second = second_axis(own)
    state = attend_near(idx, q_1, own_1, near_1)
    state, far_1, own, first, second = gate((state, far, own, first, second))
    far_near_1 = within_chip(far_1, 1)
    third = second_axis(first)
    others = [flip_wide(own, 1), flip_wide(first, 1), flip_wide(second, 1)]
    o_1, lse_1 = attend_far(idx, q_1, far_1, far_near_1, state)
    o_1, third, others, halves = gate((o_1, third, others, (cotangent[:HALF], cotangent[HALF:])))
    e = relocate_halves(halves)
    feed1 = [own, first, second, third] + others + [flip_wide(third, 1)]
    x2, x1_1, h2_1, g_1, gp_1 = run_feed(1, x1, o_1, feed1)
    x2, e = gate((x2, e))
    x_out = relocate(x2.astype(BF))

    e = jnp.concatenate(e).astype(F32)
    dm, dz, e1, da, do, small_feed1 = feed_back(idx, e, x1_1, gp_1, norm_gain[1, 1:2], feed1)
    g_feed1 = feed_grads(idx, g_1, dm, h2_1, dz, o_1, da)
    do, x_out, g_feed1 = gate((do, x_out, g_feed1))
    g_feed1 = reduce_core(g_feed1)
    dq, dr, drow = attend_back_far(idx, q_1, do, o_1, lse_1, far_1, far_near_1)
    dr, dq, g_feed1 = gate((dr, dq, g_feed1))
    dr, got, dq, g_feed1 = gate((dr, within_chip(dr, 0), dq, reduce_first_sums(g_feed1)))
    far = between_chips(added(dr, got))
    g_feed1 = reduce_first(g_feed1)
    dq, dn, dc = attend_back_near(idx, q_1, do, lse_1, drow, dq, own_1, near_1)
    keep, gained, passed, stays = g_feed1
    dc, far, keep, gained, passed = gate((dc, far, keep, gained, passed))
    got = within_chip(dc, 0)
    g_feed1 = keep, gained, stays, reduce_second(keep, gained, passed)
    dpz, e, small_mixer1 = project_back(
        idx, dq, dn, dc, got, far, cosine, sine, x1, e1, norm_gain[1, 0:1], mixer1
    )
    dpz, e, g_feed1 = gate((dpz, e, g_feed1))
    g_feed1 = reduce_near(g_feed1)
    g_mixer1 = project_grads(idx, h1_1, dpz)
    e, g_mixer1 = gate((e, g_mixer1))
    g_mixer1 = reduce_core(g_mixer1)
    dm, dz, e1, da, do, small_feed0 = feed_back(idx, e, x1_0, gp_0, norm_gain[0, 1:2], feed0)
    dm, do, g_feed1, g_mixer1 = gate((dm, do, g_feed1, g_mixer1))
    g_feed1, g_mixer1 = reduce_far(g_feed1), reduce_first_whole(g_mixer1)
    g_feed0 = feed_grads(idx, g_0, dm, h2_0, dz, o_0, da)
    do, g_feed1, g_mixer1, g_feed0 = gate((do, g_feed1, g_mixer1, g_feed0))
    keep1, gained1, both1 = g_mixer1
    second1, g_feed0 = reduce_second(keep1, gained1, both1[1]), reduce_core(g_feed0)
    g_feed1 = spread_first(g_feed1)
    dq, dr, drow = attend_back_far(idx, q_0, do, o_0, lse_0, far_0, far_near_0)
    dr, dq, g_feed1, second1, g_feed0 = gate((dr, dq, g_feed1, second1, g_feed0))
    dr, got, dq, g_feed0, g_feed1 = gate((dr, within_chip(dr, 0), dq, reduce_first_sums(g_feed0), g_feed1))
    far = between_chips(added(dr, got))
    g_feed0, g_feed1 = reduce_first(g_feed0), gather_second(g_feed1)
    dq, dn, dc = attend_back_near(idx, q_0, do, lse_0, drow, dq, own_0, near_0)
    keep, gained, passed, stays = g_feed0
    dc, far, keep, gained, passed, g_feed1 = gate((dc, far, keep, gained, passed, g_feed1))
    got = within_chip(dc, 0)
    g_feed0 = keep, gained, stays, reduce_second(keep, gained, passed)
    g_mixer1 = reduce_near((keep1, gained1, both1[0], second1))
    dpz, e, small_mixer0 = project_back(
        idx, dq, dn, dc, got, far, cosine, sine, x0, e1, norm_gain[0, 0:1], mixer0
    )
    e, dpz, g_feed0, g_mixer1 = gate((e, dpz, g_feed0, g_mixer1))
    g_feed0, g_mixer1 = reduce_near(g_feed0), reduce_far(g_mixer1)
    g_mixer0 = reduce_core(project_grads(idx, h1_0, dpz))
    smalls = jnp.concatenate([small_feed0, small_mixer0, small_feed1, small_mixer1])
    g_feed1 = gather_last(g_feed1)
    smalls = smalls, flip_wide(smalls, 1)
    g_mixer0, smalls, e, g_feed1, g_mixer1 = gate((g_mixer0, smalls, e, g_feed1, g_mixer1))
    g_mixer0 = reduce_plane(g_mixer0)
    early, e_late = relocate_first(e[:HALF].astype(BF)), e
    feed_out = finish_feed(idx, 1, layers, g_feed1, None)
    g_mixer0, g_feed0, smalls, feed_out, early, e_late, g_mixer1 = gate(
        (g_mixer0, g_feed0, smalls, feed_out, early, e_late, g_mixer1)
    )
    keep, gained, *others = g_mixer0
    total = added(keep[0], gained[0], *others)
    bit = 8
    while bit < lax.axis_size("wide"):
        total = added(total, flip_wide(total, bit))
        bit *= 2
    g_mixer0 = total, flip_narrow(total[2:], 1)
    g_feed0 = reduce_far(g_feed0)
    smalls = smalls[0] + smalls[1]
    smalls = smalls, first_axis(smalls)
    g_mixer1 = spread_first(g_mixer1)
    g_mixer0, g_feed0, smalls, g_mixer1, e_late = gate((g_mixer0, g_feed0, smalls, g_mixer1, e_late))
    g_mixer0, g_feed0 = reduce_far(g_mixer0), spread_first(g_feed0)
    smalls = smalls[0] + smalls[1]
    smalls = smalls, second_axis(smalls)
    own, first = g_mixer1
    both = second_axis(jnp.stack([own, first]))
    late = relocate_second(e_late[HALF:].astype(BF))
    g_mixer0, g_feed0, smalls, own, first, both, late = gate((g_mixer0, g_feed0, smalls, own, first, both, late))
    g_mixer1 = [own, first, both[0], both[1]]
    g_mixer0, g_feed0 = spread_first(g_mixer0), gather_second(g_feed0)
    smalls = smalls[0] + smalls[1]
    bit = 8
    while bit < lax.axis_size("wide"):
        smalls = smalls + flip_wide(smalls, bit)
        bit *= 2
    smalls = smalls, flip_narrow(smalls, 1)
    g_mixer1 = gather_last(g_mixer1)
    mixer_out = finish_mixer(idx, 1, layers, g_mixer1, None)
    g_mixer0, g_feed0, smalls, mixer_out = gate((g_mixer0, g_feed0, smalls, mixer_out))
    g_mixer0, g_feed0 = gather_second(g_mixer0), gather_last(g_feed0)
    smalls = smalls[0] + smalls[1]
    smalls = smalls, flip_narrow(smalls, 2)
    feed_out = finish_feed(idx, 0, layers, g_feed0, feed_out)
    g_mixer0, smalls, feed_out = gate((g_mixer0, smalls, feed_out))
    smalls = smalls[0] + smalls[1]
    g_mixer0 = gather_last(g_mixer0)
    mixer_out = finish_mixer(idx, 0, layers, g_mixer0, mixer_out)
    tokens_grad = jnp.concatenate([early, late])
    x_out = jnp.concatenate(x_out)

    small = smalls.reshape(layers, 16, D)
    up_bias_grad = lax.dynamic_index_in_dim(small[:, 0:4], z, 1, keepdims=False)
    mixer_bias_grad = lax.dynamic_index_in_dim(small[:, 8:12, :PARTS], z, 1, keepdims=False)
    return (
        x_out,
        tokens_grad,
        jnp.stack([small[:, 12], small[:, 6]], axis=1),
        jnp.stack([small[:, 13], small[:, 7]], axis=1),
        mixer_out.reshape(layers, D, 3, HEADS_COLS),
        mixer_bias_grad.reshape(layers, 3, HEADS_COLS),
        feed_out[2],
        jnp.stack([small[:, 5], small[:, 4]], axis=1),
        feed_out[0],
        up_bias_grad,
        feed_out[1],
    )


def solution(mesh):
    rows = P(("wide", "narrow"), None)
    quarters = (
        P(None, None, None, "narrow"),
        P(None, None, "narrow"),
        P(None, "narrow", None),
        P(),
        P(None, None, "narrow"),
        P(None, "narrow"),
        P(None, "narrow", None),
    )
    return jax.shard_map(
        per_device,
        mesh=mesh,
        in_specs=(rows, P("wide"), P(), P()) + quarters + (rows,),
        out_specs=(rows, rows, P(), P()) + quarters,
        check_vma=False,
    )
```
